32 devices in a mesh: fsdp: 8 (over z, core), seq: 4 (over y, x).
Axes of the slice: x: 2, y: 2, z: 4, core: 2. Of those that a mesh axis runs over, the one named last changes fastest.
Arguments:
- tokens: bfloat16 [4096, 1024], P(('fsdp', 'seq')), may hold values from -6 to 6
- segment_ids: int32 [4096], P('fsdp'), may hold values from -1 to 1, as said below
- first_gain: bfloat16 [1024], P('fsdp'), may hold values from 0.25 to 1.75
- first_bias: bfloat16 [1024], P('fsdp'), may hold values from -3 to 3
- input_weight: bfloat16 [1024, 3072], P('fsdp'), may hold values from -0.1875 to 0.1875
- query_bias: bfloat16 [1024], P('fsdp'), may hold values from -3 to 3
- value_bias: bfloat16 [1024], P('fsdp'), may hold values from -3 to 3
- output_weight: bfloat16 [1024, 1024], P('fsdp'), may hold values from -0.75 to 0.75
- output_bias: bfloat16 [1024], P('fsdp'), may hold values from -3 to 3
- scale_one: bfloat16 [1024], P('fsdp'), may hold values from 0.5 to 2
- second_gain: bfloat16 [1024], P('fsdp'), may hold values from 0.25 to 1.75
- second_bias: bfloat16 [1024], P('fsdp'), may hold values from -3 to 3
- up_weight: bfloat16 [1024, 4096], P('fsdp'), may hold values from -0.1875 to 0.1875
- up_bias: bfloat16 [4096], P('fsdp'), may hold values from -3 to 3
- down_weight: bfloat16 [4096, 1024], P('fsdp'), may hold values from -0.09375 to 0.09375
- down_bias: bfloat16 [1024], P('fsdp'), may hold values from -3 to 3
- scale_two: bfloat16 [1024], P('fsdp'), may hold values from 0.5 to 2
- out_grad: bfloat16 [4096, 1024], P(('fsdp', 'seq')), may hold values from -6 to 6
Outputs:
- layer_out: bfloat16 [4096, 1024], P(('fsdp', 'seq'))
- tokens_grad: bfloat16 [4096, 1024], P(('fsdp', 'seq'))
- first_gain_grad: float32 [1024], P('fsdp')
- first_bias_grad: float32 [1024], P('fsdp')
- input_weight_grad: float32 [1024, 3072], P('fsdp')
- query_bias_grad: float32 [1024], P('fsdp')
- value_bias_grad: float32 [1024], P('fsdp')
- output_weight_grad: float32 [1024, 1024], P('fsdp')
- output_bias_grad: float32 [1024], P('fsdp')
- scale_one_grad: float32 [1024], P('fsdp')
- second_gain_grad: float32 [1024], P('fsdp')
- second_bias_grad: float32 [1024], P('fsdp')
- up_weight_grad: float32 [1024, 4096], P('fsdp')
- up_bias_grad: float32 [4096], P('fsdp')
- down_weight_grad: float32 [4096, 1024], P('fsdp')
- down_bias_grad: float32 [1024], P('fsdp')
- scale_two_grad: float32 [1024], P('fsdp')
The draws below stay inside these ranges and needn't reach their ends.
Inputs may be any that keep to these rules, and one draw needn't show every extreme that they name: `segment_ids`: each group of 512 consecutive slots holds two images and then padding: one image fills all but fewer than 128 of the group's slots, the other has 1 to 64 tokens and stands before or after it; the group ends with 1 to 63 padding slots marked -1; the first image in the group has id 0, the second id 1.
All inputs are finite; a program needn't handle non-finite values.
Results may differ from the reference program's by a relative error of at most 0.018.
Values may be sent and summed in bfloat16 or wider, within the bound.
No kernel may reach another device: no remote copies, remote signals or barrier semaphores. Data moves between devices by JAX's collectives and lax.ppermute only.
A program may use at most 192 MiB of HBM per device.

```python
import math
from functools import partial
import jax
import jax.numpy as jnp
from jax import lax

HEADS = 16
HEAD_DIM = 64
FF = 4096
TOK_DEV = 128
D = 1024
SLOTS = 512
TOKENS = 4096


def draw_segment_ids(key, part):
    key = jax.random.fold_in(key, 11)
    key_short, key_pad, key_order = jax.random.split(key, 3)
    groups = TOKENS // SLOTS
    short_len = jax.random.randint(key_short, (groups,), 1, TOK_DEV // 2 + 1)
    pad_len = jax.random.randint(key_pad, (groups,), 1, (TOK_DEV - 1) // 2 + 1)
    short_first = jax.random.randint(key_order, (groups,), 0, 2)
    position = jnp.arange(SLOTS, dtype=jnp.int32)[None, :]
    used_len = SLOTS - pad_len
    long_len = used_len - short_len
    boundary = jnp.where(short_first == 1, short_len, long_len)
    ident = jnp.where(position < boundary[:, None], 0, 1)
    ident = jnp.where(position >= used_len[:, None], -1, ident)
    return ident.reshape(-1).astype(jnp.int32)


def shard_levels(own_key, extent, shards, smallest, largest):
    factor_of = 1.0
    for dim, shards_of in shards:
        heights = jax.random.uniform(jax.random.fold_in(jax.random.fold_in(own_key, 6), dim), (shards_of,), jnp.float32, smallest / len(shards), largest / len(shards))
        factor_of = factor_of * jnp.repeat(jnp.exp(heights), extent[dim] // shards_of).reshape((-1,) + (1,) * (len(extent) - 1 - dim))
    return factor_of


def bell_draw(own_key, dims, scale, reach, cuts=(), kind=jnp.bfloat16):
    loudness = shard_levels(own_key, dims, cuts, -0.22, 0.18) if cuts else 1.0
    values = jax.random.normal(own_key, dims, jnp.float32) * scale * loudness
    return jnp.minimum(jnp.maximum(values, -reach), reach).astype(kind)


def setup_inputs(seed: int = 0) -> dict:
    seeds = jax.random.split(jax.random.key(seed), 19)
    tokens = bell_draw(seeds[0], (TOKENS, D), 1.0, 6.0, ((0, 32),))
    segment_ids = draw_segment_ids(jax.random.fold_in(seeds[18], 71), 0)
    first_gain = jnp.clip(1.0 + 0.15 * jax.random.normal(seeds[2], (D,), jnp.float32), 0.25, 1.75).astype(jnp.bfloat16)
    first_bias = bell_draw(seeds[3], (D,), 0.5, 3.0, ((0, 8),))
    input_weight = bell_draw(seeds[4], (D, 3 * D), D ** -0.5, 0.1875, ((0, 8),))
    query_bias = bell_draw(seeds[5], (D,), 0.5, 3.0, ((0, 8),))
    value_bias = bell_draw(seeds[6], (D,), 0.5, 3.0, ((0, 8),))
    output_weight = bell_draw(seeds[7], (D, D), (D // 16) ** -0.5, 0.75, ((0, 8),))
    output_bias = bell_draw(seeds[8], (D,), 0.5, 3.0, ((0, 8),))
    scale_one = jnp.clip(jnp.exp(math.log(2.0) - 1.3862944 * jax.random.uniform(seeds[9], (D,), jnp.float32) ** shard_levels(seeds[9], (D,), ((0, 8),), -0.2, 0.2)), 0.5, 2.0).astype(jnp.bfloat16)
    second_gain = jnp.clip(1.0 + 0.15 * jax.random.normal(seeds[10], (D,), jnp.float32), 0.25, 1.75).astype(jnp.bfloat16)
    second_bias = bell_draw(seeds[11], (D,), 0.5, 3.0, ((0, 8),))
    up_weight = bell_draw(seeds[12], (D, FF), D ** -0.5, 0.1875, ((0, 8),))
    up_bias = bell_draw(seeds[13], (FF,), 0.5, 3.0, ((0, 8),))
    down_weight = bell_draw(seeds[14], (FF, D), FF ** -0.5, 0.09375, ((0, 8),))
    down_bias = bell_draw(seeds[15], (D,), 0.5, 3.0, ((0, 8),))
    scale_two = jnp.clip(jnp.exp(math.log(2.0) - 1.3862944 * jax.random.uniform(seeds[16], (D,), jnp.float32) ** shard_levels(seeds[16], (D,), ((0, 8),), -0.2, 0.2)), 0.5, 2.0).astype(jnp.bfloat16)
    out_grad = bell_draw(seeds[17], (TOKENS, D), 1.0, 6.0, ((0, 32),))
    return {"tokens": tokens, "segment_ids": segment_ids, "first_gain": first_gain, "first_bias": first_bias, "input_weight": input_weight, "query_bias": query_bias, "value_bias": value_bias, "output_weight": output_weight, "output_bias": output_bias, "scale_one": scale_one, "second_gain": second_gain, "second_bias": second_bias, "up_weight": up_weight, "up_bias": up_bias, "down_weight": down_weight, "down_bias": down_bias, "scale_two": scale_two, "out_grad": out_grad}


@jax.custom_vjp
def low(v):
    return lax.optimization_barrier(v.astype(jnp.bfloat16)).astype(jnp.float32)

@jax.custom_vjp
def low_back(v):
    return v

def low_keep(v):
    return (low(v), None)

def low_pass(kept, grad):
    return (grad,)

def back_keep(v):
    return (v, None)

def back_low(kept, grad):
    return (low(grad),)
low.defvjp(low_keep, low_pass)
low_back.defvjp(back_keep, back_low)
epsilon = 1e-06
masked_value = -1000000000.0

def matmul(left, right):
    return jnp.dot(left, right, precision=lax.Precision.HIGHEST, preferred_element_type=jnp.float32)

def layer_norm(values, gain, offset):
    center = values - lax.optimization_barrier(jnp.mean(values, axis=-1, keepdims=True))
    spread = lax.rsqrt(lax.optimization_barrier(jnp.mean(center * center, axis=-1, keepdims=True)) + epsilon)
    return center * spread * gain + offset

def head_attend(query_rows, key_rows, value_rows, allowed):
    products = matmul(query_rows, key_rows.T) * HEAD_DIM ** (-0.5)
    scores = low_back(jnp.where(allowed, products, masked_value))
    softmax_weights = low(jax.nn.softmax(scores, axis=-1))
    return matmul(softmax_weights, value_rows)

def group_forward(inputs, allowed, params):
    gain_one, offset_one, weight_in, bias_query, bias_value, weight_out, bias_out, factor_one, gain_two, offset_two, weight_up, bias_up, weight_down, bias_down, factor_two = params
    hidden_one = low(layer_norm(inputs, gain_one, offset_one))
    zeros_key = jnp.zeros((HEADS, HEAD_DIM), inputs.dtype)
    bias_full = jnp.stack([bias_query.reshape(HEADS, HEAD_DIM), zeros_key, bias_value.reshape(HEADS, HEAD_DIM)], axis=1).reshape(-1)
    triple = low_back(low(matmul(hidden_one, weight_in) + bias_full))
    triple = triple.reshape(-1, HEADS, 3, HEAD_DIM).transpose(1, 2, 0, 3)
    attend = jax.checkpoint(partial(head_attend, allowed=allowed))
    heads_out = lax.map(lambda pieces: attend(pieces[0], pieces[1], pieces[2]), triple)
    attended = low_back(low(heads_out.transpose(1, 0, 2).reshape(-1, HEADS * HEAD_DIM)))
    branch_one = low_back(matmul(attended, weight_out) + bias_out)
    middle = inputs + factor_one * branch_one
    hidden_two = low(layer_norm(middle, gain_two, offset_two))
    before = low_back(matmul(hidden_two, weight_up) + bias_up)
    activated = low(jax.nn.gelu(before, approximate=False))
    branch_two = low_back(matmul(activated, weight_down) + bias_down)
    return middle + factor_two * branch_two

def reference(tokens, segment_ids, first_gain, first_bias, input_weight, query_bias, value_bias, output_weight, output_bias, scale_one, second_gain, second_bias, up_weight, up_bias, down_weight, down_bias, scale_two, out_grad):
    params = tuple((member.astype(jnp.float32) for member in (first_gain, first_bias, input_weight, query_bias, value_bias, output_weight, output_bias, scale_one, second_gain, second_bias, up_weight, up_bias, down_weight, down_bias, scale_two)))
    groups = TOKENS // SLOTS
    width = HEADS * HEAD_DIM
    inputs = tokens.astype(jnp.float32).reshape(groups, SLOTS, width)
    segments = segment_ids.reshape(groups, SLOTS)
    cotangents = out_grad.astype(jnp.float32).reshape(groups, SLOTS, width)

    def accumulate(totals, member):
        group_in, group_seg, group_cot = member
        allowed = group_seg[:, None] == group_seg[None, :]
        validity = (group_seg >= 0).astype(jnp.float32)[:, None]
        result, pullback = jax.vjp(lambda values, weights: group_forward(values, allowed, weights), group_in, params)
        grad_in, grad_params = pullback(group_cot * validity)
        totals = jax.tree.map(jnp.add, totals, grad_params)
        return (totals, (result.astype(jnp.bfloat16), grad_in.astype(jnp.bfloat16)))
    initial = tuple((jnp.zeros_like(member) for member in params))
    totals, (results, grads_in) = lax.scan(accumulate, initial, (inputs, segments, cotangents))
    return (results.reshape(TOKENS, width), grads_in.reshape(TOKENS, width), totals[0], totals[1], totals[2], totals[3], totals[4], totals[5], totals[6], totals[7], totals[8], totals[9], totals[10], totals[11], totals[12], totals[13], totals[14])
```

```python
import math

import jax
import jax.numpy as jnp
from jax import lax
from jax.sharding import PartitionSpec as P

HEADS = 16
HEAD_DIM = 64
epsilon = 1e-06
masked_value = -1000000000.0
bf16 = jnp.bfloat16
f32 = jnp.float32


def product(left, right):
    return jnp.dot(left, right, preferred_element_type=f32)


def product_left(left, right):
    return lax.dot_general(left, right, (((0,), (0,)), ((), ())), preferred_element_type=f32)


def product_right(left, right):
    return lax.dot_general(left, right, (((1,), (1,)), ((), ())), preferred_element_type=f32)


def normalize(values):
    center = values - jnp.mean(values, axis=1, keepdims=True)
    spread = lax.rsqrt(jnp.mean(center * center, axis=1, keepdims=True) + epsilon)
    return (center * spread, spread)


def normalize_back(grad_normed, normed, spread):
    return spread * (
        grad_normed
        - jnp.mean(grad_normed, axis=1, keepdims=True)
        - normed * jnp.mean(grad_normed * normed, axis=1, keepdims=True)
    )


def gelu_pair(before):
    normal_cdf = 0.5 * (1.0 + lax.erf(before * (1.0 / math.sqrt(2.0))))
    density = jnp.exp(-0.5 * before * before) * (1.0 / math.sqrt(2.0 * math.pi))
    return (before * normal_cdf, normal_cdf + before * density)


def swap(x, axis, k):
    count = lax.axis_size(axis)
    return lax.ppermute(x, axis, [(i, i ^ k) for i in range(count)])


def from_others(x):
    return [x] + [swap(x, "seq", k) for k in range(1, lax.axis_size("seq"))]


def exchange(blocks):
    return [blocks[0]] + [swap(blocks[k], "seq", k) for k in range(1, len(blocks))]


def gather_fsdp(x):
    count = lax.axis_size("fsdp")
    f = lax.axis_index("fsdp")
    same = [x] + [swap(x, "fsdp", 2 * k) for k in range(1, count // 2)]
    other = swap(jnp.stack(same), "fsdp", 1)
    out = jnp.zeros((count,) + x.shape, x.dtype)
    for k in range(count // 2):
        out = lax.dynamic_update_index_in_dim(out, same[k], f ^ (2 * k), 0)
        out = lax.dynamic_update_index_in_dim(out, other[k], f ^ (2 * k + 1), 0)
    return out


def scatter_fsdp(g):
    count = g.shape[0]
    f = lax.axis_index("fsdp")
    z, core = f // 2, f % 2
    pairs = g.reshape((count // 2, 2) + g.shape[1:])
    mine = lax.dynamic_index_in_dim(pairs, core, 1, keepdims=False)
    theirs = lax.dynamic_index_in_dim(pairs, 1 - core, 1, keepdims=False)
    sums = (mine.astype(f32) + swap(theirs, "fsdp", 1).astype(f32)).astype(bf16)
    total = lax.dynamic_index_in_dim(sums, z, 0, keepdims=False).astype(f32)
    for k in range(1, count // 2):
        block = lax.dynamic_index_in_dim(sums, z ^ k, 0, keepdims=False)
        total = total + swap(block, "fsdp", 2 * k).astype(f32)
    return total


def attend(triple, segments, heads):
    rows = triple.shape[0]
    parts = triple.reshape(rows, heads, 3, HEAD_DIM)
    outs = []
    logsums = []
    same = segments[:, None] == segments[None, :]
    for h in range(heads):
        q, k, v = parts[:, h, 0], parts[:, h, 1], parts[:, h, 2]
        scores = jnp.where(same, product_right(q, k) * HEAD_DIM**-0.5, masked_value)
        highest = jnp.max(scores, axis=1, keepdims=True)
        powers = jnp.exp(scores - highest)
        totals = jnp.sum(powers, axis=1, keepdims=True)
        outs.append(product((powers / totals).astype(bf16), v).astype(bf16))
        logsums.append(highest + jnp.log(totals))
    return jnp.concatenate(outs, axis=1), logsums


def attend_back(triple, segments, logsums, grad, heads):
    rows = triple.shape[0]
    parts = triple.reshape(rows, heads, 3, HEAD_DIM)
    same = segments[:, None] == segments[None, :]
    outs = []
    for h in range(heads):
        q, k, v = parts[:, h, 0], parts[:, h, 1], parts[:, h, 2]
        g = grad[:, h * HEAD_DIM : (h + 1) * HEAD_DIM]
        scores = jnp.where(same, product_right(q, k) * HEAD_DIM**-0.5, masked_value)
        weights = jnp.exp(scores - logsums[h])
        grad_v = product_left(weights.astype(bf16), g)
        grad_weights = product_right(g, v)
        dots = jnp.sum(weights * grad_weights, axis=1, keepdims=True)
        grad_scores = (weights * (grad_weights - dots)).astype(bf16)
        grad_q = product(grad_scores, k) * HEAD_DIM**-0.5
        grad_k = product_left(grad_scores, q) * HEAD_DIM**-0.5
        outs.extend([grad_q, grad_k, grad_v])
    return jnp.concatenate(outs, axis=1).astype(bf16)


def body(
    tokens,
    segment_ids,
    first_gain,
    first_bias,
    input_weight,
    query_bias,
    value_bias,
    output_weight,
    output_bias,
    scale_one,
    second_gain,
    second_bias,
    up_weight,
    up_bias,
    down_weight,
    down_bias,
    scale_two,
    out_grad,
):
    members = lax.axis_size("seq")
    fsdp = lax.axis_size("fsdp")
    s = lax.axis_index("seq")
    rows, width = tokens.shape
    heads = HEADS // members
    own_cols = 3 * HEAD_DIM * heads
    part = width // members
    shard = input_weight.shape[0]
    ff_shard = down_weight.shape[0]
    ff_part = ff_shard // members

    local_vectors = (
        first_gain,
        first_bias,
        query_bias,
        value_bias,
        output_bias,
        scale_one,
        second_gain,
        second_bias,
        up_bias,
        down_bias,
        scale_two,
    )
    widths = [v.shape[0] for v in local_vectors]
    packed_width = sum(widths)

    own_in = lax.dynamic_slice_in_dim(input_weight, s * own_cols, own_cols, 1)
    own_out = lax.dynamic_slice_in_dim(output_weight, s * part, part, 1)
    own_up = lax.dynamic_slice_in_dim(
        up_weight.reshape(shard, fsdp, ff_shard), s * ff_part, ff_part, 2
    ).reshape(shard, fsdp * ff_part)
    own_down = lax.dynamic_slice_in_dim(down_weight, s * ff_part, ff_part, 0)

    vectors = gather_fsdp(jnp.concatenate(local_vectors)[None, :])[:, 0]
    w_in = gather_fsdp(own_in).reshape(width, own_cols)
    w_out_part = gather_fsdp(own_out).reshape(width, part)
    w_up = gather_fsdp(own_up).reshape(width, fsdp * ff_part)
    w_down = gather_fsdp(own_down).reshape(fsdp * ff_part, width)
    w_out = jnp.zeros((width, width), bf16)
    for k, block in enumerate(from_others(w_out_part)):
        w_out = lax.dynamic_update_slice_in_dim(w_out, block, (s ^ k) * part, 1)

    pieces = []
    offset = 0
    for size in widths:
        pieces.append(vectors[:, offset : offset + size].reshape(-1).astype(f32))
        offset += size
    (
        gain_one,
        offset_one,
        bias_query,
        bias_value,
        bias_output,
        factor_one,
        gain_two,
        offset_two,
        bias_up,
        bias_down,
        factor_two,
    ) = pieces
    own_bias_up = lax.dynamic_slice_in_dim(
        bias_up.reshape(fsdp, ff_shard), s * ff_part, ff_part, 1
    ).reshape(-1)
    own_query = lax.dynamic_slice_in_dim(bias_query, s * part, part, 0)
    own_value = lax.dynamic_slice_in_dim(bias_value, s * part, part, 0)

    inputs = jnp.concatenate(from_others(tokens), axis=0).astype(f32)
    out_grads = jnp.concatenate(from_others(out_grad), axis=0).astype(f32)
    segments = jnp.concatenate(
        [lax.dynamic_slice_in_dim(segment_ids, (s ^ k) * rows, rows, 0) for k in range(members)]
    )

    normed_one, spread_one = normalize(inputs)
    hidden_one = (normed_one * gain_one + offset_one).astype(bf16)
    bias_own = jnp.stack(
        [
            own_query.reshape(heads, HEAD_DIM),
            jnp.zeros((heads, HEAD_DIM), f32),
            own_value.reshape(heads, HEAD_DIM),
        ],
        axis=1,
    ).reshape(-1)
    triple = (product(hidden_one, w_in) + bias_own).astype(bf16)
    attended_own, logsums = attend(triple, segments, heads)

    attended = jnp.zeros((members * rows, width), bf16)
    for k, block in enumerate(from_others(attended_own)):
        block = block.reshape(members, rows, part)
        block = jnp.concatenate([block[j ^ k] for j in range(members)], axis=0)
        attended = lax.dynamic_update_slice_in_dim(attended, block, (s ^ k) * part, 1)

    branch_one = product(attended, w_out) + bias_output
    middle = inputs + factor_one * branch_one
    normed_two, spread_two = normalize(middle)
    hidden_two = (normed_two * gain_two + offset_two).astype(bf16)
    before = product(hidden_two, w_up) + own_bias_up
    activated_full, slope = gelu_pair(before)
    activated = activated_full.astype(bf16)

    grads = out_grads * (segments >= 0).astype(f32)[:, None]
    grad_two = (grads * factor_two).astype(bf16)
    grad_before = (product_right(grad_two, w_down) * slope).astype(bf16)
    partial_hidden_two = product_right(grad_before, w_up)
    grad_hidden_two = sum(
        block.astype(f32)
        for block in exchange(
            [partial_hidden_two[:rows]]
            + [partial_hidden_two[k * rows : (k + 1) * rows].astype(bf16) for k in range(1, members)]
        )
    )

    partial_two = product(activated, w_down)
    branch_two = bias_down + sum(
        block.astype(f32)
        for block in exchange(
            [partial_two[:rows]]
            + [partial_two[k * rows : (k + 1) * rows].astype(bf16) for k in range(1, members)]
        )
    )
    own_middle, own_grad = middle[:rows], grads[:rows]
    layer_out = (own_middle + factor_two * branch_two).astype(bf16)
    grad_factor_two = jnp.sum(own_grad * branch_two, axis=0)
    grad_bias_down = jnp.sum(grad_two[:rows].astype(f32), axis=0)
    grad_bias_up = jnp.sum(grad_before.astype(f32), axis=0)

    own_normed_two = normed_two[:rows]
    grad_gain_two = jnp.sum(grad_hidden_two * own_normed_two, axis=0)
    grad_offset_two = jnp.sum(grad_hidden_two, axis=0)
    grad_middle = own_grad + normalize_back(
        grad_hidden_two * gain_two, own_normed_two, spread_two[:rows]
    )
    grad_factor_one = jnp.sum(grad_middle * branch_one[:rows], axis=0)
    grad_one = (grad_middle * factor_one).astype(bf16)
    grad_bias_output = jnp.sum(grad_one.astype(f32), axis=0)
    grad_attended = product_right(grad_one, w_out).astype(bf16)

    def columns(x, k):
        return lax.dynamic_slice_in_dim(x, (s ^ k) * part, part, 1)

    grad_heads = jnp.concatenate(
        exchange([columns(grad_attended, k) for k in range(members)]), axis=0
    )
    grad_one_cols = jnp.concatenate(exchange([columns(grad_one, k) for k in range(members)]), axis=0)
    grad_triple = attend_back(triple, segments, logsums, grad_heads, heads)
    partial_hidden_one = product_right(grad_triple, w_in)
    grad_hidden_one = sum(
        block.astype(f32)
        for block in exchange(
            [partial_hidden_one[:rows]]
            + [partial_hidden_one[k * rows : (k + 1) * rows].astype(bf16) for k in range(1, members)]
        )
    )
    own_normed_one = normed_one[:rows]
    grad_gain_one = jnp.sum(grad_hidden_one * own_normed_one, axis=0)
    grad_offset_one = jnp.sum(grad_hidden_one, axis=0)
    tokens_grad = (
        grad_middle
        + normalize_back(grad_hidden_one * gain_one, own_normed_one, spread_one[:rows])
    ).astype(bf16)

    def own_share(left, right, lead):
        full = product_left(left, right).astype(bf16)
        return scatter_fsdp(full.reshape(fsdp, lead, full.shape[1])).astype(bf16)

    share_down = own_share(activated, grad_two, ff_part)
    share_up = own_share(hidden_two, grad_before, shard)
    share_out = own_share(attended, grad_one_cols, shard)
    share_in = own_share(hidden_one, grad_triple, shard)

    grad_down = jnp.zeros(down_weight.shape, f32)
    for k, block in enumerate(from_others(share_down)):
        grad_down = lax.dynamic_update_slice_in_dim(
            grad_down, block.astype(f32), (s ^ k) * ff_part, 0
        )
    grad_up = jnp.zeros((shard, fsdp, ff_shard), f32)
    for k, block in enumerate(from_others(share_up)):
        grad_up = lax.dynamic_update_slice_in_dim(
            grad_up, block.astype(f32).reshape(shard, fsdp, ff_part), (s ^ k) * ff_part, 2
        )
    grad_up = grad_up.reshape(up_weight.shape)
    grad_out = jnp.zeros(output_weight.shape, f32)
    for k, block in enumerate(from_others(share_out)):
        grad_out = lax.dynamic_update_slice_in_dim(
            grad_out, block.astype(f32), (s ^ k) * part, 1
        )
    grad_in = jnp.zeros(input_weight.shape, f32)
    for k, block in enumerate(from_others(share_in)):
        grad_in = lax.dynamic_update_slice_in_dim(
            grad_in, block.astype(f32), (s ^ k) * own_cols, 1
        )

    triple_sums = jnp.sum(grad_triple.astype(f32), axis=0).reshape(heads, 3, HEAD_DIM)

    def placed(x, total):
        return lax.dynamic_update_slice_in_dim(
            jnp.zeros((total,), f32), x.reshape(-1), s * x.size, 0
        )

    grad_bias_up_full = lax.dynamic_update_slice_in_dim(
        jnp.zeros((fsdp, ff_shard), f32), grad_bias_up.reshape(fsdp, ff_part), s * ff_part, 1
    )
    vector_grads = (
        grad_gain_one,
        grad_offset_one,
        placed(triple_sums[:, 0], width),
        placed(triple_sums[:, 2], width),
        grad_bias_output,
        grad_factor_one,
        grad_gain_two,
        grad_offset_two,
        grad_bias_up_full,
        grad_bias_down,
        grad_factor_two,
    )
    packed = jnp.concatenate([v.reshape(fsdp, -1) for v in vector_grads], axis=1)
    packed = sum(from_others(packed))
    vector_total = scatter_fsdp(packed.astype(bf16)[:, None, :])[0]
    outs = []
    offset = 0
    for size in widths:
        outs.append(vector_total[offset : offset + size])
        offset += size
    return (
        layer_out,
        tokens_grad,
        outs[0],
        outs[1],
        grad_in,
        outs[2],
        outs[3],
        grad_out,
        outs[4],
        outs[5],
        outs[6],
        outs[7],
        grad_up,
        outs[8],
        grad_down,
        outs[9],
        outs[10],
    )


def solution(mesh):
    rows, vec, mat = P(("fsdp", "seq"), None), P("fsdp"), P("fsdp", None)
    return jax.shard_map(
        body,
        mesh=mesh,
        in_specs=(
            rows, vec, vec, vec, mat, vec, vec, mat, vec,
            vec, vec, vec, mat, vec, mat, vec, vec, rows,
        ),
        out_specs=(
            rows, rows, vec, vec, mat, vec, vec, mat, vec,
            vec, vec, vec, mat, vec, mat, vec, vec,
        ),
        check_vma=False,
    )
```

```python
import math

import jax
import jax.numpy as jnp
from jax import lax
from jax.experimental import pallas as pl
from jax.experimental.pallas import tpu as pltpu
from jax.sharding import PartitionSpec as P

HEADS = 16
HEAD_DIM = 64
epsilon = 1e-06
masked_value = -1000000000.0
bf16 = jnp.bfloat16
f32 = jnp.float32


def product(left, right):
    return jnp.dot(left, right, preferred_element_type=f32)


def product_left(left, right):
    return lax.dot_general(left, right, (((0,), (0,)), ((), ())), preferred_element_type=f32)


def product_right(left, right):
    return lax.dot_general(left, right, (((1,), (1,)), ((), ())), preferred_element_type=f32)


def normalize(values):
    center = values - jnp.mean(values, axis=1, keepdims=True)
    spread = lax.rsqrt(jnp.mean(center * center, axis=1, keepdims=True) + epsilon)
    return (center * spread, spread)


def normalize_back(grad_normed, normed, spread):
    return spread * (
        grad_normed
        - jnp.mean(grad_normed, axis=1, keepdims=True)
        - normed * jnp.mean(grad_normed * normed, axis=1, keepdims=True)
    )


def gelu_pair(before):
    normal_cdf = 0.5 * (1.0 + lax.erf(before * (1.0 / math.sqrt(2.0))))
    density = jnp.exp(-0.5 * before * before) * (1.0 / math.sqrt(2.0 * math.pi))
    return (before * normal_cdf, normal_cdf + before * density)


def swap(x, axis, k):
    count = lax.axis_size(axis)
    return lax.ppermute(x, axis, [(i, i ^ k) for i in range(count)])


def from_others(x):
    return [x] + [swap(x, "seq", k) for k in range(1, lax.axis_size("seq"))]


def exchange(blocks):
    return [blocks[0]] + [swap(blocks[k], "seq", k) for k in range(1, len(blocks))]


def gather_fsdp(x):
    count = lax.axis_size("fsdp")
    f = lax.axis_index("fsdp")
    same = [x] + [swap(x, "fsdp", 2 * k) for k in range(1, count // 2)]
    other = swap(jnp.stack(same), "fsdp", 1)
    out = jnp.zeros((count,) + x.shape, x.dtype)
    for k in range(count // 2):
        out = lax.dynamic_update_index_in_dim(out, same[k], f ^ (2 * k), 0)
        out = lax.dynamic_update_index_in_dim(out, other[k], f ^ (2 * k + 1), 0)
    return out


def scatter_fsdp(g):
    count = g.shape[0]
    f = lax.axis_index("fsdp")
    z, core = f // 2, f % 2
    pairs = g.reshape((count // 2, 2) + g.shape[1:])
    mine = lax.dynamic_index_in_dim(pairs, core, 1, keepdims=False)
    theirs = lax.dynamic_index_in_dim(pairs, 1 - core, 1, keepdims=False)
    sums = (mine.astype(f32) + swap(theirs, "fsdp", 1).astype(f32)).astype(bf16)
    total = lax.dynamic_index_in_dim(sums, z, 0, keepdims=False).astype(f32)
    for k in range(1, count // 2):
        block = lax.dynamic_index_in_dim(sums, z ^ k, 0, keepdims=False)
        total = total + swap(block, "fsdp", 2 * k).astype(f32)
    return total


def attend(triple, segments, heads):
    rows = triple.shape[0]
    parts = triple.reshape(rows, heads, 3, HEAD_DIM)
    outs = []
    logsums = []
    same = segments[:, None] == segments[None, :]
    for h in range(heads):
        q, k, v = parts[:, h, 0], parts[:, h, 1], parts[:, h, 2]
        scores = jnp.where(same, product_right(q, k) * HEAD_DIM**-0.5, masked_value)
        highest = jnp.max(scores, axis=1, keepdims=True)
        powers = jnp.exp(scores - highest)
        totals = jnp.sum(powers, axis=1, keepdims=True)
        outs.append(product((powers / totals).astype(bf16), v).astype(bf16))
        logsums.append(highest + jnp.log(totals))
    return jnp.concatenate(outs, axis=1), logsums


def attend_back(triple, segments, logsums, grad, heads):
    rows = triple.shape[0]
    parts = triple.reshape(rows, heads, 3, HEAD_DIM)
    same = segments[:, None] == segments[None, :]
    outs = []
    for h in range(heads):
        q, k, v = parts[:, h, 0], parts[:, h, 1], parts[:, h, 2]
        g = grad[:, h * HEAD_DIM : (h + 1) * HEAD_DIM]
        scores = jnp.where(same, product_right(q, k) * HEAD_DIM**-0.5, masked_value)
        weights = jnp.exp(scores - logsums[h])
        grad_v = product_left(weights.astype(bf16), g)
        grad_weights = product_right(g, v)
        dots = jnp.sum(weights * grad_weights, axis=1, keepdims=True)
        grad_scores = (weights * (grad_weights - dots)).astype(bf16)
        grad_q = product(grad_scores, k) * HEAD_DIM**-0.5
        grad_k = product_left(grad_scores, q) * HEAD_DIM**-0.5
        outs.extend([grad_q, grad_k, grad_v])
    return jnp.concatenate(outs, axis=1).astype(bf16)


def body_any(
    tokens,
    segment_ids,
    first_gain,
    first_bias,
    input_weight,
    query_bias,
    value_bias,
    output_weight,
    output_bias,
    scale_one,
    second_gain,
    second_bias,
    up_weight,
    up_bias,
    down_weight,
    down_bias,
    scale_two,
    out_grad,
):
    members = lax.axis_size("seq")
    fsdp = lax.axis_size("fsdp")
    s = lax.axis_index("seq")
    rows, width = tokens.shape
    heads = HEADS // members
    own_cols = 3 * HEAD_DIM * heads
    part = width // members
    shard = input_weight.shape[0]
    ff_shard = down_weight.shape[0]
    ff_part = ff_shard // members

    local_vectors = (
        first_gain,
        first_bias,
        query_bias,
        value_bias,
        output_bias,
        scale_one,
        second_gain,
        second_bias,
        up_bias,
        down_bias,
        scale_two,
    )
    widths = [v.shape[0] for v in local_vectors]
    packed_width = sum(widths)

    own_in = lax.dynamic_slice_in_dim(input_weight, s * own_cols, own_cols, 1)
    own_out = lax.dynamic_slice_in_dim(output_weight, s * part, part, 1)
    own_up = lax.dynamic_slice_in_dim(
        up_weight.reshape(shard, fsdp, ff_shard), s * ff_part, ff_part, 2
    ).reshape(shard, fsdp * ff_part)
    own_down = lax.dynamic_slice_in_dim(down_weight, s * ff_part, ff_part, 0)

    vectors = gather_fsdp(jnp.concatenate(local_vectors)[None, :])[:, 0]
    w_in = gather_fsdp(own_in).reshape(width, own_cols)
    w_out_part = gather_fsdp(own_out).reshape(width, part)
    w_up = gather_fsdp(own_up).reshape(width, fsdp * ff_part)
    w_down = gather_fsdp(own_down).reshape(fsdp * ff_part, width)
    w_out = jnp.zeros((width, width), bf16)
    for k, block in enumerate(from_others(w_out_part)):
        w_out = lax.dynamic_update_slice_in_dim(w_out, block, (s ^ k) * part, 1)

    pieces = []
    offset = 0
    for size in widths:
        pieces.append(vectors[:, offset : offset + size].reshape(-1).astype(f32))
        offset += size
    (
        gain_one,
        offset_one,
        bias_query,
        bias_value,
        bias_output,
        factor_one,
        gain_two,
        offset_two,
        bias_up,
        bias_down,
        factor_two,
    ) = pieces
    own_bias_up = lax.dynamic_slice_in_dim(
        bias_up.reshape(fsdp, ff_shard), s * ff_part, ff_part, 1
    ).reshape(-1)
    own_query = lax.dynamic_slice_in_dim(bias_query, s * part, part, 0)
    own_value = lax.dynamic_slice_in_dim(bias_value, s * part, part, 0)

    inputs = jnp.concatenate(from_others(tokens), axis=0).astype(f32)
    out_grads = jnp.concatenate(from_others(out_grad), axis=0).astype(f32)
    segments = jnp.concatenate(
        [lax.dynamic_slice_in_dim(segment_ids, (s ^ k) * rows, rows, 0) for k in range(members)]
    )

    normed_one, spread_one = normalize(inputs)
    hidden_one = (normed_one * gain_one + offset_one).astype(bf16)
    bias_own = jnp.stack(
        [
            own_query.reshape(heads, HEAD_DIM),
            jnp.zeros((heads, HEAD_DIM), f32),
            own_value.reshape(heads, HEAD_DIM),
        ],
        axis=1,
    ).reshape(-1)
    triple = (product(hidden_one, w_in) + bias_own).astype(bf16)
    attended_own, logsums = attend(triple, segments, heads)

    attended = jnp.zeros((members * rows, width), bf16)
    for k, block in enumerate(from_others(attended_own)):
        block = block.reshape(members, rows, part)
        block = jnp.concatenate([block[j ^ k] for j in range(members)], axis=0)
        attended = lax.dynamic_update_slice_in_dim(attended, block, (s ^ k) * part, 1)

    branch_one = product(attended, w_out) + bias_output
    middle = inputs + factor_one * branch_one
    normed_two, spread_two = normalize(middle)
    hidden_two = (normed_two * gain_two + offset_two).astype(bf16)
    before = product(hidden_two, w_up) + own_bias_up
    activated_full, slope = gelu_pair(before)
    activated = activated_full.astype(bf16)

    grads = out_grads * (segments >= 0).astype(f32)[:, None]
    grad_two = (grads * factor_two).astype(bf16)
    grad_before = (product_right(grad_two, w_down) * slope).astype(bf16)
    partial_hidden_two = product_right(grad_before, w_up)
    grad_hidden_two = sum(
        block.astype(f32)
        for block in exchange(
            [partial_hidden_two[:rows]]
            + [partial_hidden_two[k * rows : (k + 1) * rows].astype(bf16) for k in range(1, members)]
        )
    )

    partial_two = product(activated, w_down)
    branch_two = bias_down + sum(
        block.astype(f32)
        for block in exchange(
            [partial_two[:rows]]
            + [partial_two[k * rows : (k + 1) * rows].astype(bf16) for k in range(1, members)]
        )
    )
    own_middle, own_grad = middle[:rows], grads[:rows]
    layer_out = (own_middle + factor_two * branch_two).astype(bf16)
    grad_factor_two = jnp.sum(own_grad * branch_two, axis=0)
    grad_bias_down = jnp.sum(grad_two[:rows].astype(f32), axis=0)
    grad_bias_up = jnp.sum(grad_before.astype(f32), axis=0)

    own_normed_two = normed_two[:rows]
    grad_gain_two = jnp.sum(grad_hidden_two * own_normed_two, axis=0)
    grad_offset_two = jnp.sum(grad_hidden_two, axis=0)
    grad_middle = own_grad + normalize_back(
        grad_hidden_two * gain_two, own_normed_two, spread_two[:rows]
    )
    grad_factor_one = jnp.sum(grad_middle * branch_one[:rows], axis=0)
    grad_one = (grad_middle * factor_one).astype(bf16)
    grad_bias_output = jnp.sum(grad_one.astype(f32), axis=0)
    grad_attended = product_right(grad_one, w_out).astype(bf16)

    def columns(x, k):
        return lax.dynamic_slice_in_dim(x, (s ^ k) * part, part, 1)

    grad_heads = jnp.concatenate(
        exchange([columns(grad_attended, k) for k in range(members)]), axis=0
    )
    grad_one_cols = jnp.concatenate(exchange([columns(grad_one, k) for k in range(members)]), axis=0)
    grad_triple = attend_back(triple, segments, logsums, grad_heads, heads)
    partial_hidden_one = product_right(grad_triple, w_in)
    grad_hidden_one = sum(
        block.astype(f32)
        for block in exchange(
            [partial_hidden_one[:rows]]
            + [partial_hidden_one[k * rows : (k + 1) * rows].astype(bf16) for k in range(1, members)]
        )
    )
    own_normed_one = normed_one[:rows]
    grad_gain_one = jnp.sum(grad_hidden_one * own_normed_one, axis=0)
    grad_offset_one = jnp.sum(grad_hidden_one, axis=0)
    tokens_grad = (
        grad_middle
        + normalize_back(grad_hidden_one * gain_one, own_normed_one, spread_one[:rows])
    ).astype(bf16)

    def own_share(left, right, lead):
        full = product_left(left, right).astype(bf16)
        return scatter_fsdp(full.reshape(fsdp, lead, full.shape[1])).astype(bf16)

    share_down = own_share(activated, grad_two, ff_part)
    share_up = own_share(hidden_two, grad_before, shard)
    share_out = own_share(attended, grad_one_cols, shard)
    share_in = own_share(hidden_one, grad_triple, shard)

    grad_down = jnp.zeros(down_weight.shape, f32)
    for k, block in enumerate(from_others(share_down)):
        grad_down = lax.dynamic_update_slice_in_dim(
            grad_down, block.astype(f32), (s ^ k) * ff_part, 0
        )
    grad_up = jnp.zeros((shard, fsdp, ff_shard), f32)
    for k, block in enumerate(from_others(share_up)):
        grad_up = lax.dynamic_update_slice_in_dim(
            grad_up, block.astype(f32).reshape(shard, fsdp, ff_part), (s ^ k) * ff_part, 2
        )
    grad_up = grad_up.reshape(up_weight.shape)
    grad_out = jnp.zeros(output_weight.shape, f32)
    for k, block in enumerate(from_others(share_out)):
        grad_out = lax.dynamic_update_slice_in_dim(
            grad_out, block.astype(f32), (s ^ k) * part, 1
        )
    grad_in = jnp.zeros(input_weight.shape, f32)
    for k, block in enumerate(from_others(share_in)):
        grad_in = lax.dynamic_update_slice_in_dim(
            grad_in, block.astype(f32), (s ^ k) * own_cols, 1
        )

    triple_sums = jnp.sum(grad_triple.astype(f32), axis=0).reshape(heads, 3, HEAD_DIM)

    def placed(x, total):
        return lax.dynamic_update_slice_in_dim(
            jnp.zeros((total,), f32), x.reshape(-1), s * x.size, 0
        )

    grad_bias_up_full = lax.dynamic_update_slice_in_dim(
        jnp.zeros((fsdp, ff_shard), f32), grad_bias_up.reshape(fsdp, ff_part), s * ff_part, 1
    )
    vector_grads = (
        grad_gain_one,
        grad_offset_one,
        placed(triple_sums[:, 0], width),
        placed(triple_sums[:, 2], width),
        grad_bias_output,
        grad_factor_one,
        grad_gain_two,
        grad_offset_two,
        grad_bias_up_full,
        grad_bias_down,
        grad_factor_two,
    )
    packed = jnp.concatenate([v.reshape(fsdp, -1) for v in vector_grads], axis=1)
    packed = lax.psum(packed, "seq")
    vector_total = scatter_fsdp(packed.astype(bf16)[:, None, :])[0]
    outs = []
    offset = 0
    for size in widths:
        outs.append(vector_total[offset : offset + size])
        offset += size
    return (
        layer_out,
        tokens_grad,
        outs[0],
        outs[1],
        grad_in,
        outs[2],
        outs[3],
        grad_out,
        outs[4],
        outs[5],
        outs[6],
        outs[7],
        grad_up,
        outs[8],
        grad_down,
        outs[9],
        outs[10],
    )


def spec(kind=pltpu.VMEM):
    return pl.BlockSpec(memory_space=kind)


def shape(dims, kind):
    return jax.ShapeDtypeStruct(dims, kind)


def call(kernel, where, ins, outs, flops=0, name=None, scratch=(), in_hbm=(), out_hbm=False):
    moved = sum(x.size * x.dtype.itemsize for x in ins) + sum(
        math.prod(o.shape) * o.dtype.itemsize for o in outs
    )
    in_specs = [spec(pl.ANY) if i in in_hbm else spec() for i in range(len(ins))]
    return pl.pallas_call(
        kernel,
        out_shape=outs,
        in_specs=[spec(pltpu.SMEM)] + in_specs,
        out_specs=[spec(pl.ANY) if out_hbm else spec() for _ in outs],
        scratch_shapes=list(scratch),
        compiler_params=pltpu.CompilerParams(vmem_limit_bytes=50 * 1024 * 1024),
        cost_estimate=pl.CostEstimate(flops=flops, bytes_accessed=moved, transcendentals=0),
        name=name,
    )(where, *ins)


def at(index, size):
    return pl.ds(pl.multiple_of(index * size, size), size)


def prepare(where, w_in, w_out, w_up, w_down, tokens, grad, vec, first, second, rows, sems):
    s = where[1]
    shard, parts = w_in.shape[0], first.shape[1]
    cols, out_cols = w_in.shape[1] // 4, w_out.shape[1] // 4
    lane, wide = 128, w_up.shape[1] // 8
    pairs = [
        (w_in.at[:, at(s, cols)], first.at[0:shard, 0:cols]),
        (w_out.at[:, at(s, out_cols)], first.at[0:shard, cols:parts]),
        (vec, first.at[shard : shard + 16]),
        (tokens, rows.at[0:shard]),
        (grad, rows.at[shard : 2 * shard]),
        (w_down.at[at(s, lane)], second.at[shard : 2 * shard]),
    ]
    for i in range(8):
        lanes = pl.ds(pl.multiple_of(i * wide + s * lane, lane), lane)
        pairs.append((w_up.at[:, lanes], second.at[0:shard, i * lane : (i + 1) * lane]))
    copies = [pltpu.make_async_copy(a, b, sems.at[i]) for i, (a, b) in enumerate(pairs)]
    for copy in copies:
        copy.start()
    for copy in copies:
        copy.wait()


def place_first(where, *refs):
    blocks, (w_in, w_out, vecs) = refs[:8], refs[8:]
    for j in range(8):
        n = where[0] ^ j
        w_in[at(n, 128)] = blocks[j][0:128, 0:768]
        w_out[at(n, 128)] = blocks[j][0:128, 768:1024]
        vecs[:, at(n, 128)] = blocks[j][128:144, 0:128].astype(f32)


def column_segments(where, seg):
    return jnp.concatenate([seg[at(where[1] ^ k, 128)] for k in range(4)], axis=0)


def row_segments(where, seg):
    return jnp.concatenate([seg[:, at(where[1] ^ k, 128)] for k in range(4)], axis=1)


def attention(where, t0, t1, t2, t3, w_in, vecs, seg_col, seg_row, triple, attended, logsum, hidden):
    gain, offset = vecs[0:1], vecs[1:2]
    for k, ref in enumerate((t0, t1, t2, t3)):
        normed, _ = normalize(ref[0:128].astype(f32))
        hidden[k * 128 : (k + 1) * 128] = (normed * gain + offset).astype(bf16)
    own = at(where[1], 256)
    query, value = vecs[2:3, own], vecs[3:4, own]
    zero = jnp.zeros((1, 64), f32)
    pieces = []
    for h in range(4):
        pieces += [query[:, h * 64 : (h + 1) * 64], zero, value[:, h * 64 : (h + 1) * 64]]
    triple[...] = (product(hidden[...], w_in[...]) + jnp.concatenate(pieces, axis=1)).astype(bf16)
    same = column_segments(where, seg_col) == row_segments(where, seg_row)
    outs = []
    for h in range(4):
        q, k, v = (triple[:, h * 192 + c * 64 : h * 192 + (c + 1) * 64] for c in range(3))
        scores = jnp.where(same, product_right(q, k) * HEAD_DIM**-0.5, masked_value)
        highest = jnp.max(scores, axis=1, keepdims=True)
        powers = jnp.exp(scores - highest)
        totals = jnp.sum(powers, axis=1, keepdims=True)
        probs = (powers * (1.0 / totals)).astype(bf16)
        outs.append(product(probs, v).astype(bf16))
        logsum[:, h : h + 1] = highest + jnp.log(totals)
    attended[...] = jnp.concatenate(outs, axis=1)


def project(
    where, a0, a1, a2, a3, w0, w1, w2, w3, t0, t1, t2, t3, vecs, full, hidden, own_middle, own_branch, branch
):
    for k, ref in enumerate((a0, a1, a2, a3)):
        cols = at(where[1] ^ k, 256)
        for j in range(4):
            full[j * 128 : (j + 1) * 128, cols] = ref[(j ^ k) * 128 : ((j ^ k) + 1) * 128]
    for k, ref in enumerate((w0, w1, w2, w3)):
        branch[:, at(where[1] ^ k, 256)] = product(full[...], ref[...])
    for r, ref in enumerate((t0, t1, t2, t3)):
        rows = slice(r * 128, (r + 1) * 128)
        piece = branch[rows] + vecs[4:5]
        middle = ref[0:128].astype(f32) + vecs[5:6] * piece
        normed, _ = normalize(middle)
        hidden[rows] = (normed * vecs[6:7] + vecs[7:8]).astype(bf16)
        if r == 0:
            own_middle[...] = middle
            own_branch[...] = piece


def feed(where, *refs):
    hidden, blocks, tokens, (vecs, seg_col) = refs[0], refs[1:9], refs[9:13], refs[13:15]
    w_down, act, grad_two, grad_before, sums, p0, p1, p2, p3, w_up = refs[15:]
    for j in range(8):
        rows = at(where[0] ^ j, 128)
        w_up[rows] = blocks[j][0:128]
        w_down[rows] = blocks[j][128:256]
    valid = (column_segments(where, seg_col) >= 0).astype(f32)
    for k in range(4):
        rows = slice(k * 128, (k + 1) * 128)
        grad = tokens[k][128:256].astype(f32) * valid[rows]
        grad_two[rows] = (grad * vecs[9:10]).astype(bf16)
    bias = vecs[pl.ds(10 + where[1], 1)]
    for c in range(4):
        cols = slice(c * 256, (c + 1) * 256)
        before = product(hidden[...], w_up[:, cols]) + bias[:, cols]
        value, slope = gelu_pair(before)
        act[:, cols] = value.astype(bf16)
        back = (product_right(grad_two[...], w_down[cols]) * slope).astype(bf16)
        grad_before[:, cols] = back
        sums[:, cols] = jnp.sum(back.astype(f32), axis=0, keepdims=True)
    p0[...] = product_right(grad_before[0:128], w_up[...])
    for k, ref in ((1, p1), (2, p2), (3, p3)):
        ref[...] = product_right(grad_before[k * 128 : (k + 1) * 128], w_up[...]).astype(bf16)


def halves(where, mine, theirs, k, first_row, result):
    rows = pl.ds(first_row, 128)

    @pl.when(where[0] % 2 == 0)
    def _():
        mine[k, rows] = result[0:128]
        theirs[k, rows] = result[128:256]

    @pl.when(where[0] % 2 == 1)
    def _():
        mine[k, rows] = result[128:256]
        theirs[k, rows] = result[0:128]


def feed_weights(where, *refs):
    hidden, grad_before, act, grad_two, w_down, t0, t1, t2, t3, vecs, seg_col = refs[:11]
    mine, theirs, sums, o0, o1, o2, o3 = refs[11:]
    for k in range(4):
        cols = at((where[0] // 2) ^ k, 256)
        up = product_left(hidden[:, cols], grad_before[...]).astype(bf16)
        halves(where, mine, theirs, k, 0, up)
        down = product_left(act[:, cols], grad_two[...]).astype(bf16)
        halves(where, mine, theirs, k, 128, down)
    valid = (column_segments(where, seg_col) >= 0).astype(f32)
    scale = jnp.zeros((1, 1024), f32)
    for k, (ref, out) in enumerate(((t0, o0), (t1, o1), (t2, o2), (t3, o3))):
        rows = slice(k * 128, (k + 1) * 128)
        part = product(act[rows], w_down[...])
        grad = ref[128:256].astype(f32) * valid[rows]
        out[...] = part.astype(out.dtype)
        if k == 0:
            part = part + vecs[8:9]
        scale = scale + jnp.sum(grad * part, axis=0, keepdims=True)
    sums[0:1] = jnp.sum(grad_two[0:128].astype(f32), axis=0, keepdims=True)
    sums[1:2] = scale


def middle_back(
    where, p0, p1, p2, p3, own_middle, own_branch, t0, seg_col, vecs, w0, w1, w2, w3,
    grad_middle, sums, m0, m1, m2, m3, attended, one,
):
    total = p0[...] + p1[...].astype(f32) + p2[...].astype(f32) + p3[...].astype(f32)
    normed, spread = normalize(own_middle[...])
    valid = (seg_col[at(where[1], 128)] >= 0).astype(f32)
    back = t0[128:256].astype(f32) * valid + normalize_back(total * vecs[6:7], normed, spread)
    grad_middle[...] = back
    grad_one = (back * vecs[5:6]).astype(bf16)
    one[...] = grad_one
    sums[0:1] = jnp.sum(total * normed, axis=0, keepdims=True)
    sums[1:2] = jnp.sum(total, axis=0, keepdims=True)
    sums[2:3] = jnp.sum(back * own_branch[...], axis=0, keepdims=True)
    sums[3:4] = jnp.sum(grad_one.astype(f32), axis=0, keepdims=True)
    result = jnp.zeros((128, 1024), f32)
    for k, ref in enumerate((w0, w1, w2, w3)):
        result = result + product_right(one[:, at(where[1] ^ k, 256)], ref[...])
    attended[...] = result.astype(bf16)
    for k, ref in enumerate((m0, m1, m2, m3)):
        cols = at(where[1] ^ k, 256)
        ref[0:128] = attended[:, cols]
        ref[128:256] = one[:, cols]


def attention_back(
    where, triple, logsum, m0, m1, m2, m3, seg_col, seg_row, w_in, t0, t1, t2, t3, o1, o2, o3,
    grad_triple, sums, own, n1, n2, n3,
):
    same = column_segments(where, seg_col) == row_segments(where, seg_row)
    grads = jnp.concatenate([m[0:128] for m in (m0, m1, m2, m3)], axis=0)
    pieces = []
    for h in range(4):
        q, k, v = (triple[:, h * 192 + c * 64 : h * 192 + (c + 1) * 64] for c in range(3))
        g = grads[:, h * 64 : (h + 1) * 64]
        scores = jnp.where(same, product_right(q, k) * HEAD_DIM**-0.5, masked_value)
        weights = jnp.exp(scores - logsum[:, h : h + 1])
        grad_v = product_left(weights.astype(bf16), g)
        grad_weights = product_right(g, v)
        dots = jnp.sum(weights * grad_weights, axis=1, keepdims=True)
        grad_scores = (weights * (grad_weights - dots)).astype(bf16)
        grad_q = product(grad_scores, k) * HEAD_DIM**-0.5
        grad_k = product_left(grad_scores, q) * HEAD_DIM**-0.5
        pieces += [grad_q.astype(bf16), grad_k.astype(bf16), grad_v.astype(bf16)]
    whole = jnp.concatenate(pieces, axis=1)
    grad_triple[...] = whole
    columns = jnp.sum(whole.astype(f32), axis=0, keepdims=True)
    sums[...] = jnp.zeros(sums.shape, f32)
    lanes = at(where[1], 256)
    for row, c in ((2, 0), (3, 2)):
        sums[row : row + 1, lanes] = jnp.concatenate(
            [columns[:, h * 192 + c * 64 : h * 192 + (c + 1) * 64] for h in range(4)], axis=1
        )
    gain = jnp.zeros((1, 1024), f32)
    offset = jnp.zeros((1, 1024), f32)
    sent = ((t0, own, None), (t1, n1, o1), (t2, n2, o2), (t3, n3, o3))
    for k, (ref, out, other) in enumerate(sent):
        part = product_right(grad_triple[k * 128 : (k + 1) * 128], w_in[...])
        normed, _ = normalize(ref[0:128].astype(f32))
        gain = gain + jnp.sum(part * normed, axis=0, keepdims=True)
        offset = offset + jnp.sum(part, axis=0, keepdims=True)
        if k == 0:
            out[...] = part
        else:
            out[0:128] = part.astype(bf16)
            out[128:256] = other[...]
    sums[0:1] = gain
    sums[1:2] = offset


def attention_weights(
    where, hidden, grad_triple, attended, m0, m1, m2, m3, up_sums, two_sums, mid_sums, one_sums,
    mine, theirs, vecs,
):
    ones = jnp.concatenate([m[128:256] for m in (m0, m1, m2, m3)], axis=0)
    vecs[...] = jnp.zeros(vecs.shape, f32)
    vecs[0:4] = one_sums[...]
    vecs[4:5] = mid_sums[3:4]
    vecs[5:6] = mid_sums[2:3]
    vecs[6:8] = mid_sums[0:2]
    vecs[8:10] = two_sums[0:2]
    vecs[pl.ds(10 + where[1], 1)] = up_sums[...]
    blank = jnp.zeros((16, 896), bf16)
    core = where[0] % 2
    for k in range(4):
        pair = (where[0] // 2) ^ k
        cols = at(pair, 256)
        left = product_left(hidden[:, cols], grad_triple[...]).astype(bf16)
        right = product_left(attended[:, cols], ones).astype(bf16)
        halves(where, mine, theirs, k, 0, jnp.concatenate([left, right], axis=1))
        for ref, half in ((mine, core), (theirs, 1 - core)):
            block = vecs[:, at(2 * pair + half, 128)].astype(bf16)
            ref[k, 128:144] = jnp.concatenate([block, blank], axis=1)


def finish_rows(where, own, n1, n2, n3, own_two, own_middle, grad_middle, t0, vecs, out, grad):
    total = own[...] + sum(n[0:128].astype(f32) for n in (n1, n2, n3))
    two = own_two[...] + sum(n[128:256].astype(f32) for n in (n1, n2, n3)) + vecs[8:9]
    out[...] = (own_middle[...] + vecs[9:10] * two).astype(bf16)
    normed, spread = normalize(t0[0:128].astype(f32))
    grad[...] = (grad_middle[...] + normalize_back(total * vecs[0:1], normed, spread)).astype(bf16)


def finish_feed(where, s0, s1, s2, s3, up, down):
    for k, ref in enumerate((s0, s1, s2, s3)):
        m = where[1] ^ k
        down[at(m, 128)] = ref[128:256].astype(f32)
        for n in range(8):
            lanes = pl.ds(pl.multiple_of(n * 512 + m * 128, 128), 128)
            up[:, lanes] = ref[0:128, n * 128 : (n + 1) * 128].astype(f32)


def finish_attention(where, s0, s1, s2, s3, w_in, w_out, *refs):
    outs, held = refs[:-1], refs[-1]
    for k, ref in enumerate((s0, s1, s2, s3)):
        m = where[1] ^ k
        w_in[:, at(m, 768)] = ref[0:128, 0:768].astype(f32)
        w_out[:, at(m, 256)] = ref[0:128, 768:1024].astype(f32)
        held[m] = ref[128:144, 0:128].astype(f32)
    total = held[0] + held[1] + held[2] + held[3]
    for i in range(10):
        outs[i][...] = total[i : i + 1]
    outs[10][...] = jnp.concatenate([total[i : i + 1] for i in range(10, 14)], axis=1)


def gather_blocks(x):
    out = []
    for k in range(4):
        block = swap(x, "fsdp", 2 * k) if k else x
        out += [block, swap(block, "fsdp", 1)]
    return out


def scatter_blocks(mine, theirs):
    other = swap(theirs, "fsdp", 1)
    sums = [(mine[k].astype(f32) + other[k].astype(f32)).astype(bf16) for k in range(4)]
    total = sums[0].astype(f32)
    for k in range(1, 4):
        total = total + swap(sums[k], "fsdp", 2 * k).astype(f32)
    return total.astype(bf16)


def body(*args):
    tokens, input_weight, up_weight = args[0], args[4], args[12]
    fits = (
        lax.axis_size("seq") == 4
        and lax.axis_size("fsdp") == 8
        and tokens.shape == (128, 1024)
        and input_weight.shape == (128, 3072)
        and up_weight.shape == (128, 4096)
    )
    return body_fast(*args) if fits else body_any(*args)


def body_fast(
    tokens,
    segment_ids,
    first_gain,
    first_bias,
    input_weight,
    query_bias,
    value_bias,
    output_weight,
    output_bias,
    scale_one,
    second_gain,
    second_bias,
    up_weight,
    up_bias,
    down_weight,
    down_bias,
    scale_two,
    out_grad,
):
    where = jnp.stack([lax.axis_index("fsdp"), lax.axis_index("seq")]).astype(jnp.int32)
    vectors = (
        first_gain, first_bias, query_bias, value_bias, output_bias,
        scale_one, second_gain, second_bias, down_bias, scale_two,
    )
    packed = jnp.pad(up_bias.reshape(4, 128), ((10, 2), (0, 896)))
    for i, v in enumerate(vectors):
        packed = packed + jnp.pad(v.reshape(1, 128), ((i, 15 - i), (0, 896)))
    seg_col, seg_row = segment_ids.reshape(512, 1), segment_ids.reshape(1, 512)
    mat = shape((512, 1024), bf16)
    rows_f, rows_b = shape((128, 1024), f32), shape((128, 1024), bf16)

    first, second, rows = call(
        prepare,
        where,
        [input_weight, output_weight, up_weight, down_weight, tokens, out_grad, packed],
        [shape((144, 1024), bf16), shape((256, 1024), bf16), shape((256, 1024), bf16)],
        name="prepare",
        scratch=[pltpu.SemaphoreType.DMA((14,))],
        in_hbm=range(7),
        out_hbm=True,
    )
    shared = from_others(rows)
    first_blocks = gather_blocks(first)
    w_in, w_out_own, vecs = call(
        place_first,
        where,
        first_blocks,
        [shape((1024, 768), bf16), shape((1024, 256), bf16), shape((16, 1024), f32)],
        name="place_first",
    )
    second, _ = lax.optimization_barrier((second, vecs))
    second_blocks = gather_blocks(second)
    w_out = from_others(w_out_own)
    triple, attended_own, logsum, hidden_one = call(
        attention,
        where,
        shared + [w_in, vecs, seg_col, seg_row],
        [shape((512, 768), bf16), shape((512, 256), bf16), shape((512, 128), f32), mat],
        flops=2 * 512 * (1024 * 768 + 4 * 512 * 128),
        name="attention",
    )
    attended, hidden_two, own_middle, own_branch = call(
        project,
        where,
        from_others(attended_own) + w_out + shared + [vecs],
        [mat, mat, rows_f, rows_f],
        flops=2 * 512 * 1024 * 1024,
        name="project",
        scratch=[pltpu.VMEM((512, 1024), f32)],
    )
    w_down, act, grad_two, grad_before, up_sums, *partial = call(
        feed,
        where,
        [hidden_two] + second_blocks + shared + [vecs, seg_col],
        [shape((1024, 1024), bf16), mat, mat, mat, shape((1, 1024), f32), rows_f, rows_b, rows_b, rows_b],
        flops=3 * 2 * 512 * 1024 * 1024,
        name="feed",
        scratch=[pltpu.VMEM((1024, 1024), bf16)],
    )
    second_mine, second_theirs, two_sums, *two = call(
        feed_weights,
        where,
        [hidden_two, grad_before, act, grad_two, w_down] + shared + [vecs, seg_col],
        [shape((4, 256, 1024), bf16)] * 2 + [shape((2, 1024), f32), rows_f, rows_b, rows_b, rows_b],
        flops=3 * 2 * 512 * 1024 * 1024,
        name="feed_weights",
    )
    grad_middle, mid_sums, *messages = call(
        middle_back,
        where,
        exchange(partial) + [own_middle, own_branch, shared[0], seg_col, vecs] + w_out,
        [rows_f, shape((4, 1024), f32)] + [shape((256, 256), bf16)] * 4,
        flops=2 * 128 * 1024 * 1024,
        name="middle_back",
        scratch=[pltpu.VMEM((128, 1024), bf16), pltpu.VMEM((128, 1024), bf16)],
    )
    second_mine, second_theirs, messages = lax.optimization_barrier(
        (second_mine, second_theirs, messages)
    )
    got = exchange(messages)
    grad_triple, one_sums, own_one, *last = call(
        attention_back,
        where,
        [triple, logsum] + got + [seg_col, seg_row, w_in] + shared + two[1:],
        [shape((512, 768), bf16), shape((4, 1024), f32), rows_f] + [shape((256, 1024), bf16)] * 3,
        flops=2 * 512 * (1024 * 768 + 4 * 512 * 64 * 5),
        name="attention_back",
    )
    first_mine, first_theirs = call(
        attention_weights,
        where,
        [hidden_one, grad_triple, attended] + got + [up_sums, two_sums, mid_sums, one_sums],
        [shape((4, 144, 1024), bf16)] * 2,
        flops=2 * 512 * 1024 * 1024,
        name="attention_weights",
        scratch=[pltpu.VMEM((16, 1024), f32)],
    )
    layer_out, tokens_grad = call(
        finish_rows,
        where,
        exchange([own_one] + last) + [two[0], own_middle, grad_middle, shared[0], vecs],
        [rows_b, rows_b],
        name="finish_rows",
    )
    second_share = scatter_blocks(second_mine, second_theirs)
    grad_up, grad_down = call(
        finish_feed,
        where,
        from_others(second_share),
        [shape((128, 4096), f32), shape((512, 1024), f32)],
        name="finish_feed",
    )
    first_share = scatter_blocks(first_mine, first_theirs)
    grad_in, grad_out, *small = call(
        finish_attention,
        where,
        from_others(first_share),
        [shape((128, 3072), f32), rows_f] + [shape((1, 128), f32)] * 10 + [shape((1, 512), f32)],
        name="finish_attention",
        scratch=[pltpu.VMEM((4, 16, 128), f32)],
    )
    g = [v.reshape(-1) for v in small]
    return (
        layer_out, tokens_grad, g[0], g[1], grad_in, g[2], g[3], grad_out, g[4],
        g[5], g[6], g[7], grad_up, g[10], grad_down, g[8], g[9],
    )


def solution(mesh):
    rows, vec, mat = P(("fsdp", "seq"), None), P("fsdp"), P("fsdp", None)
    return jax.shard_map(
        body,
        mesh=mesh,
        in_specs=(
            rows, vec, vec, vec, mat, vec, vec, mat, vec,
            vec, vec, vec, mat, vec, mat, vec, vec, rows,
        ),
        out_specs=(
            rows, rows, vec, vec, mat, vec, vec, mat, vec,
            vec, vec, vec, mat, vec, mat, vec, vec,
        ),
        check_vma=False,
    )
```

```python
import math

import jax
import jax.numpy as jnp
from jax import lax
from jax.experimental import pallas as pl
from jax.experimental.pallas import tpu as pltpu
from jax.sharding import PartitionSpec as P

HEADS = 16
HEAD_DIM = 64
epsilon = 1e-06
masked_value = -1000000000.0
bf16 = jnp.bfloat16
f32 = jnp.float32


def product(left, right):
    return jnp.dot(left, right, preferred_element_type=f32)


def product_left(left, right):
    return lax.dot_general(left, right, (((0,), (0,)), ((), ())), preferred_element_type=f32)


def product_right(left, right):
    return lax.dot_general(left, right, (((1,), (1,)), ((), ())), preferred_element_type=f32)


def normalize(values):
    center = values - jnp.mean(values, axis=1, keepdims=True)
    spread = lax.rsqrt(jnp.mean(center * center, axis=1, keepdims=True) + epsilon)
    return (center * spread, spread)


def normalize_back(grad_normed, normed, spread):
    return spread * (
        grad_normed
        - jnp.mean(grad_normed, axis=1, keepdims=True)
        - normed * jnp.mean(grad_normed * normed, axis=1, keepdims=True)
    )


def gelu_pair(before):
    normal_cdf = 0.5 * (1.0 + lax.erf(before * (1.0 / math.sqrt(2.0))))
    density = jnp.exp(-0.5 * before * before) * (1.0 / math.sqrt(2.0 * math.pi))
    return (before * normal_cdf, normal_cdf + before * density)


def swap(x, axis, k):
    count = lax.axis_size(axis)
    return lax.ppermute(x, axis, [(i, i ^ k) for i in range(count)])


def from_others(x):
    return [x] + [swap(x, "seq", k) for k in range(1, lax.axis_size("seq"))]


def exchange(blocks):
    return [blocks[0]] + [swap(blocks[k], "seq", k) for k in range(1, len(blocks))]


def gather_fsdp(x):
    count = lax.axis_size("fsdp")
    f = lax.axis_index("fsdp")
    same = [x] + [swap(x, "fsdp", 2 * k) for k in range(1, count // 2)]
    other = swap(jnp.stack(same), "fsdp", 1)
    out = jnp.zeros((count,) + x.shape, x.dtype)
    for k in range(count // 2):
        out = lax.dynamic_update_index_in_dim(out, same[k], f ^ (2 * k), 0)
        out = lax.dynamic_update_index_in_dim(out, other[k], f ^ (2 * k + 1), 0)
    return out


def scatter_fsdp(g):
    count = g.shape[0]
    f = lax.axis_index("fsdp")
    z, core = f // 2, f % 2
    pairs = g.reshape((count // 2, 2) + g.shape[1:])
    mine = lax.dynamic_index_in_dim(pairs, core, 1, keepdims=False)
    theirs = lax.dynamic_index_in_dim(pairs, 1 - core, 1, keepdims=False)
    sums = (mine.astype(f32) + swap(theirs, "fsdp", 1).astype(f32)).astype(bf16)
    total = lax.dynamic_index_in_dim(sums, z, 0, keepdims=False).astype(f32)
    for k in range(1, count // 2):
        block = lax.dynamic_index_in_dim(sums, z ^ k, 0, keepdims=False)
        total = total + swap(block, "fsdp", 2 * k).astype(f32)
    return total


def attend(triple, segments, heads):
    rows = triple.shape[0]
    parts = triple.reshape(rows, heads, 3, HEAD_DIM)
    outs = []
    logsums = []
    same = segments[:, None] == segments[None, :]
    for h in range(heads):
        q, k, v = parts[:, h, 0], parts[:, h, 1], parts[:, h, 2]
        scores = jnp.where(same, product_right(q, k) * HEAD_DIM**-0.5, masked_value)
        highest = jnp.max(scores, axis=1, keepdims=True)
        powers = jnp.exp(scores - highest)
        totals = jnp.sum(powers, axis=1, keepdims=True)
        outs.append(product((powers / totals).astype(bf16), v).astype(bf16))
        logsums.append(highest + jnp.log(totals))
    return jnp.concatenate(outs, axis=1), logsums


def attend_back(triple, segments, logsums, grad, heads):
    rows = triple.shape[0]
    parts = triple.reshape(rows, heads, 3, HEAD_DIM)
    same = segments[:, None] == segments[None, :]
    outs = []
    for h in range(heads):
        q, k, v = parts[:, h, 0], parts[:, h, 1], parts[:, h, 2]
        g = grad[:, h * HEAD_DIM : (h + 1) * HEAD_DIM]
        scores = jnp.where(same, product_right(q, k) * HEAD_DIM**-0.5, masked_value)
        weights = jnp.exp(scores - logsums[h])
        grad_v = product_left(weights.astype(bf16), g)
        grad_weights = product_right(g, v)
        dots = jnp.sum(weights * grad_weights, axis=1, keepdims=True)
        grad_scores = (weights * (grad_weights - dots)).astype(bf16)
        grad_q = product(grad_scores, k) * HEAD_DIM**-0.5
        grad_k = product_left(grad_scores, q) * HEAD_DIM**-0.5
        outs.extend([grad_q, grad_k, grad_v])
    return jnp.concatenate(outs, axis=1).astype(bf16)


def body_any(
    tokens,
    segment_ids,
    first_gain,
    first_bias,
    input_weight,
    query_bias,
    value_bias,
    output_weight,
    output_bias,
    scale_one,
    second_gain,
    second_bias,
    up_weight,
    up_bias,
    down_weight,
    down_bias,
    scale_two,
    out_grad,
):
    members = lax.axis_size("seq")
    fsdp = lax.axis_size("fsdp")
    s = lax.axis_index("seq")
    rows, width = tokens.shape
    heads = HEADS // members
    own_cols = 3 * HEAD_DIM * heads
    part = width // members
    shard = input_weight.shape[0]
    ff_shard = down_weight.shape[0]
    ff_part = ff_shard // members

    local_vectors = (
        first_gain,
        first_bias,
        query_bias,
        value_bias,
        output_bias,
        scale_one,
        second_gain,
        second_bias,
        up_bias,
        down_bias,
        scale_two,
    )
    widths = [v.shape[0] for v in local_vectors]
    packed_width = sum(widths)

    own_in = lax.dynamic_slice_in_dim(input_weight, s * own_cols, own_cols, 1)
    own_out = lax.dynamic_slice_in_dim(output_weight, s * part, part, 1)
    own_up = lax.dynamic_slice_in_dim(
        up_weight.reshape(shard, fsdp, ff_shard), s * ff_part, ff_part, 2
    ).reshape(shard, fsdp * ff_part)
    own_down = lax.dynamic_slice_in_dim(down_weight, s * ff_part, ff_part, 0)

    vectors = gather_fsdp(jnp.concatenate(local_vectors)[None, :])[:, 0]
    w_in = gather_fsdp(own_in).reshape(width, own_cols)
    w_out_part = gather_fsdp(own_out).reshape(width, part)
    w_up = gather_fsdp(own_up).reshape(width, fsdp * ff_part)
    w_down = gather_fsdp(own_down).reshape(fsdp * ff_part, width)
    w_out = jnp.zeros((width, width), bf16)
    for k, block in enumerate(from_others(w_out_part)):
        w_out = lax.dynamic_update_slice_in_dim(w_out, block, (s ^ k) * part, 1)

    pieces = []
    offset = 0
    for size in widths:
        pieces.append(vectors[:, offset : offset + size].reshape(-1).astype(f32))
        offset += size
    (
        gain_one,
        offset_one,
        bias_query,
        bias_value,
        bias_output,
        factor_one,
        gain_two,
        offset_two,
        bias_up,
        bias_down,
        factor_two,
    ) = pieces
    own_bias_up = lax.dynamic_slice_in_dim(
        bias_up.reshape(fsdp, ff_shard), s * ff_part, ff_part, 1
    ).reshape(-1)
    own_query = lax.dynamic_slice_in_dim(bias_query, s * part, part, 0)
    own_value = lax.dynamic_slice_in_dim(bias_value, s * part, part, 0)

    inputs = jnp.concatenate(from_others(tokens), axis=0).astype(f32)
    out_grads = jnp.concatenate(from_others(out_grad), axis=0).astype(f32)
    segments = jnp.concatenate(
        [lax.dynamic_slice_in_dim(segment_ids, (s ^ k) * rows, rows, 0) for k in range(members)]
    )

    normed_one, spread_one = normalize(inputs)
    hidden_one = (normed_one * gain_one + offset_one).astype(bf16)
    bias_own = jnp.stack(
        [
            own_query.reshape(heads, HEAD_DIM),
            jnp.zeros((heads, HEAD_DIM), f32),
            own_value.reshape(heads, HEAD_DIM),
        ],
        axis=1,
    ).reshape(-1)
    triple = (product(hidden_one, w_in) + bias_own).astype(bf16)
    attended_own, logsums = attend(triple, segments, heads)

    attended = jnp.zeros((members * rows, width), bf16)
    for k, block in enumerate(from_others(attended_own)):
        block = block.reshape(members, rows, part)
        block = jnp.concatenate([block[j ^ k] for j in range(members)], axis=0)
        attended = lax.dynamic_update_slice_in_dim(attended, block, (s ^ k) * part, 1)

    branch_one = product(attended, w_out) + bias_output
    middle = inputs + factor_one * branch_one
    normed_two, spread_two = normalize(middle)
    hidden_two = (normed_two * gain_two + offset_two).astype(bf16)
    before = product(hidden_two, w_up) + own_bias_up
    activated_full, slope = gelu_pair(before)
    activated = activated_full.astype(bf16)

    grads = out_grads * (segments >= 0).astype(f32)[:, None]
    grad_two = (grads * factor_two).astype(bf16)
    grad_before = (product_right(grad_two, w_down) * slope).astype(bf16)
    partial_hidden_two = product_right(grad_before, w_up)
    grad_hidden_two = sum(
        block.astype(f32)
        for block in exchange(
            [partial_hidden_two[:rows]]
            + [partial_hidden_two[k * rows : (k + 1) * rows].astype(bf16) for k in range(1, members)]
        )
    )

    partial_two = product(activated, w_down)
    branch_two = bias_down + sum(
        block.astype(f32)
        for block in exchange(
            [partial_two[:rows]]
            + [partial_two[k * rows : (k + 1) * rows].astype(bf16) for k in range(1, members)]
        )
    )
    own_middle, own_grad = middle[:rows], grads[:rows]
    layer_out = (own_middle + factor_two * branch_two).astype(bf16)
    grad_factor_two = jnp.sum(own_grad * branch_two, axis=0)
    grad_bias_down = jnp.sum(grad_two[:rows].astype(f32), axis=0)
    grad_bias_up = jnp.sum(grad_before.astype(f32), axis=0)

    own_normed_two = normed_two[:rows]
    grad_gain_two = jnp.sum(grad_hidden_two * own_normed_two, axis=0)
    grad_offset_two = jnp.sum(grad_hidden_two, axis=0)
    grad_middle = own_grad + normalize_back(
        grad_hidden_two * gain_two, own_normed_two, spread_two[:rows]
    )
    grad_factor_one = jnp.sum(grad_middle * branch_one[:rows], axis=0)
    grad_one = (grad_middle * factor_one).astype(bf16)
    grad_bias_output = jnp.sum(grad_one.astype(f32), axis=0)
    grad_attended = product_right(grad_one, w_out).astype(bf16)

    def columns(x, k):
        return lax.dynamic_slice_in_dim(x, (s ^ k) * part, part, 1)

    grad_heads = jnp.concatenate(
        exchange([columns(grad_attended, k) for k in range(members)]), axis=0
    )
    grad_one_cols = jnp.concatenate(exchange([columns(grad_one, k) for k in range(members)]), axis=0)
    grad_triple = attend_back(triple, segments, logsums, grad_heads, heads)
    partial_hidden_one = product_right(grad_triple, w_in)
    grad_hidden_one = sum(
        block.astype(f32)
        for block in exchange(
            [partial_hidden_one[:rows]]
            + [partial_hidden_one[k * rows : (k + 1) * rows].astype(bf16) for k in range(1, members)]
        )
    )
    own_normed_one = normed_one[:rows]
    grad_gain_one = jnp.sum(grad_hidden_one * own_normed_one, axis=0)
    grad_offset_one = jnp.sum(grad_hidden_one, axis=0)
    tokens_grad = (
        grad_middle
        + normalize_back(grad_hidden_one * gain_one, own_normed_one, spread_one[:rows])
    ).astype(bf16)

    def own_share(left, right, lead):
        full = product_left(left, right).astype(bf16)
        return scatter_fsdp(full.reshape(fsdp, lead, full.shape[1])).astype(bf16)

    share_down = own_share(activated, grad_two, ff_part)
    share_up = own_share(hidden_two, grad_before, shard)
    share_out = own_share(attended, grad_one_cols, shard)
    share_in = own_share(hidden_one, grad_triple, shard)

    grad_down = jnp.zeros(down_weight.shape, f32)
    for k, block in enumerate(from_others(share_down)):
        grad_down = lax.dynamic_update_slice_in_dim(
            grad_down, block.astype(f32), (s ^ k) * ff_part, 0
        )
    grad_up = jnp.zeros((shard, fsdp, ff_shard), f32)
    for k, block in enumerate(from_others(share_up)):
        grad_up = lax.dynamic_update_slice_in_dim(
            grad_up, block.astype(f32).reshape(shard, fsdp, ff_part), (s ^ k) * ff_part, 2
        )
    grad_up = grad_up.reshape(up_weight.shape)
    grad_out = jnp.zeros(output_weight.shape, f32)
    for k, block in enumerate(from_others(share_out)):
        grad_out = lax.dynamic_update_slice_in_dim(
            grad_out, block.astype(f32), (s ^ k) * part, 1
        )
    grad_in = jnp.zeros(input_weight.shape, f32)
    for k, block in enumerate(from_others(share_in)):
        grad_in = lax.dynamic_update_slice_in_dim(
            grad_in, block.astype(f32), (s ^ k) * own_cols, 1
        )

    triple_sums = jnp.sum(grad_triple.astype(f32), axis=0).reshape(heads, 3, HEAD_DIM)

    def placed(x, total):
        return lax.dynamic_update_slice_in_dim(
            jnp.zeros((total,), f32), x.reshape(-1), s * x.size, 0
        )

    grad_bias_up_full = lax.dynamic_update_slice_in_dim(
        jnp.zeros((fsdp, ff_shard), f32), grad_bias_up.reshape(fsdp, ff_part), s * ff_part, 1
    )
    vector_grads = (
        grad_gain_one,
        grad_offset_one,
        placed(triple_sums[:, 0], width),
        placed(triple_sums[:, 2], width),
        grad_bias_output,
        grad_factor_one,
        grad_gain_two,
        grad_offset_two,
        grad_bias_up_full,
        grad_bias_down,
        grad_factor_two,
    )
    packed = jnp.concatenate([v.reshape(fsdp, -1) for v in vector_grads], axis=1)
    packed = lax.psum(packed, "seq")
    vector_total = scatter_fsdp(packed.astype(bf16)[:, None, :])[0]
    outs = []
    offset = 0
    for size in widths:
        outs.append(vector_total[offset : offset + size])
        offset += size
    return (
        layer_out,
        tokens_grad,
        outs[0],
        outs[1],
        grad_in,
        outs[2],
        outs[3],
        grad_out,
        outs[4],
        outs[5],
        outs[6],
        outs[7],
        grad_up,
        outs[8],
        grad_down,
        outs[9],
        outs[10],
    )


def spec(kind=pltpu.VMEM):
    return pl.BlockSpec(memory_space=kind)


def shape(dims, kind):
    return jax.ShapeDtypeStruct(dims, kind)


def call(kernel, where, ins, outs, flops=0, name=None, scratch=(), in_hbm=False, limit=50):
    in_specs = [spec(pltpu.HBM) if in_hbm else spec() for _ in ins]
    return pl.pallas_call(
        kernel,
        out_shape=outs,
        in_specs=[spec(pltpu.SMEM)] + in_specs,
        out_specs=[spec() for _ in outs],
        scratch_shapes=list(scratch),
        compiler_params=pltpu.CompilerParams(vmem_limit_bytes=limit * 1024 * 1024),
        cost_estimate=pl.CostEstimate(flops=0, bytes_accessed=0, transcendentals=0),
        name=name,
    )(where, *ins)


def at(index, size):
    return pl.ds(pl.multiple_of(index * size, size), size)


def run_copies(pairs, sems):
    copies = [pltpu.make_async_copy(a, b, sems.at[i]) for i, (a, b) in enumerate(pairs)]
    for copy in copies:
        copy.start()
    return copies


def prepare_first(where, *refs):
    w_in, w_out, tokens, grad, vectors = refs[0], refs[1], refs[2], refs[3], refs[4:15]
    first, rows, held, (pack, sems) = refs[15], refs[16], refs[17:28], refs[28:]
    s = where[1]
    pairs = list(zip(vectors, held)) + [
        (pair[0], pair[1])
        for m in range(4)
        for pair in (
            (w_in.at[:, at(s, 768)], first.at[m, 0:128, 0:768]),
            (w_out.at[:, at(s, 256)], first.at[m, 0:128, 768:1024]),
        )
    ]
    pairs += [(tokens, rows.at[0:128]), (grad, rows.at[128:256])]
    copies = run_copies(pairs, sems)
    for copy in copies[:11]:
        copy.wait()
    pack[...] = jnp.zeros(pack.shape, f32)
    for i in range(10):
        pack[i : i + 1, 0:128] = held[i][...].astype(f32).reshape(1, 128)
    for i in range(4):
        pack[10 + i : 11 + i, 0:128] = (
            held[10][i * 128 : (i + 1) * 128].astype(f32).reshape(1, 128)
        )
    for m in range(4):
        first[m, 128:144] = pack[...].astype(bf16)
    for copy in copies[11:]:
        copy.wait()


def prepare_second(where, w_up, w_down, second, sems):
    s = where[1]
    pairs = [(w_down.at[at(s, 128)], second.at[128:256])]
    for i in range(8):
        lanes = pl.ds(pl.multiple_of(i * 512 + s * 128, 128), 128)
        pairs.append((w_up.at[:, lanes], second.at[0:128, i * 128 : (i + 1) * 128]))
    for copy in run_copies(pairs, sems):
        copy.wait()


def owner(where, t, b):
    return 2 * where[2 + t] + ((where[0] % 2) ^ b)


def place_first(where, own, other, w_in, w_out, vecs):
    for b, blocks in enumerate((own, other)):
        for z in range(4):
            n = 2 * z + ((where[0] % 2) ^ b)
            w_in[at(n, 128)] = blocks[z, 0:128, 0:768]
            w_out[at(n, 128)] = blocks[z, 0:128, 768:1024]
            vecs[:, at(n, 128)] = blocks[z, 128:144, 0:128].astype(f32)


def column_segments(where, seg):
    return jnp.concatenate([seg[at(where[1] ^ k, 128)] for k in range(4)], axis=0)


def row_segments(where, seg):
    return jnp.concatenate([seg[:, at(where[1] ^ k, 128)] for k in range(4)], axis=1)


def attention(where, t0, t1, t2, t3, w_in, vecs, seg_col, seg_row, triple, attended, logsum, hidden):
    gain, offset = vecs[0:1], vecs[1:2]
    for k, ref in enumerate((t0, t1, t2, t3)):
        normed, _ = normalize(ref[0:128].astype(f32))
        hidden[k * 128 : (k + 1) * 128] = (normed * gain + offset).astype(bf16)
    own = at(where[1], 256)
    query, value = vecs[2:3, own], vecs[3:4, own]
    zero = jnp.zeros((1, 64), f32)
    pieces = []
    for h in range(4):
        pieces += [query[:, h * 64 : (h + 1) * 64], zero, value[:, h * 64 : (h + 1) * 64]]
    triple[...] = (product(hidden[...], w_in[...]) + jnp.concatenate(pieces, axis=1)).astype(bf16)
    same = column_segments(where, seg_col) == row_segments(where, seg_row)
    outs = []
    for h in range(4):
        q, k, v = (triple[:, h * 192 + c * 64 : h * 192 + (c + 1) * 64] for c in range(3))
        scores = jnp.where(same, product_right(q, k) * HEAD_DIM**-0.5, masked_value)
        highest = jnp.max(scores, axis=1, keepdims=True)
        powers = jnp.exp(scores - highest)
        totals = jnp.sum(powers, axis=1, keepdims=True)
        probs = (powers * (1.0 / totals)).astype(bf16)
        outs.append(product(probs, v).astype(bf16))
        logsum[:, h : h + 1] = highest + jnp.log(totals)
    whole = jnp.concatenate(outs, axis=1)
    for m in range(4):
        attended[m] = whole


def project(
    where, sent, w0, w1, w2, w3, t0, t1, t2, t3, vecs, full, hidden, own_middle, own_branch, branch
):
    for m in range(4):
        for j in range(4):
            rows = at(where[1] ^ (j ^ m), 128)
            full[j * 128 : (j + 1) * 128, m * 256 : (m + 1) * 256] = sent[m, rows]
    for k, ref in enumerate((w0, w1, w2, w3)):
        branch[:, at(where[1] ^ k, 256)] = product(full[...], ref[...])
    for r, ref in enumerate((t0, t1, t2, t3)):
        rows = slice(r * 128, (r + 1) * 128)
        piece = branch[rows] + vecs[4:5]
        middle = ref[0:128].astype(f32) + vecs[5:6] * piece
        normed, _ = normalize(middle)
        hidden[rows] = (normed * vecs[6:7] + vecs[7:8]).astype(bf16)
        if r == 0:
            own_middle[...] = middle
            own_branch[...] = piece


def feed(where, *refs):
    hidden, blocks, tokens, (vecs, seg_col) = refs[0], refs[1:9], refs[9:13], refs[13:15]
    w_down, act, grad_two, grad_before, sums, p0, p1, p2, p3, w_up = refs[15:]
    for j in range(8):
        rows = at(owner(where, j // 2, j % 2), 128)
        w_up[rows] = blocks[j][0:128]
        w_down[rows] = blocks[j][128:256]
    valid = (column_segments(where, seg_col) >= 0).astype(f32)
    for k in range(4):
        rows = slice(k * 128, (k + 1) * 128)
        grad = tokens[k][128:256].astype(f32) * valid[rows]
        grad_two[rows] = (grad * vecs[9:10]).astype(bf16)
    bias = vecs[pl.ds(10 + where[1], 1)]
    for c in range(4):
        cols = slice(c * 256, (c + 1) * 256)
        before = product(hidden[...], w_up[:, cols]) + bias[:, cols]
        value, slope = gelu_pair(before)
        act[:, cols] = value.astype(bf16)
        back = (product_right(grad_two[...], w_down[cols]) * slope).astype(bf16)
        grad_before[:, cols] = back
        sums[:, cols] = jnp.sum(back.astype(f32), axis=0, keepdims=True)
    p0[...] = product_right(grad_before[0:128], w_up[...])
    for k, ref in ((1, p1), (2, p2), (3, p3)):
        ref[...] = product_right(grad_before[k * 128 : (k + 1) * 128], w_up[...]).astype(bf16)


def core_rows(where, z, own):
    return at(2 * z + ((where[0] % 2) if own else 1 - (where[0] % 2)), 128)


def feed_weights_sent(where, hidden, grad_before, act, grad_two, theirs):
    for k in range(4):
        cols = core_rows(where, k, False)
        theirs[k, 0:128] = product_left(hidden[:, cols], grad_before[...]).astype(bf16)
        theirs[k, 128:256] = product_left(act[:, cols], grad_two[...]).astype(bf16)


def feed_weights(where, *refs):
    hidden, grad_before, act, grad_two, w_down = refs[:5]
    tokens, (vecs, seg_col, mine, sums, *two) = refs[5:9], refs[9:]
    for k in range(4):
        cols = core_rows(where, k, True)
        mine[k, 0:128] = product_left(hidden[:, cols], grad_before[...]).astype(bf16)
        mine[k, 128:256] = product_left(act[:, cols], grad_two[...]).astype(bf16)
    valid = (column_segments(where, seg_col) >= 0).astype(f32)
    scale = jnp.zeros((1, 1024), f32)
    for k in range(4):
        rows = slice(k * 128, (k + 1) * 128)
        part = product(act[rows], w_down[...])
        grad = tokens[k][128:256].astype(f32) * valid[rows]
        two[k][...] = part.astype(bf16)
        if k == 0:
            part = part + vecs[8:9]
        scale = scale + jnp.sum(grad * part, axis=0, keepdims=True)
    sums[0:1] = jnp.sum(grad_two[0:128].astype(f32), axis=0, keepdims=True)
    sums[1:2] = scale


def middle_back(
    where, p0, p1, p2, p3, own_middle, own_branch, tokens, seg_col, vecs, w0, w1, w2, w3,
    grad_middle, sums, m0, m1, m2, m3, attended, one,
):
    total = p0[...] + p1[...].astype(f32) + p2[...].astype(f32) + p3[...].astype(f32)
    normed, spread = normalize(own_middle[...])
    valid = (seg_col[at(where[1], 128)] >= 0).astype(f32)
    back = tokens[128:256].astype(f32) * valid + normalize_back(total * vecs[6:7], normed, spread)
    grad_middle[...] = back
    grad_one = (back * vecs[5:6]).astype(bf16)
    one[...] = grad_one
    sums[0:1] = jnp.sum(total * normed, axis=0, keepdims=True)
    sums[1:2] = jnp.sum(total, axis=0, keepdims=True)
    sums[2:3] = jnp.sum(back * own_branch[...], axis=0, keepdims=True)
    sums[3:4] = jnp.sum(grad_one.astype(f32), axis=0, keepdims=True)
    result = jnp.zeros((128, 1024), f32)
    for k, ref in enumerate((w0, w1, w2, w3)):
        result = result + product_right(one[:, at(where[1] ^ k, 256)], ref[...])
    attended[...] = result.astype(bf16)
    for k, ref in enumerate((m0, m1, m2, m3)):
        cols = at(where[1] ^ k, 256)
        ref[0:128] = attended[:, cols]
        ref[128:256] = one[:, cols]


def attention_back(
    where, triple, logsum, m0, m1, m2, m3, seg_col, seg_row, w_in, t0, t1, t2, t3,
    grad_triple, sums, *last,
):
    same = column_segments(where, seg_col) == row_segments(where, seg_row)
    grads = jnp.concatenate([m[0:128] for m in (m0, m1, m2, m3)], axis=0)
    pieces = []
    for h in range(4):
        q, k, v = (triple[:, h * 192 + c * 64 : h * 192 + (c + 1) * 64] for c in range(3))
        g = grads[:, h * 64 : (h + 1) * 64]
        scores = jnp.where(same, product_right(q, k) * HEAD_DIM**-0.5, masked_value)
        weights = jnp.exp(scores - logsum[:, h : h + 1])
        grad_v = product_left(weights.astype(bf16), g)
        grad_weights = product_right(g, v)
        dots = jnp.sum(weights * grad_weights, axis=1, keepdims=True)
        grad_scores = (weights * (grad_weights - dots)).astype(bf16)
        grad_q = product(grad_scores, k) * HEAD_DIM**-0.5
        grad_k = product_left(grad_scores, q) * HEAD_DIM**-0.5
        pieces += [grad_q.astype(bf16), grad_k.astype(bf16), grad_v.astype(bf16)]
    whole = jnp.concatenate(pieces, axis=1)
    grad_triple[...] = whole
    columns = jnp.sum(whole.astype(f32), axis=0, keepdims=True)
    sums[...] = jnp.zeros(sums.shape, f32)
    lanes = at(where[1], 256)
    for row, c in ((2, 0), (3, 2)):
        sums[row : row + 1, lanes] = jnp.concatenate(
            [columns[:, h * 192 + c * 64 : h * 192 + (c + 1) * 64] for h in range(4)], axis=1
        )
    gain = jnp.zeros((1, 1024), f32)
    offset = jnp.zeros((1, 1024), f32)
    for k, ref in enumerate((t0, t1, t2, t3)):
        part = product_right(grad_triple[k * 128 : (k + 1) * 128], w_in[...])
        normed, _ = normalize(ref[0:128].astype(f32))
        gain = gain + jnp.sum(part * normed, axis=0, keepdims=True)
        offset = offset + jnp.sum(part, axis=0, keepdims=True)
        last[k][...] = part.astype(bf16)
    sums[0:1] = gain
    sums[1:2] = offset


def attention_weights(
    where, hidden, grad_triple, attended, m0, m1, m2, m3, up_sums, two_sums, mid_sums, one_sums,
    mine, theirs, vecs,
):
    ones = jnp.concatenate([m[128:256] for m in (m0, m1, m2, m3)], axis=0)
    vecs[...] = jnp.zeros(vecs.shape, f32)
    vecs[0:4] = one_sums[...]
    vecs[4:5] = mid_sums[3:4]
    vecs[5:6] = mid_sums[2:3]
    vecs[6:8] = mid_sums[0:2]
    vecs[8:10] = two_sums[0:2]
    vecs[pl.ds(10 + where[1], 1)] = up_sums[...]
    blank = jnp.zeros((16, 896), bf16)
    for k in range(4):
        for ref, own in ((mine, True), (theirs, False)):
            cols = core_rows(where, where[2 + k], own)
            ref[k, 0:128, 0:768] = product_left(hidden[:, cols], grad_triple[...]).astype(bf16)
            ref[k, 0:128, 768:1024] = product_left(attended[:, cols], ones).astype(bf16)
            ref[k, 128:144] = jnp.concatenate([vecs[:, cols].astype(bf16), blank], axis=1)


def finish_rows(where, *refs):
    ones, twos, (own_middle, grad_middle, tokens, vecs, out, grad) = refs[:4], refs[4:8], refs[8:]
    total = sum(ref[...].astype(f32) for ref in ones)
    two = sum(ref[...].astype(f32) for ref in twos) + vecs[8:9]
    out[...] = (own_middle[...] + vecs[9:10] * two).astype(bf16)
    normed, spread = normalize(tokens[0:128].astype(f32))
    grad[...] = (grad_middle[...] + normalize_back(total * vecs[0:1], normed, spread)).astype(bf16)


def finish_feed(where, got, up, down):
    for m in range(4):
        down[m * 128 : (m + 1) * 128] = got[m, 128:256].astype(f32)
        for n in range(8):
            lanes = slice(n * 512 + m * 128, n * 512 + (m + 1) * 128)
            up[:, lanes] = got[m, 0:128, n * 128 : (n + 1) * 128].astype(f32)


def finish_attention(where, s0, s1, s2, s3, w_in, w_out, *refs):
    outs, held = refs[:-1], refs[-1]
    for k, ref in enumerate((s0, s1, s2, s3)):
        m = where[1] ^ k
        w_in[:, at(m, 768)] = ref[0:128, 0:768].astype(f32)
        w_out[:, at(m, 256)] = ref[0:128, 768:1024].astype(f32)
        held[m] = ref[128:144, 0:128].astype(f32)
    total = held[0] + held[1] + held[2] + held[3]
    for i in range(10):
        outs[i][...] = total[i : i + 1]
    outs[10][...] = jnp.concatenate([total[i : i + 1] for i in range(10, 14)], axis=1)


def ring(count):
    return list(range(0, count, 2)) + list(range(count - 1, 0, -2))


def step(x, hops=1):
    order = ring(lax.axis_size("fsdp") // 2)
    count = len(order)
    pairs = [(order[i], order[(i + hops) % count]) for i in range(count)]
    return lax.ppermute(x, "fsdp", [(2 * a + c, 2 * b + c) for a, b in pairs for c in (0, 1)])


def along(x):
    count = lax.axis_size("fsdp") // 2
    groups = [[2 * z + c for z in range(count)] for c in (0, 1)]
    return lax.all_to_all(
        x, "fsdp", split_axis=0, concat_axis=0, axis_index_groups=groups, tiled=True
    )


def after(x, *earlier):
    return lax.optimization_barrier((x,) + earlier)[0]


def both_cores(blocks):
    return [b for block in blocks for b in (block, swap(block, "fsdp", 1))]


def pair_sums(mine, theirs):
    return [add(mine[t], theirs[t]) for t in range(4)]


def deal(x):
    return lax.all_to_all(x, "seq", split_axis=0, concat_axis=0, tiled=True)


def share_total(where, parts, out):
    total = sum(parts[z].astype(f32) for z in range(4)).astype(bf16)
    for m in range(4):
        out[m] = total


def deal_total(where, x, name):
    (copies,) = call(share_total, where, [x], [shape(x.shape, bf16)], name=name)
    return deal(copies)


def add(x, y):
    return (x.astype(f32) + y.astype(f32)).astype(bf16)


def body(*args):
    tokens, input_weight, up_weight = args[0], args[4], args[12]
    fits = (
        lax.axis_size("seq") == 4
        and lax.axis_size("fsdp") == 8
        and tokens.shape == (128, 1024)
        and input_weight.shape == (128, 3072)
        and up_weight.shape == (128, 4096)
    )
    return body_fast(*args) if fits else body_any(*args)


def body_fast(
    tokens,
    segment_ids,
    first_gain,
    first_bias,
    input_weight,
    query_bias,
    value_bias,
    output_weight,
    output_bias,
    scale_one,
    second_gain,
    second_bias,
    up_weight,
    up_bias,
    down_weight,
    down_bias,
    scale_two,
    out_grad,
):
    f, s = lax.axis_index("fsdp"), lax.axis_index("seq")
    z = f // 2
    odd = (z ^ (z // 2)) % 2
    where = jnp.stack([f, s, z, z ^ (1 + odd), z ^ 3, z ^ (2 - odd)]).astype(jnp.int32)
    vectors = [
        first_gain, first_bias, query_bias, value_bias, output_bias,
        scale_one, second_gain, second_bias, down_bias, scale_two, up_bias,
    ]
    seg_col, seg_row = segment_ids.reshape(512, 1), segment_ids.reshape(1, 512)
    mat = shape((512, 1024), bf16)
    rows_f, rows_b = shape((128, 1024), f32), shape((128, 1024), bf16)

    first, rows = call(
        prepare_first,
        where,
        [input_weight, output_weight, tokens, out_grad] + vectors,
        [shape((4, 144, 1024), bf16), shape((256, 1024), bf16)],
        name="prepare_first",
        scratch=[pltpu.VMEM(v.shape, bf16) for v in vectors] + [pltpu.VMEM((16, 1024), f32), pltpu.SemaphoreType.DMA((32,))],
        in_hbm=True,
        limit=63,
    )
    shared = from_others(rows)
    first_own = along(first)
    (second,) = call(
        prepare_second,
        where,
        [up_weight, down_weight],
        [shape((256, 1024), bf16)],
        name="prepare_second",
        scratch=[pltpu.SemaphoreType.DMA((36,))],
        in_hbm=True,
        limit=63,
    )
    second_1 = step(after(second, first_own, *shared[1:]))
    w_in, w_out_own, vecs = call(
        place_first,
        where,
        [first_own, swap(after(first_own, second, *shared[1:]), "fsdp", 1)],
        [shape((1024, 768), bf16), shape((1024, 256), bf16), shape((16, 1024), f32)],
        name="place_first",
        limit=63,
    )
    w_out = from_others(w_out_own)
    triple, attended_own, logsum, hidden_one = call(
        attention,
        where,
        shared + [w_in, vecs, seg_col, seg_row],
        [shape((512, 768), bf16), shape((4, 512, 256), bf16), shape((512, 128), f32), mat],
        name="attention",
    )
    second_2 = step(after(second_1, attended_own))
    second_3 = step(after(second_2, *w_out[1:]))
    shares = deal(attended_own)
    attended, hidden_two, own_middle, own_branch = call(
        project,
        where,
        [shares] + w_out + shared + [vecs],
        [mat, mat, rows_f, rows_f],
        name="project",
        scratch=[pltpu.VMEM((512, 1024), f32)],
    )
    w_down, act, grad_two, grad_before, up_sums, *partial = call(
        feed,
        where,
        [hidden_two]
        + both_cores([after(x, shares) for x in (second, second_1, second_2)] + [after(second_3, hidden_two)])
        + shared + [vecs, seg_col],
        [shape((1024, 1024), bf16), mat, mat, mat, shape((1, 1024), f32), rows_f, rows_b, rows_b, rows_b],
        name="feed",
        scratch=[pltpu.VMEM((1024, 1024), bf16)],
    )
    partial = exchange(partial)
    (second_theirs,) = call(
        feed_weights_sent,
        where,
        [hidden_two, grad_before, act, grad_two],
        [shape((4, 256, 1024), bf16)],
        name="feed_weights_sent",
    )
    second_mine, two_sums, *two = call(
        feed_weights,
        where,
        [hidden_two, grad_before, act, grad_two, w_down] + shared + [vecs, seg_col],
        [shape((4, 256, 1024), bf16), shape((2, 1024), f32)] + [rows_b] * 4,
        name="feed_weights",
    )
    second_theirs = swap(after(second_theirs, two[0], *partial[1:]), "fsdp", 1)
    grad_middle, mid_sums, *messages = call(
        middle_back,
        where,
        partial + [own_middle, own_branch, rows, seg_col, vecs] + w_out,
        [rows_f, shape((4, 1024), f32)] + [shape((256, 256), bf16)] * 4,
        name="middle_back",
        scratch=[pltpu.VMEM((128, 1024), bf16), pltpu.VMEM((128, 1024), bf16)],
    )
    got = exchange(messages)
    second_sums = along(add(after(second_mine, messages[1]), second_theirs))
    twos = exchange([two[0]] + [after(x, *got[1:]) for x in two[1:]])
    grad_triple, one_sums, *last = call(
        attention_back,
        where,
        [triple, logsum] + got + [seg_col, seg_row, w_in] + shared,
        [shape((512, 768), bf16), shape((4, 1024), f32)] + [rows_b] * 4,
        flops=20 * 512 * 1024 * 1024,
        name="attention_back",
    )
    grad_triple = after(grad_triple, *twos[1:])
    first_mine, first_theirs = call(
        attention_weights,
        where,
        [hidden_one, grad_triple, attended] + got + [up_sums, two_sums, mid_sums, one_sums],
        [shape((4, 144, 1024), bf16)] * 2,
        flops=20 * 512 * 1024 * 1024,
        name="attention_weights",
        scratch=[pltpu.VMEM((16, 1024), f32)],
    )
    ones = exchange([last[0]] + [after(x, *twos[1:]) for x in last[1:]])
    first_sums = pair_sums(first_mine, swap(first_theirs, "fsdp", 1))
    first_total = step(after(first_sums[1], *ones[1:]))
    layer_out, tokens_grad = call(
        finish_rows,
        where,
        ones + twos + [own_middle, grad_middle, rows, vecs],
        [rows_b, rows_b],
        name="finish_rows",
    )
    grad_up, grad_down = call(
        finish_feed,
        where,
        [deal_total(where, after(second_sums, first_total), "share_feed")],
        [shape((128, 4096), f32), shape((512, 1024), f32)],
        name="finish_feed",
    )
    first_total = step(add(first_total, first_sums[2]))
    first_total = step(after(add(first_total, first_sums[3]), layer_out))
    first_share = from_others(add(first_total, first_sums[0]))
    grad_in, grad_out, *small = call(
        finish_attention,
        where,
        [after(first_share[0], grad_up)] + first_share[1:],
        [shape((128, 3072), f32), rows_f] + [shape((1, 128), f32)] * 10 + [shape((1, 512), f32)],
        name="finish_attention",
        scratch=[pltpu.VMEM((4, 16, 128), f32)],
    )
    g = [v.reshape(-1) for v in small]
    return (
        layer_out, tokens_grad, g[0], g[1], grad_in, g[2], g[3], grad_out, g[4],
        g[5], g[6], g[7], grad_up, g[10], grad_down, g[8], g[9],
    )


def solution(mesh):
    rows, vec, mat = P(("fsdp", "seq"), None), P("fsdp"), P("fsdp", None)
    return jax.shard_map(
        body,
        mesh=mesh,
        in_specs=(
            rows, vec, vec, vec, mat, vec, vec, mat, vec,
            vec, vec, vec, mat, vec, mat, vec, vec, rows,
        ),
        out_specs=(
            rows, rows, vec, vec, mat, vec, vec, mat, vec,
            vec, vec, vec, mat, vec, mat, vec, vec,
        ),
        check_vma=False,
    )
```

```python
import math

import jax
import jax.numpy as jnp
from jax import lax
from jax.experimental import pallas as pl
from jax.experimental.pallas import tpu as pltpu
from jax.sharding import PartitionSpec as P

HEADS = 16
HEAD_DIM = 64
epsilon = 1e-06
masked_value = -1000000000.0
bf16 = jnp.bfloat16
f32 = jnp.float32


def product(left, right):
    return jnp.dot(left, right, preferred_element_type=f32)


def product_left(left, right):
    return lax.dot_general(left, right, (((0,), (0,)), ((), ())), preferred_element_type=f32)


def product_right(left, right):
    return lax.dot_general(left, right, (((1,), (1,)), ((), ())), preferred_element_type=f32)


def normalize(values):
    center = values - jnp.mean(values, axis=1, keepdims=True)
    spread = lax.rsqrt(jnp.mean(center * center, axis=1, keepdims=True) + epsilon)
    return (center * spread, spread)


def normalize_back(grad_normed, normed, spread):
    return spread * (
        grad_normed
        - jnp.mean(grad_normed, axis=1, keepdims=True)
        - normed * jnp.mean(grad_normed * normed, axis=1, keepdims=True)
    )


def gelu_pair(before):
    normal_cdf = 0.5 * (1.0 + lax.erf(before * (1.0 / math.sqrt(2.0))))
    density = jnp.exp(-0.5 * before * before) * (1.0 / math.sqrt(2.0 * math.pi))
    return (before * normal_cdf, normal_cdf + before * density)


def swap(x, axis, k):
    count = lax.axis_size(axis)
    return lax.ppermute(x, axis, [(i, i ^ k) for i in range(count)])


def from_others(x):
    return [x] + [swap(x, "seq", k) for k in range(1, lax.axis_size("seq"))]


def exchange(blocks):
    return [blocks[0]] + [swap(blocks[k], "seq", k) for k in range(1, len(blocks))]


def gather_fsdp(x):
    count = lax.axis_size("fsdp")
    f = lax.axis_index("fsdp")
    same = [x] + [swap(x, "fsdp", 2 * k) for k in range(1, count // 2)]
    other = swap(jnp.stack(same), "fsdp", 1)
    out = jnp.zeros((count,) + x.shape, x.dtype)
    for k in range(count // 2):
        out = lax.dynamic_update_index_in_dim(out, same[k], f ^ (2 * k), 0)
        out = lax.dynamic_update_index_in_dim(out, other[k], f ^ (2 * k + 1), 0)
    return out


def scatter_fsdp(g):
    count = g.shape[0]
    f = lax.axis_index("fsdp")
    z, core = f // 2, f % 2
    pairs = g.reshape((count // 2, 2) + g.shape[1:])
    mine = lax.dynamic_index_in_dim(pairs, core, 1, keepdims=False)
    theirs = lax.dynamic_index_in_dim(pairs, 1 - core, 1, keepdims=False)
    sums = (mine.astype(f32) + swap(theirs, "fsdp", 1).astype(f32)).astype(bf16)
    total = lax.dynamic_index_in_dim(sums, z, 0, keepdims=False).astype(f32)
    for k in range(1, count // 2):
        block = lax.dynamic_index_in_dim(sums, z ^ k, 0, keepdims=False)
        total = total + swap(block, "fsdp", 2 * k).astype(f32)
    return total


def attend(triple, segments, heads):
    rows = triple.shape[0]
    parts = triple.reshape(rows, heads, 3, HEAD_DIM)
    outs = []
    logsums = []
    same = segments[:, None] == segments[None, :]
    for h in range(heads):
        q, k, v = parts[:, h, 0], parts[:, h, 1], parts[:, h, 2]
        scores = jnp.where(same, product_right(q, k) * HEAD_DIM**-0.5, masked_value)
        highest = jnp.max(scores, axis=1, keepdims=True)
        powers = jnp.exp(scores - highest)
        totals = jnp.sum(powers, axis=1, keepdims=True)
        outs.append(product((powers / totals).astype(bf16), v).astype(bf16))
        logsums.append(highest + jnp.log(totals))
    return jnp.concatenate(outs, axis=1), logsums


def attend_back(triple, segments, logsums, grad, heads):
    rows = triple.shape[0]
    parts = triple.reshape(rows, heads, 3, HEAD_DIM)
    same = segments[:, None] == segments[None, :]
    outs = []
    for h in range(heads):
        q, k, v = parts[:, h, 0], parts[:, h, 1], parts[:, h, 2]
        g = grad[:, h * HEAD_DIM : (h + 1) * HEAD_DIM]
        scores = jnp.where(same, product_right(q, k) * HEAD_DIM**-0.5, masked_value)
        weights = jnp.exp(scores - logsums[h])
        grad_v = product_left(weights.astype(bf16), g)
        grad_weights = product_right(g, v)
        dots = jnp.sum(weights * grad_weights, axis=1, keepdims=True)
        grad_scores = (weights * (grad_weights - dots)).astype(bf16)
        grad_q = product(grad_scores, k) * HEAD_DIM**-0.5
        grad_k = product_left(grad_scores, q) * HEAD_DIM**-0.5
        outs.extend([grad_q, grad_k, grad_v])
    return jnp.concatenate(outs, axis=1).astype(bf16)


def body_any(
    tokens,
    segment_ids,
    first_gain,
    first_bias,
    input_weight,
    query_bias,
    value_bias,
    output_weight,
    output_bias,
    scale_one,
    second_gain,
    second_bias,
    up_weight,
    up_bias,
    down_weight,
    down_bias,
    scale_two,
    out_grad,
):
    members = lax.axis_size("seq")
    fsdp = lax.axis_size("fsdp")
    s = lax.axis_index("seq")
    rows, width = tokens.shape
    heads = HEADS // members
    own_cols = 3 * HEAD_DIM * heads
    part = width // members
    shard = input_weight.shape[0]
    ff_shard = down_weight.shape[0]
    ff_part = ff_shard // members

    local_vectors = (
        first_gain,
        first_bias,
        query_bias,
        value_bias,
        output_bias,
        scale_one,
        second_gain,
        second_bias,
        up_bias,
        down_bias,
        scale_two,
    )
    widths = [v.shape[0] for v in local_vectors]
    packed_width = sum(widths)

    own_in = lax.dynamic_slice_in_dim(input_weight, s * own_cols, own_cols, 1)
    own_out = lax.dynamic_slice_in_dim(output_weight, s * part, part, 1)
    own_up = lax.dynamic_slice_in_dim(
        up_weight.reshape(shard, fsdp, ff_shard), s * ff_part, ff_part, 2
    ).reshape(shard, fsdp * ff_part)
    own_down = lax.dynamic_slice_in_dim(down_weight, s * ff_part, ff_part, 0)

    vectors = gather_fsdp(jnp.concatenate(local_vectors)[None, :])[:, 0]
    w_in = gather_fsdp(own_in).reshape(width, own_cols)
    w_out_part = gather_fsdp(own_out).reshape(width, part)
    w_up = gather_fsdp(own_up).reshape(width, fsdp * ff_part)
    w_down = gather_fsdp(own_down).reshape(fsdp * ff_part, width)
    w_out = jnp.zeros((width, width), bf16)
    for k, block in enumerate(from_others(w_out_part)):
        w_out = lax.dynamic_update_slice_in_dim(w_out, block, (s ^ k) * part, 1)

    pieces = []
    offset = 0
    for size in widths:
        pieces.append(vectors[:, offset : offset + size].reshape(-1).astype(f32))
        offset += size
    (
        gain_one,
        offset_one,
        bias_query,
        bias_value,
        bias_output,
        factor_one,
        gain_two,
        offset_two,
        bias_up,
        bias_down,
        factor_two,
    ) = pieces
    own_bias_up = lax.dynamic_slice_in_dim(
        bias_up.reshape(fsdp, ff_shard), s * ff_part, ff_part, 1
    ).reshape(-1)
    own_query = lax.dynamic_slice_in_dim(bias_query, s * part, part, 0)
    own_value = lax.dynamic_slice_in_dim(bias_value, s * part, part, 0)

    inputs = jnp.concatenate(from_others(tokens), axis=0).astype(f32)
    out_grads = jnp.concatenate(from_others(out_grad), axis=0).astype(f32)
    segments = jnp.concatenate(
        [lax.dynamic_slice_in_dim(segment_ids, (s ^ k) * rows, rows, 0) for k in range(members)]
    )

    normed_one, spread_one = normalize(inputs)
    hidden_one = (normed_one * gain_one + offset_one).astype(bf16)
    bias_own = jnp.stack(
        [
            own_query.reshape(heads, HEAD_DIM),
            jnp.zeros((heads, HEAD_DIM), f32),
            own_value.reshape(heads, HEAD_DIM),
        ],
        axis=1,
    ).reshape(-1)
    triple = (product(hidden_one, w_in) + bias_own).astype(bf16)
    attended_own, logsums = attend(triple, segments, heads)

    attended = jnp.zeros((members * rows, width), bf16)
    for k, block in enumerate(from_others(attended_own)):
        block = block.reshape(members, rows, part)
        block = jnp.concatenate([block[j ^ k] for j in range(members)], axis=0)
        attended = lax.dynamic_update_slice_in_dim(attended, block, (s ^ k) * part, 1)

    branch_one = product(attended, w_out) + bias_output
    middle = inputs + factor_one * branch_one
    normed_two, spread_two = normalize(middle)
    hidden_two = (normed_two * gain_two + offset_two).astype(bf16)
    before = product(hidden_two, w_up) + own_bias_up
    activated_full, slope = gelu_pair(before)
    activated = activated_full.astype(bf16)

    grads = out_grads * (segments >= 0).astype(f32)[:, None]
    grad_two = (grads * factor_two).astype(bf16)
    grad_before = (product_right(grad_two, w_down) * slope).astype(bf16)
    partial_hidden_two = product_right(grad_before, w_up)
    grad_hidden_two = sum(
        block.astype(f32)
        for block in exchange(
            [partial_hidden_two[:rows]]
            + [partial_hidden_two[k * rows : (k + 1) * rows].astype(bf16) for k in range(1, members)]
        )
    )

    partial_two = product(activated, w_down)
    branch_two = bias_down + sum(
        block.astype(f32)
        for block in exchange(
            [partial_two[:rows]]
            + [partial_two[k * rows : (k + 1) * rows].astype(bf16) for k in range(1, members)]
        )
    )
    own_middle, own_grad = middle[:rows], grads[:rows]
    layer_out = (own_middle + factor_two * branch_two).astype(bf16)
    grad_factor_two = jnp.sum(own_grad * branch_two, axis=0)
    grad_bias_down = jnp.sum(grad_two[:rows].astype(f32), axis=0)
    grad_bias_up = jnp.sum(grad_before.astype(f32), axis=0)

    own_normed_two = normed_two[:rows]
    grad_gain_two = jnp.sum(grad_hidden_two * own_normed_two, axis=0)
    grad_offset_two = jnp.sum(grad_hidden_two, axis=0)
    grad_middle = own_grad + normalize_back(
        grad_hidden_two * gain_two, own_normed_two, spread_two[:rows]
    )
    grad_factor_one = jnp.sum(grad_middle * branch_one[:rows], axis=0)
    grad_one = (grad_middle * factor_one).astype(bf16)
    grad_bias_output = jnp.sum(grad_one.astype(f32), axis=0)
    grad_attended = product_right(grad_one, w_out).astype(bf16)

    def columns(x, k):
        return lax.dynamic_slice_in_dim(x, (s ^ k) * part, part, 1)

    grad_heads = jnp.concatenate(
        exchange([columns(grad_attended, k) for k in range(members)]), axis=0
    )
    grad_one_cols = jnp.concatenate(exchange([columns(grad_one, k) for k in range(members)]), axis=0)
    grad_triple = attend_back(triple, segments, logsums, grad_heads, heads)
    partial_hidden_one = product_right(grad_triple, w_in)
    grad_hidden_one = sum(
        block.astype(f32)
        for block in exchange(
            [partial_hidden_one[:rows]]
            + [partial_hidden_one[k * rows : (k + 1) * rows].astype(bf16) for k in range(1, members)]
        )
    )
    own_normed_one = normed_one[:rows]
    grad_gain_one = jnp.sum(grad_hidden_one * own_normed_one, axis=0)
    grad_offset_one = jnp.sum(grad_hidden_one, axis=0)
    tokens_grad = (
        grad_middle
        + normalize_back(grad_hidden_one * gain_one, own_normed_one, spread_one[:rows])
    ).astype(bf16)

    def own_share(left, right, lead):
        full = product_left(left, right).astype(bf16)
        return scatter_fsdp(full.reshape(fsdp, lead, full.shape[1])).astype(bf16)

    share_down = own_share(activated, grad_two, ff_part)
    share_up = own_share(hidden_two, grad_before, shard)
    share_out = own_share(attended, grad_one_cols, shard)
    share_in = own_share(hidden_one, grad_triple, shard)

    grad_down = jnp.zeros(down_weight.shape, f32)
    for k, block in enumerate(from_others(share_down)):
        grad_down = lax.dynamic_update_slice_in_dim(
            grad_down, block.astype(f32), (s ^ k) * ff_part, 0
        )
    grad_up = jnp.zeros((shard, fsdp, ff_shard), f32)
    for k, block in enumerate(from_others(share_up)):
        grad_up = lax.dynamic_update_slice_in_dim(
            grad_up, block.astype(f32).reshape(shard, fsdp, ff_part), (s ^ k) * ff_part, 2
        )
    grad_up = grad_up.reshape(up_weight.shape)
    grad_out = jnp.zeros(output_weight.shape, f32)
    for k, block in enumerate(from_others(share_out)):
        grad_out = lax.dynamic_update_slice_in_dim(
            grad_out, block.astype(f32), (s ^ k) * part, 1
        )
    grad_in = jnp.zeros(input_weight.shape, f32)
    for k, block in enumerate(from_others(share_in)):
        grad_in = lax.dynamic_update_slice_in_dim(
            grad_in, block.astype(f32), (s ^ k) * own_cols, 1
        )

    triple_sums = jnp.sum(grad_triple.astype(f32), axis=0).reshape(heads, 3, HEAD_DIM)

    def placed(x, total):
        return lax.dynamic_update_slice_in_dim(
            jnp.zeros((total,), f32), x.reshape(-1), s * x.size, 0
        )

    grad_bias_up_full = lax.dynamic_update_slice_in_dim(
        jnp.zeros((fsdp, ff_shard), f32), grad_bias_up.reshape(fsdp, ff_part), s * ff_part, 1
    )
    vector_grads = (
        grad_gain_one,
        grad_offset_one,
        placed(triple_sums[:, 0], width),
        placed(triple_sums[:, 2], width),
        grad_bias_output,
        grad_factor_one,
        grad_gain_two,
        grad_offset_two,
        grad_bias_up_full,
        grad_bias_down,
        grad_factor_two,
    )
    packed = jnp.concatenate([v.reshape(fsdp, -1) for v in vector_grads], axis=1)
    packed = lax.psum(packed, "seq")
    vector_total = scatter_fsdp(packed.astype(bf16)[:, None, :])[0]
    outs = []
    offset = 0
    for size in widths:
        outs.append(vector_total[offset : offset + size])
        offset += size
    return (
        layer_out,
        tokens_grad,
        outs[0],
        outs[1],
        grad_in,
        outs[2],
        outs[3],
        grad_out,
        outs[4],
        outs[5],
        outs[6],
        outs[7],
        grad_up,
        outs[8],
        grad_down,
        outs[9],
        outs[10],
    )


def spec(kind=pltpu.VMEM):
    return pl.BlockSpec(memory_space=kind)


def shape(dims, kind):
    return jax.ShapeDtypeStruct(dims, kind)


def call(kernel, where, ins, outs, flops=0, name=None, scratch=(), in_hbm=False, limit=50):
    in_specs = [spec(pltpu.HBM) if in_hbm else spec() for _ in ins]
    return pl.pallas_call(
        kernel,
        out_shape=outs,
        in_specs=[spec(pltpu.SMEM)] + in_specs,
        out_specs=[spec() for _ in outs],
        scratch_shapes=list(scratch),
        compiler_params=pltpu.CompilerParams(vmem_limit_bytes=limit * 1024 * 1024),
        cost_estimate=pl.CostEstimate(flops=0, bytes_accessed=0, transcendentals=0),
        name=name,
    )(where, *ins)


def at(index, size):
    return pl.ds(pl.multiple_of(index * size, size), size)


def run_copies(pairs, sems):
    copies = [pltpu.make_async_copy(a, b, sems.at[i]) for i, (a, b) in enumerate(pairs)]
    for copy in copies:
        copy.start()
    return copies


def prepare_first(where, *refs):
    w_in, w_out, tokens, grad, vectors = refs[0], refs[1], refs[2], refs[3], refs[4:15]
    first, rows, held, (pack, sems) = refs[15], refs[16], refs[17:28], refs[28:]
    s = where[1]
    pairs = list(zip(vectors, held)) + [
        (pair[0], pair[1])
        for m in range(4)
        for pair in (
            (w_in.at[:, at(s, 768)], first.at[m, 0:128, 0:768]),
            (w_out.at[:, at(s, 256)], first.at[m, 0:128, 768:1024]),
        )
    ]
    pairs += [(tokens, rows.at[0:128]), (grad, rows.at[128:256])]
    copies = run_copies(pairs, sems)
    for copy in copies[:11]:
        copy.wait()
    pack[...] = jnp.zeros(pack.shape, f32)
    for i in range(10):
        pack[i : i + 1, 0:128] = held[i][...].astype(f32).reshape(1, 128)
    for i in range(4):
        pack[10 + i : 11 + i, 0:128] = (
            held[10][i * 128 : (i + 1) * 128].astype(f32).reshape(1, 128)
        )
    for m in range(4):
        first[m, 128:144] = pack[...].astype(bf16)
    for copy in copies[11:]:
        copy.wait()


def prepare_second(where, w_up, w_down, second, sems):
    s = where[1]
    pairs = [(w_down.at[at(s, 128)], second.at[128:256])]
    for i in range(8):
        lanes = pl.ds(pl.multiple_of(i * 512 + s * 128, 128), 128)
        pairs.append((w_up.at[:, lanes], second.at[0:128, i * 128 : (i + 1) * 128]))
    for copy in run_copies(pairs, sems):
        copy.wait()


def owner(where, t, b):
    return 2 * where[2 + t] + ((where[0] % 2) ^ b)


def place_first(where, own, other, w_in, w_out, vecs):
    for b, blocks in enumerate((own, other)):
        for z in range(4):
            n = 2 * z + ((where[0] % 2) ^ b)
            w_in[at(n, 128)] = blocks[z, 0:128, 0:768]
            w_out[at(n, 128)] = blocks[z, 0:128, 768:1024]
            vecs[:, at(n, 128)] = blocks[z, 128:144, 0:128].astype(f32)


def column_segments(where, seg):
    return jnp.concatenate([seg[at(where[1] ^ k, 128)] for k in range(4)], axis=0)


def row_segments(where, seg):
    return jnp.concatenate([seg[:, at(where[1] ^ k, 128)] for k in range(4)], axis=1)


def attention(where, t0, t1, t2, t3, w_in, vecs, seg_col, seg_row, triple, attended, logsum, hidden):
    gain, offset = vecs[0:1], vecs[1:2]
    for k, ref in enumerate((t0, t1, t2, t3)):
        normed, _ = normalize(ref[0:128].astype(f32))
        hidden[k * 128 : (k + 1) * 128] = (normed * gain + offset).astype(bf16)
    own = at(where[1], 256)
    query, value = vecs[2:3, own], vecs[3:4, own]
    zero = jnp.zeros((1, 64), f32)
    pieces = []
    for h in range(4):
        pieces += [query[:, h * 64 : (h + 1) * 64], zero, value[:, h * 64 : (h + 1) * 64]]
    triple[...] = (product(hidden[...], w_in[...]) + jnp.concatenate(pieces, axis=1)).astype(bf16)
    same = column_segments(where, seg_col) == row_segments(where, seg_row)
    outs = []
    for h in range(4):
        q, k, v = (triple[:, h * 192 + c * 64 : h * 192 + (c + 1) * 64] for c in range(3))
        scores = jnp.where(same, product_right(q, k) * HEAD_DIM**-0.5, masked_value)
        highest = jnp.max(scores, axis=1, keepdims=True)
        powers = jnp.exp(scores - highest)
        totals = jnp.sum(powers, axis=1, keepdims=True)
        probs = (powers * (1.0 / totals)).astype(bf16)
        outs.append(product(probs, v).astype(bf16))
        logsum[:, h : h + 1] = highest + jnp.log(totals)
    whole = jnp.concatenate(outs, axis=1)
    for m in range(4):
        attended[m] = whole


def project(
    where, sent, w0, w1, w2, w3, t0, t1, t2, t3, vecs, full, hidden, own_middle, own_branch, branch
):
    for m in range(4):
        for j in range(4):
            rows = at(where[1] ^ (j ^ m), 128)
            full[j * 128 : (j + 1) * 128, m * 256 : (m + 1) * 256] = sent[m, rows]
    for k, ref in enumerate((w0, w1, w2, w3)):
        branch[:, at(where[1] ^ k, 256)] = product(full[...], ref[...])
    for r, ref in enumerate((t0, t1, t2, t3)):
        rows = slice(r * 128, (r + 1) * 128)
        piece = branch[rows] + vecs[4:5]
        middle = ref[0:128].astype(f32) + vecs[5:6] * piece
        normed, _ = normalize(middle)
        hidden[rows] = (normed * vecs[6:7] + vecs[7:8]).astype(bf16)
        if r == 0:
            own_middle[...] = middle
            own_branch[...] = piece


def feed(where, *refs):
    hidden, blocks, tokens, (vecs, seg_col) = refs[0], refs[1:9], refs[9:13], refs[13:15]
    w_down, act, grad_two, grad_before, sums, p0, p1, p2, p3, w_up = refs[15:]
    for j in range(8):
        rows = at(owner(where, j // 2, j % 2), 128)
        w_up[rows] = blocks[j][0:128]
        w_down[rows] = blocks[j][128:256]
    valid = (column_segments(where, seg_col) >= 0).astype(f32)
    for k in range(4):
        rows = slice(k * 128, (k + 1) * 128)
        grad = tokens[k][128:256].astype(f32) * valid[rows]
        grad_two[rows] = (grad * vecs[9:10]).astype(bf16)
    bias = vecs[pl.ds(10 + where[1], 1)]
    for c in range(4):
        cols = slice(c * 256, (c + 1) * 256)
        before = product(hidden[...], w_up[:, cols]) + bias[:, cols]
        value, slope = gelu_pair(before)
        act[:, cols] = value.astype(bf16)
        back = (product_right(grad_two[...], w_down[cols]) * slope).astype(bf16)
        grad_before[:, cols] = back
        sums[:, cols] = jnp.sum(back.astype(f32), axis=0, keepdims=True)
    p0[...] = product_right(grad_before[0:128], w_up[...])
    for k, ref in ((1, p1), (2, p2), (3, p3)):
        ref[...] = product_right(grad_before[k * 128 : (k + 1) * 128], w_up[...]).astype(bf16)


def core_rows(where, z, own):
    return at(2 * z + ((where[0] % 2) if own else 1 - (where[0] % 2)), 128)


def feed_weights(where, *refs):
    hidden, grad_before, act, grad_two, w_down = refs[:5]
    tokens, (vecs, seg_col, mine, theirs, sums, *two) = refs[5:9], refs[9:]
    for k in range(4):
        for ref, own in ((mine, True), (theirs, False)):
            cols = core_rows(where, where[2 + k], own)
            ref[k, 0:128] = product_left(hidden[:, cols], grad_before[...]).astype(bf16)
            ref[k, 128:256] = product_left(act[:, cols], grad_two[...]).astype(bf16)
    valid = (column_segments(where, seg_col) >= 0).astype(f32)
    scale = jnp.zeros((1, 1024), f32)
    for k in range(4):
        rows = slice(k * 128, (k + 1) * 128)
        part = product(act[rows], w_down[...])
        grad = tokens[k][128:256].astype(f32) * valid[rows]
        two[k][...] = part.astype(bf16)
        if k == 0:
            part = part + vecs[8:9]
        scale = scale + jnp.sum(grad * part, axis=0, keepdims=True)
    sums[0:1] = jnp.sum(grad_two[0:128].astype(f32), axis=0, keepdims=True)
    sums[1:2] = scale


def middle_back(
    where, p0, p1, p2, p3, own_middle, own_branch, tokens, seg_col, vecs, w0, w1, w2, w3,
    grad_middle, sums, m0, m1, m2, m3, attended, one,
):
    total = p0[...] + p1[...].astype(f32) + p2[...].astype(f32) + p3[...].astype(f32)
    normed, spread = normalize(own_middle[...])
    valid = (seg_col[at(where[1], 128)] >= 0).astype(f32)
    back = tokens[128:256].astype(f32) * valid + normalize_back(total * vecs[6:7], normed, spread)
    grad_middle[...] = back
    grad_one = (back * vecs[5:6]).astype(bf16)
    one[...] = grad_one
    sums[0:1] = jnp.sum(total * normed, axis=0, keepdims=True)
    sums[1:2] = jnp.sum(total, axis=0, keepdims=True)
    sums[2:3] = jnp.sum(back * own_branch[...], axis=0, keepdims=True)
    sums[3:4] = jnp.sum(grad_one.astype(f32), axis=0, keepdims=True)
    result = jnp.zeros((128, 1024), f32)
    for k, ref in enumerate((w0, w1, w2, w3)):
        result = result + product_right(one[:, at(where[1] ^ k, 256)], ref[...])
    attended[...] = result.astype(bf16)
    for k, ref in enumerate((m0, m1, m2, m3)):
        cols = at(where[1] ^ k, 256)
        ref[0:128] = attended[:, cols]
        ref[128:256] = one[:, cols]


def attention_back(
    where, triple, logsum, m0, m1, m2, m3, seg_col, seg_row, w_in, t0, t1, t2, t3,
    grad_triple, sums, *last,
):
    same = column_segments(where, seg_col) == row_segments(where, seg_row)
    grads = jnp.concatenate([m[0:128] for m in (m0, m1, m2, m3)], axis=0)
    pieces = []
    for h in range(4):
        q, k, v = (triple[:, h * 192 + c * 64 : h * 192 + (c + 1) * 64] for c in range(3))
        g = grads[:, h * 64 : (h + 1) * 64]
        scores = jnp.where(same, product_right(q, k) * HEAD_DIM**-0.5, masked_value)
        weights = jnp.exp(scores - logsum[:, h : h + 1])
        grad_v = product_left(weights.astype(bf16), g)
        grad_weights = product_right(g, v)
        dots = jnp.sum(weights * grad_weights, axis=1, keepdims=True)
        grad_scores = (weights * (grad_weights - dots)).astype(bf16)
        grad_q = product(grad_scores, k) * HEAD_DIM**-0.5
        grad_k = product_left(grad_scores, q) * HEAD_DIM**-0.5
        pieces += [grad_q.astype(bf16), grad_k.astype(bf16), grad_v.astype(bf16)]
    whole = jnp.concatenate(pieces, axis=1)
    grad_triple[...] = whole
    columns = jnp.sum(whole.astype(f32), axis=0, keepdims=True)
    sums[...] = jnp.zeros(sums.shape, f32)
    lanes = at(where[1], 256)
    for row, c in ((2, 0), (3, 2)):
        sums[row : row + 1, lanes] = jnp.concatenate(
            [columns[:, h * 192 + c * 64 : h * 192 + (c + 1) * 64] for h in range(4)], axis=1
        )
    gain = jnp.zeros((1, 1024), f32)
    offset = jnp.zeros((1, 1024), f32)
    for k, ref in enumerate((t0, t1, t2, t3)):
        part = product_right(grad_triple[k * 128 : (k + 1) * 128], w_in[...])
        normed, _ = normalize(ref[0:128].astype(f32))
        gain = gain + jnp.sum(part * normed, axis=0, keepdims=True)
        offset = offset + jnp.sum(part, axis=0, keepdims=True)
        last[k][...] = part.astype(bf16)
    sums[0:1] = gain
    sums[1:2] = offset


def attention_weights(
    where, hidden, grad_triple, attended, m0, m1, m2, m3, up_sums, two_sums, mid_sums, one_sums,
    mine, theirs, vecs,
):
    ones = jnp.concatenate([m[128:256] for m in (m0, m1, m2, m3)], axis=0)
    vecs[...] = jnp.zeros(vecs.shape, f32)
    vecs[0:4] = one_sums[...]
    vecs[4:5] = mid_sums[3:4]
    vecs[5:6] = mid_sums[2:3]
    vecs[6:8] = mid_sums[0:2]
    vecs[8:10] = two_sums[0:2]
    vecs[pl.ds(10 + where[1], 1)] = up_sums[...]
    blank = jnp.zeros((16, 896), bf16)
    for k in range(4):
        for ref, own in ((mine, True), (theirs, False)):
            cols = core_rows(where, where[2 + k], own)
            ref[k, 0:128, 0:768] = product_left(hidden[:, cols], grad_triple[...]).astype(bf16)
            ref[k, 0:128, 768:1024] = product_left(attended[:, cols], ones).astype(bf16)
            ref[k, 128:144] = jnp.concatenate([vecs[:, cols].astype(bf16), blank], axis=1)


def finish_rows(where, *refs):
    ones, twos, (own_middle, grad_middle, tokens, vecs, out, grad) = refs[:4], refs[4:8], refs[8:]
    total = sum(ref[...].astype(f32) for ref in ones)
    two = sum(ref[...].astype(f32) for ref in twos) + vecs[8:9]
    out[...] = (own_middle[...] + vecs[9:10] * two).astype(bf16)
    normed, spread = normalize(tokens[0:128].astype(f32))
    grad[...] = (grad_middle[...] + normalize_back(total * vecs[0:1], normed, spread)).astype(bf16)


def finish_feed(where, got, up, down):
    for m in range(4):
        down[m * 128 : (m + 1) * 128] = got[m, 128:256].astype(f32)
        for n in range(8):
            lanes = slice(n * 512 + m * 128, n * 512 + (m + 1) * 128)
            up[:, lanes] = got[m, 0:128, n * 128 : (n + 1) * 128].astype(f32)


def finish_attention(where, s0, s1, s2, s3, w_in, w_out, *refs):
    outs, held = refs[:-1], refs[-1]
    for k, ref in enumerate((s0, s1, s2, s3)):
        m = where[1] ^ k
        w_in[:, at(m, 768)] = ref[0:128, 0:768].astype(f32)
        w_out[:, at(m, 256)] = ref[0:128, 768:1024].astype(f32)
        held[m] = ref[128:144, 0:128].astype(f32)
    total = held[0] + held[1] + held[2] + held[3]
    for i in range(10):
        outs[i][...] = total[i : i + 1]
    outs[10][...] = jnp.concatenate([total[i : i + 1] for i in range(10, 14)], axis=1)


def ring(count):
    return list(range(0, count, 2)) + list(range(count - 1, 0, -2))


def step(x, hops=1):
    order = ring(lax.axis_size("fsdp") // 2)
    count = len(order)
    pairs = [(order[i], order[(i + hops) % count]) for i in range(count)]
    return lax.ppermute(x, "fsdp", [(2 * a + c, 2 * b + c) for a, b in pairs for c in (0, 1)])


def along(x):
    count = lax.axis_size("fsdp") // 2
    groups = [[2 * z + c for z in range(count)] for c in (0, 1)]
    return lax.all_to_all(
        x, "fsdp", split_axis=0, concat_axis=0, axis_index_groups=groups, tiled=True
    )


def after(x, *earlier):
    return lax.optimization_barrier((x,) + earlier)[0]


def both_cores(blocks):
    return [b for block in blocks for b in (block, swap(block, "fsdp", 1))]


def pair_sums(mine, theirs):
    return [add(mine[t], theirs[t]) for t in range(4)]


def deal(x):
    return lax.all_to_all(x, "seq", split_axis=0, concat_axis=0, tiled=True)


def share(where, received, own, out):
    total = (received[...].astype(f32) + own[...].astype(f32)).astype(bf16)
    for m in range(4):
        out[m] = total


def deal_sum(where, x, y, name):
    (copies,) = call(share, where, [x, y], [shape((4,) + x.shape, bf16)], name=name)
    return deal(copies)


def add(x, y):
    return (x.astype(f32) + y.astype(f32)).astype(bf16)


def body(*args):
    tokens, input_weight, up_weight = args[0], args[4], args[12]
    fits = (
        lax.axis_size("seq") == 4
        and lax.axis_size("fsdp") == 8
        and tokens.shape == (128, 1024)
        and input_weight.shape == (128, 3072)
        and up_weight.shape == (128, 4096)
    )
    return body_fast(*args) if fits else body_any(*args)


def body_fast(
    tokens,
    segment_ids,
    first_gain,
    first_bias,
    input_weight,
    query_bias,
    value_bias,
    output_weight,
    output_bias,
    scale_one,
    second_gain,
    second_bias,
    up_weight,
    up_bias,
    down_weight,
    down_bias,
    scale_two,
    out_grad,
):
    f, s = lax.axis_index("fsdp"), lax.axis_index("seq")
    z = f // 2
    odd = (z ^ (z // 2)) % 2
    where = jnp.stack([f, s, z, z ^ (1 + odd), z ^ 3, z ^ (2 - odd)]).astype(jnp.int32)
    vectors = [
        first_gain, first_bias, query_bias, value_bias, output_bias,
        scale_one, second_gain, second_bias, down_bias, scale_two, up_bias,
    ]
    seg_col, seg_row = segment_ids.reshape(512, 1), segment_ids.reshape(1, 512)
    mat = shape((512, 1024), bf16)
    rows_f, rows_b = shape((128, 1024), f32), shape((128, 1024), bf16)

    first, rows = call(
        prepare_first,
        where,
        [input_weight, output_weight, tokens, out_grad] + vectors,
        [shape((4, 144, 1024), bf16), shape((256, 1024), bf16)],
        name="prepare_first",
        scratch=[pltpu.VMEM(v.shape, bf16) for v in vectors] + [pltpu.VMEM((16, 1024), f32), pltpu.SemaphoreType.DMA((32,))],
        in_hbm=True,
        limit=63,
    )
    shared = from_others(rows)
    first_own = along(first)
    (second,) = call(
        prepare_second,
        where,
        [up_weight, down_weight],
        [shape((256, 1024), bf16)],
        name="prepare_second",
        scratch=[pltpu.SemaphoreType.DMA((36,))],
        in_hbm=True,
        limit=63,
    )
    second_1 = step(after(second, first_own, *shared[1:]))
    w_in, w_out_own, vecs = call(
        place_first,
        where,
        [first_own, swap(after(first_own, second, *shared[1:]), "fsdp", 1)],
        [shape((1024, 768), bf16), shape((1024, 256), bf16), shape((16, 1024), f32)],
        name="place_first",
        limit=63,
    )
    w_out = from_others(w_out_own)
    triple, attended_own, logsum, hidden_one = call(
        attention,
        where,
        shared + [w_in, vecs, seg_col, seg_row],
        [shape((512, 768), bf16), shape((4, 512, 256), bf16), shape((512, 128), f32), mat],
        name="attention",
    )
    second_2 = step(after(second_1, attended_own))
    second_3 = step(after(second_2, *w_out[1:]))
    shares = deal(attended_own)
    attended, hidden_two, own_middle, own_branch = call(
        project,
        where,
        [shares] + w_out + shared + [vecs],
        [mat, mat, rows_f, rows_f],
        name="project",
        scratch=[pltpu.VMEM((512, 1024), f32)],
    )
    w_down, act, grad_two, grad_before, up_sums, *partial = call(
        feed,
        where,
        [hidden_two]
        + both_cores([after(x, shares) for x in (second, second_1, second_2)] + [after(second_3, hidden_two)])
        + shared + [vecs, seg_col],
        [shape((1024, 1024), bf16), mat, mat, mat, shape((1, 1024), f32), rows_f, rows_b, rows_b, rows_b],
        name="feed",
        scratch=[pltpu.VMEM((1024, 1024), bf16)],
    )
    partial = exchange(partial)
    second_mine, second_theirs, two_sums, *two = call(
        feed_weights,
        where,
        [hidden_two, grad_before, act, grad_two, w_down] + shared + [vecs, seg_col],
        [shape((4, 256, 1024), bf16)] * 2 + [shape((2, 1024), f32)] + [rows_b] * 4,
        name="feed_weights",
    )
    second_theirs = swap(after(second_theirs, two[0], *partial[1:]), "fsdp", 1)
    grad_middle, mid_sums, *messages = call(
        middle_back,
        where,
        partial + [own_middle, own_branch, rows, seg_col, vecs] + w_out,
        [rows_f, shape((4, 1024), f32)] + [shape((256, 256), bf16)] * 4,
        name="middle_back",
        scratch=[pltpu.VMEM((128, 1024), bf16), pltpu.VMEM((128, 1024), bf16)],
    )
    got = exchange(messages)
    second_sums = pair_sums(after(second_mine, messages[1]), second_theirs)
    second_added = add(step(second_sums[1]), after(second_sums[2], *got[1:]))
    got = [after(got[0], second_added)] + got[1:]
    second_total = step(second_added)
    twos = exchange([two[0]] + [after(x, *got[1:]) for x in two[1:]])
    grad_triple, one_sums, *last = call(
        attention_back,
        where,
        [triple, logsum] + got + [seg_col, seg_row, w_in] + shared,
        [shape((512, 768), bf16), shape((4, 1024), f32)] + [rows_b] * 4,
        flops=20 * 512 * 1024 * 1024,
        name="attention_back",
    )
    first_mine, first_theirs = call(
        attention_weights,
        where,
        [hidden_one, grad_triple, attended] + got + [up_sums, two_sums, mid_sums, one_sums],
        [shape((4, 144, 1024), bf16)] * 2,
        flops=20 * 512 * 1024 * 1024,
        name="attention_weights",
        scratch=[pltpu.VMEM((16, 1024), f32)],
    )
    ones = exchange([last[0]] + [after(x, *twos[1:]) for x in last[1:]])
    first_sums = pair_sums(first_mine, swap(after(first_theirs, second_total, *twos[1:]), "fsdp", 1))
    second_total = step(add(second_total, second_sums[3]))
    first_added = after(add(step(first_sums[1]), first_sums[2]), second_total, *ones[1:])
    layer_out, tokens_grad = call(
        finish_rows,
        where,
        ones + twos + [own_middle, grad_middle, rows, vecs],
        [rows_b, rows_b],
        name="finish_rows",
        limit=63,
    )
    grad_up, grad_down = call(
        finish_feed,
        where,
        [deal_sum(where, second_total, second_sums[0], "share_feed")],
        [shape((128, 4096), f32), shape((512, 1024), f32)],
        name="finish_feed",
    )
    first_total = step(first_added)
    first_total = step(after(add(first_total, first_sums[3]), layer_out))
    first_share = from_others(add(first_total, first_sums[0]))
    grad_in, grad_out, *small = call(
        finish_attention,
        where,
        [after(first_share[0], grad_up)] + first_share[1:],
        [shape((128, 3072), f32), rows_f] + [shape((1, 128), f32)] * 10 + [shape((1, 512), f32)],
        name="finish_attention",
        scratch=[pltpu.VMEM((4, 16, 128), f32)],
    )
    g = [v.reshape(-1) for v in small]
    return (
        layer_out, tokens_grad, g[0], g[1], grad_in, g[2], g[3], grad_out, g[4],
        g[5], g[6], g[7], grad_up, g[10], grad_down, g[8], g[9],
    )


def solution(mesh):
    rows, vec, mat = P(("fsdp", "seq"), None), P("fsdp"), P("fsdp", None)
    return jax.shard_map(
        body,
        mesh=mesh,
        in_specs=(
            rows, vec, vec, vec, mat, vec, vec, mat, vec,
            vec, vec, vec, mat, vec, mat, vec, vec, rows,
        ),
        out_specs=(
            rows, rows, vec, vec, mat, vec, vec, mat, vec,
            vec, vec, vec, mat, vec, mat, vec, vec,
        ),
        check_vma=False,
    )
```

```python
import math

import jax
import jax.numpy as jnp
from jax import lax
from jax.experimental import pallas as pl
from jax.experimental.pallas import tpu as pltpu
from jax.sharding import PartitionSpec as P

HEADS = 16
HEAD_DIM = 64
epsilon = 1e-06
masked_value = -1000000000.0
bf16 = jnp.bfloat16
f32 = jnp.float32


def product(left, right):
    return jnp.dot(left, right, preferred_element_type=f32)


def product_left(left, right):
    return lax.dot_general(left, right, (((0,), (0,)), ((), ())), preferred_element_type=f32)


def product_right(left, right):
    return lax.dot_general(left, right, (((1,), (1,)), ((), ())), preferred_element_type=f32)


def normalize(values):
    center = values - jnp.mean(values, axis=1, keepdims=True)
    spread = lax.rsqrt(jnp.mean(center * center, axis=1, keepdims=True) + epsilon)
    return (center * spread, spread)


def normalize_back(grad_normed, normed, spread):
    return spread * (
        grad_normed
        - jnp.mean(grad_normed, axis=1, keepdims=True)
        - normed * jnp.mean(grad_normed * normed, axis=1, keepdims=True)
    )


def gelu_pair(before):
    normal_cdf = 0.5 * (1.0 + lax.erf(before * (1.0 / math.sqrt(2.0))))
    density = jnp.exp(-0.5 * before * before) * (1.0 / math.sqrt(2.0 * math.pi))
    return (before * normal_cdf, normal_cdf + before * density)


def swap(x, axis, k):
    count = lax.axis_size(axis)
    return lax.ppermute(x, axis, [(i, i ^ k) for i in range(count)])


def from_others(x):
    return [x] + [swap(x, "seq", k) for k in range(1, lax.axis_size("seq"))]


def exchange(blocks):
    return [blocks[0]] + [swap(blocks[k], "seq", k) for k in range(1, len(blocks))]


def gather_fsdp(x):
    count = lax.axis_size("fsdp")
    f = lax.axis_index("fsdp")
    same = [x] + [swap(x, "fsdp", 2 * k) for k in range(1, count // 2)]
    other = swap(jnp.stack(same), "fsdp", 1)
    out = jnp.zeros((count,) + x.shape, x.dtype)
    for k in range(count // 2):
        out = lax.dynamic_update_index_in_dim(out, same[k], f ^ (2 * k), 0)
        out = lax.dynamic_update_index_in_dim(out, other[k], f ^ (2 * k + 1), 0)
    return out


def scatter_fsdp(g):
    count = g.shape[0]
    f = lax.axis_index("fsdp")
    z, core = f // 2, f % 2
    pairs = g.reshape((count // 2, 2) + g.shape[1:])
    mine = lax.dynamic_index_in_dim(pairs, core, 1, keepdims=False)
    theirs = lax.dynamic_index_in_dim(pairs, 1 - core, 1, keepdims=False)
    sums = (mine.astype(f32) + swap(theirs, "fsdp", 1).astype(f32)).astype(bf16)
    total = lax.dynamic_index_in_dim(sums, z, 0, keepdims=False).astype(f32)
    for k in range(1, count // 2):
        block = lax.dynamic_index_in_dim(sums, z ^ k, 0, keepdims=False)
        total = total + swap(block, "fsdp", 2 * k).astype(f32)
    return total


def attend(triple, segments, heads):
    rows = triple.shape[0]
    parts = triple.reshape(rows, heads, 3, HEAD_DIM)
    outs = []
    logsums = []
    same = segments[:, None] == segments[None, :]
    for h in range(heads):
        q, k, v = parts[:, h, 0], parts[:, h, 1], parts[:, h, 2]
        scores = jnp.where(same, product_right(q, k) * HEAD_DIM**-0.5, masked_value)
        highest = jnp.max(scores, axis=1, keepdims=True)
        powers = jnp.exp(scores - highest)
        totals = jnp.sum(powers, axis=1, keepdims=True)
        outs.append(product((powers / totals).astype(bf16), v).astype(bf16))
        logsums.append(highest + jnp.log(totals))
    return jnp.concatenate(outs, axis=1), logsums


def attend_back(triple, segments, logsums, grad, heads):
    rows = triple.shape[0]
    parts = triple.reshape(rows, heads, 3, HEAD_DIM)
    same = segments[:, None] == segments[None, :]
    outs = []
    for h in range(heads):
        q, k, v = parts[:, h, 0], parts[:, h, 1], parts[:, h, 2]
        g = grad[:, h * HEAD_DIM : (h + 1) * HEAD_DIM]
        scores = jnp.where(same, product_right(q, k) * HEAD_DIM**-0.5, masked_value)
        weights = jnp.exp(scores - logsums[h])
        grad_v = product_left(weights.astype(bf16), g)
        grad_weights = product_right(g, v)
        dots = jnp.sum(weights * grad_weights, axis=1, keepdims=True)
        grad_scores = (weights * (grad_weights - dots)).astype(bf16)
        grad_q = product(grad_scores, k) * HEAD_DIM**-0.5
        grad_k = product_left(grad_scores, q) * HEAD_DIM**-0.5
        outs.extend([grad_q, grad_k, grad_v])
    return jnp.concatenate(outs, axis=1).astype(bf16)


def body_any(
    tokens,
    segment_ids,
    first_gain,
    first_bias,
    input_weight,
    query_bias,
    value_bias,
    output_weight,
    output_bias,
    scale_one,
    second_gain,
    second_bias,
    up_weight,
    up_bias,
    down_weight,
    down_bias,
    scale_two,
    out_grad,
):
    members = lax.axis_size("seq")
    fsdp = lax.axis_size("fsdp")
    s = lax.axis_index("seq")
    rows, width = tokens.shape
    heads = HEADS // members
    own_cols = 3 * HEAD_DIM * heads
    part = width // members
    shard = input_weight.shape[0]
    ff_shard = down_weight.shape[0]
    ff_part = ff_shard // members

    local_vectors = (
        first_gain,
        first_bias,
        query_bias,
        value_bias,
        output_bias,
        scale_one,
        second_gain,
        second_bias,
        up_bias,
        down_bias,
        scale_two,
    )
    widths = [v.shape[0] for v in local_vectors]
    packed_width = sum(widths)

    own_in = lax.dynamic_slice_in_dim(input_weight, s * own_cols, own_cols, 1)
    own_out = lax.dynamic_slice_in_dim(output_weight, s * part, part, 1)
    own_up = lax.dynamic_slice_in_dim(
        up_weight.reshape(shard, fsdp, ff_shard), s * ff_part, ff_part, 2
    ).reshape(shard, fsdp * ff_part)
    own_down = lax.dynamic_slice_in_dim(down_weight, s * ff_part, ff_part, 0)

    vectors = gather_fsdp(jnp.concatenate(local_vectors)[None, :])[:, 0]
    w_in = gather_fsdp(own_in).reshape(width, own_cols)
    w_out_part = gather_fsdp(own_out).reshape(width, part)
    w_up = gather_fsdp(own_up).reshape(width, fsdp * ff_part)
    w_down = gather_fsdp(own_down).reshape(fsdp * ff_part, width)
    w_out = jnp.zeros((width, width), bf16)
    for k, block in enumerate(from_others(w_out_part)):
        w_out = lax.dynamic_update_slice_in_dim(w_out, block, (s ^ k) * part, 1)

    pieces = []
    offset = 0
    for size in widths:
        pieces.append(vectors[:, offset : offset + size].reshape(-1).astype(f32))
        offset += size
    (
        gain_one,
        offset_one,
        bias_query,
        bias_value,
        bias_output,
        factor_one,
        gain_two,
        offset_two,
        bias_up,
        bias_down,
        factor_two,
    ) = pieces
    own_bias_up = lax.dynamic_slice_in_dim(
        bias_up.reshape(fsdp, ff_shard), s * ff_part, ff_part, 1
    ).reshape(-1)
    own_query = lax.dynamic_slice_in_dim(bias_query, s * part, part, 0)
    own_value = lax.dynamic_slice_in_dim(bias_value, s * part, part, 0)

    inputs = jnp.concatenate(from_others(tokens), axis=0).astype(f32)
    out_grads = jnp.concatenate(from_others(out_grad), axis=0).astype(f32)
    segments = jnp.concatenate(
        [lax.dynamic_slice_in_dim(segment_ids, (s ^ k) * rows, rows, 0) for k in range(members)]
    )

    normed_one, spread_one = normalize(inputs)
    hidden_one = (normed_one * gain_one + offset_one).astype(bf16)
    bias_own = jnp.stack(
        [
            own_query.reshape(heads, HEAD_DIM),
            jnp.zeros((heads, HEAD_DIM), f32),
            own_value.reshape(heads, HEAD_DIM),
        ],
        axis=1,
    ).reshape(-1)
    triple = (product(hidden_one, w_in) + bias_own).astype(bf16)
    attended_own, logsums = attend(triple, segments, heads)

    attended = jnp.zeros((members * rows, width), bf16)
    for k, block in enumerate(from_others(attended_own)):
        block = block.reshape(members, rows, part)
        block = jnp.concatenate([block[j ^ k] for j in range(members)], axis=0)
        attended = lax.dynamic_update_slice_in_dim(attended, block, (s ^ k) * part, 1)

    branch_one = product(attended, w_out) + bias_output
    middle = inputs + factor_one * branch_one
    normed_two, spread_two = normalize(middle)
    hidden_two = (normed_two * gain_two + offset_two).astype(bf16)
    before = product(hidden_two, w_up) + own_bias_up
    activated_full, slope = gelu_pair(before)
    activated = activated_full.astype(bf16)

    grads = out_grads * (segments >= 0).astype(f32)[:, None]
    grad_two = (grads * factor_two).astype(bf16)
    grad_before = (product_right(grad_two, w_down) * slope).astype(bf16)
    partial_hidden_two = product_right(grad_before, w_up)
    grad_hidden_two = sum(
        block.astype(f32)
        for block in exchange(
            [partial_hidden_two[:rows]]
            + [partial_hidden_two[k * rows : (k + 1) * rows].astype(bf16) for k in range(1, members)]
        )
    )

    partial_two = product(activated, w_down)
    branch_two = bias_down + sum(
        block.astype(f32)
        for block in exchange(
            [partial_two[:rows]]
            + [partial_two[k * rows : (k + 1) * rows].astype(bf16) for k in range(1, members)]
        )
    )
    own_middle, own_grad = middle[:rows], grads[:rows]
    layer_out = (own_middle + factor_two * branch_two).astype(bf16)
    grad_factor_two = jnp.sum(own_grad * branch_two, axis=0)
    grad_bias_down = jnp.sum(grad_two[:rows].astype(f32), axis=0)
    grad_bias_up = jnp.sum(grad_before.astype(f32), axis=0)

    own_normed_two = normed_two[:rows]
    grad_gain_two = jnp.sum(grad_hidden_two * own_normed_two, axis=0)
    grad_offset_two = jnp.sum(grad_hidden_two, axis=0)
    grad_middle = own_grad + normalize_back(
        grad_hidden_two * gain_two, own_normed_two, spread_two[:rows]
    )
    grad_factor_one = jnp.sum(grad_middle * branch_one[:rows], axis=0)
    grad_one = (grad_middle * factor_one).astype(bf16)
    grad_bias_output = jnp.sum(grad_one.astype(f32), axis=0)
    grad_attended = product_right(grad_one, w_out).astype(bf16)

    def columns(x, k):
        return lax.dynamic_slice_in_dim(x, (s ^ k) * part, part, 1)

    grad_heads = jnp.concatenate(
        exchange([columns(grad_attended, k) for k in range(members)]), axis=0
    )
    grad_one_cols = jnp.concatenate(exchange([columns(grad_one, k) for k in range(members)]), axis=0)
    grad_triple = attend_back(triple, segments, logsums, grad_heads, heads)
    partial_hidden_one = product_right(grad_triple, w_in)
    grad_hidden_one = sum(
        block.astype(f32)
        for block in exchange(
            [partial_hidden_one[:rows]]
            + [partial_hidden_one[k * rows : (k + 1) * rows].astype(bf16) for k in range(1, members)]
        )
    )
    own_normed_one = normed_one[:rows]
    grad_gain_one = jnp.sum(grad_hidden_one * own_normed_one, axis=0)
    grad_offset_one = jnp.sum(grad_hidden_one, axis=0)
    tokens_grad = (
        grad_middle
        + normalize_back(grad_hidden_one * gain_one, own_normed_one, spread_one[:rows])
    ).astype(bf16)

    def own_share(left, right, lead):
        full = product_left(left, right).astype(bf16)
        return scatter_fsdp(full.reshape(fsdp, lead, full.shape[1])).astype(bf16)

    share_down = own_share(activated, grad_two, ff_part)
    share_up = own_share(hidden_two, grad_before, shard)
    share_out = own_share(attended, grad_one_cols, shard)
    share_in = own_share(hidden_one, grad_triple, shard)

    grad_down = jnp.zeros(down_weight.shape, f32)
    for k, block in enumerate(from_others(share_down)):
        grad_down = lax.dynamic_update_slice_in_dim(
            grad_down, block.astype(f32), (s ^ k) * ff_part, 0
        )
    grad_up = jnp.zeros((shard, fsdp, ff_shard), f32)
    for k, block in enumerate(from_others(share_up)):
        grad_up = lax.dynamic_update_slice_in_dim(
            grad_up, block.astype(f32).reshape(shard, fsdp, ff_part), (s ^ k) * ff_part, 2
        )
    grad_up = grad_up.reshape(up_weight.shape)
    grad_out = jnp.zeros(output_weight.shape, f32)
    for k, block in enumerate(from_others(share_out)):
        grad_out = lax.dynamic_update_slice_in_dim(
            grad_out, block.astype(f32), (s ^ k) * part, 1
        )
    grad_in = jnp.zeros(input_weight.shape, f32)
    for k, block in enumerate(from_others(share_in)):
        grad_in = lax.dynamic_update_slice_in_dim(
            grad_in, block.astype(f32), (s ^ k) * own_cols, 1
        )

    triple_sums = jnp.sum(grad_triple.astype(f32), axis=0).reshape(heads, 3, HEAD_DIM)

    def placed(x, total):
        return lax.dynamic_update_slice_in_dim(
            jnp.zeros((total,), f32), x.reshape(-1), s * x.size, 0
        )

    grad_bias_up_full = lax.dynamic_update_slice_in_dim(
        jnp.zeros((fsdp, ff_shard), f32), grad_bias_up.reshape(fsdp, ff_part), s * ff_part, 1
    )
    vector_grads = (
        grad_gain_one,
        grad_offset_one,
        placed(triple_sums[:, 0], width),
        placed(triple_sums[:, 2], width),
        grad_bias_output,
        grad_factor_one,
        grad_gain_two,
        grad_offset_two,
        grad_bias_up_full,
        grad_bias_down,
        grad_factor_two,
    )
    packed = jnp.concatenate([v.reshape(fsdp, -1) for v in vector_grads], axis=1)
    packed = lax.psum(packed, "seq")
    vector_total = scatter_fsdp(packed.astype(bf16)[:, None, :])[0]
    outs = []
    offset = 0
    for size in widths:
        outs.append(vector_total[offset : offset + size])
        offset += size
    return (
        layer_out,
        tokens_grad,
        outs[0],
        outs[1],
        grad_in,
        outs[2],
        outs[3],
        grad_out,
        outs[4],
        outs[5],
        outs[6],
        outs[7],
        grad_up,
        outs[8],
        grad_down,
        outs[9],
        outs[10],
    )


def spec(kind=pltpu.VMEM):
    return pl.BlockSpec(memory_space=kind)


def shape(dims, kind):
    return jax.ShapeDtypeStruct(dims, kind)


def place():
    f, s = lax.axis_index("fsdp"), lax.axis_index("seq")
    z = f // 2
    odd = (z ^ (z // 2)) % 2
    return (f, s, z, z ^ (1 + odd), z ^ 3, z ^ (2 - odd))


def call(kernel, ins, outs, flops=0, name=None, scratch=(), in_hbm=False, limit=50):
    def placed(*refs):
        kernel(place(), *refs)

    in_specs = [spec(pltpu.HBM) if in_hbm else spec() for _ in ins]
    return pl.pallas_call(
        placed,
        out_shape=outs,
        in_specs=in_specs,
        out_specs=[spec() for _ in outs],
        scratch_shapes=list(scratch),
        compiler_params=pltpu.CompilerParams(vmem_limit_bytes=limit * 1024 * 1024),
        cost_estimate=pl.CostEstimate(flops=0, bytes_accessed=0, transcendentals=0),
        name=name,
    )(*ins)


def at(index, size):
    return pl.ds(pl.multiple_of(index * size, size), size)


def run_copies(pairs, sems):
    copies = [pltpu.make_async_copy(a, b, sems.at[i]) for i, (a, b) in enumerate(pairs)]
    for copy in copies:
        copy.start()
    return copies


def prepare_first(where, *refs):
    w_in, w_out, tokens, grad, vectors = refs[0], refs[1], refs[2], refs[3], refs[4:15]
    first, rows, held, (pack, sems) = refs[15], refs[16], refs[17:28], refs[28:]
    s = where[1]
    pairs = list(zip(vectors, held)) + [
        (pair[0], pair[1])
        for m in range(4)
        for pair in (
            (w_in.at[:, at(s, 768)], first.at[m, 0:128, 0:768]),
            (w_out.at[:, at(s, 256)], first.at[m, 0:128, 768:1024]),
        )
    ]
    pairs += [(tokens, rows.at[0:128]), (grad, rows.at[128:256])]
    copies = run_copies(pairs, sems)
    for copy in copies[:11]:
        copy.wait()
    pack[...] = jnp.zeros(pack.shape, f32)
    for i in range(10):
        pack[i : i + 1, 0:128] = held[i][...].astype(f32).reshape(1, 128)
    for i in range(4):
        pack[10 + i : 11 + i, 0:128] = (
            held[10][i * 128 : (i + 1) * 128].astype(f32).reshape(1, 128)
        )
    for m in range(4):
        first[m, 128:144] = pack[...].astype(bf16)
    for copy in copies[11:]:
        copy.wait()


def prepare_second(where, w_up, w_down, second, sems):
    s = where[1]
    pairs = [(w_down.at[at(s, 128)], second.at[128:256])]
    for i in range(8):
        lanes = pl.ds(pl.multiple_of(i * 512 + s * 128, 128), 128)
        pairs.append((w_up.at[:, lanes], second.at[0:128, i * 128 : (i + 1) * 128]))
    for copy in run_copies(pairs, sems):
        copy.wait()


def owner(where, t, b):
    return 2 * where[2 + t] + ((where[0] % 2) ^ b)


def place_first(where, own, other, w_in, w_out, vecs):
    for b, blocks in enumerate((own, other)):
        for z in range(4):
            n = 2 * z + ((where[0] % 2) ^ b)
            w_in[at(n, 128)] = blocks[z, 0:128, 0:768]
            w_out[at(n, 128)] = blocks[z, 0:128, 768:1024]
            vecs[:, at(n, 128)] = blocks[z, 128:144, 0:128].astype(f32)


def column_segments(where, seg):
    return jnp.concatenate([seg[at(where[1] ^ k, 128)] for k in range(4)], axis=0)


def row_segments(where, seg):
    return jnp.concatenate([seg[:, at(where[1] ^ k, 128)] for k in range(4)], axis=1)


def attention(where, t0, t1, t2, t3, w_in, vecs, seg_col, seg_row, triple, attended, logsum, hidden):
    gain, offset = vecs[0:1], vecs[1:2]
    for k, ref in enumerate((t0, t1, t2, t3)):
        normed, _ = normalize(ref[0:128].astype(f32))
        hidden[k * 128 : (k + 1) * 128] = (normed * gain + offset).astype(bf16)
    own = at(where[1], 256)
    query, value = vecs[2:3, own], vecs[3:4, own]
    zero = jnp.zeros((1, 64), f32)
    pieces = []
    for h in range(4):
        pieces += [query[:, h * 64 : (h + 1) * 64], zero, value[:, h * 64 : (h + 1) * 64]]
    triple[...] = (product(hidden[...], w_in[...]) + jnp.concatenate(pieces, axis=1)).astype(bf16)
    same = column_segments(where, seg_col) == row_segments(where, seg_row)
    outs = []
    for h in range(4):
        q, k, v = (triple[:, h * 192 + c * 64 : h * 192 + (c + 1) * 64] for c in range(3))
        scores = jnp.where(same, product_right(q, k) * HEAD_DIM**-0.5, masked_value)
        highest = jnp.max(scores, axis=1, keepdims=True)
        powers = jnp.exp(scores - highest)
        totals = jnp.sum(powers, axis=1, keepdims=True)
        probs = (powers * (1.0 / totals)).astype(bf16)
        outs.append(product(probs, v).astype(bf16))
        logsum[:, h : h + 1] = highest + jnp.log(totals)
    whole = jnp.concatenate(outs, axis=1)
    for m in range(4):
        attended[m] = whole


def project(
    where, sent, w0, w1, w2, w3, t0, t1, t2, t3, vecs, full, hidden, own_middle, own_branch, branch
):
    for m in range(4):
        for j in range(4):
            rows = at(where[1] ^ (j ^ m), 128)
            full[j * 128 : (j + 1) * 128, m * 256 : (m + 1) * 256] = sent[m, rows]
    for k, ref in enumerate((w0, w1, w2, w3)):
        branch[:, at(where[1] ^ k, 256)] = product(full[...], ref[...])
    for r, ref in enumerate((t0, t1, t2, t3)):
        rows = slice(r * 128, (r + 1) * 128)
        piece = branch[rows] + vecs[4:5]
        middle = ref[0:128].astype(f32) + vecs[5:6] * piece
        normed, _ = normalize(middle)
        hidden[rows] = (normed * vecs[6:7] + vecs[7:8]).astype(bf16)
        if r == 0:
            own_middle[...] = middle
            own_branch[...] = piece


def feed(where, *refs):
    hidden, blocks, tokens, (vecs, seg_col) = refs[0], refs[1:9], refs[9:13], refs[13:15]
    w_down, act, grad_two, grad_before, sums, p0, p1, p2, p3, w_up = refs[15:]
    for j in range(8):
        rows = at(owner(where, j // 2, j % 2), 128)
        w_up[rows] = blocks[j][0:128]
        w_down[rows] = blocks[j][128:256]
    valid = (column_segments(where, seg_col) >= 0).astype(f32)
    for k in range(4):
        rows = slice(k * 128, (k + 1) * 128)
        grad = tokens[k][128:256].astype(f32) * valid[rows]
        grad_two[rows] = (grad * vecs[9:10]).astype(bf16)
    bias = vecs[pl.ds(10 + where[1], 1)]
    for c in range(4):
        cols = slice(c * 256, (c + 1) * 256)
        before = product(hidden[...], w_up[:, cols]) + bias[:, cols]
        value, slope = gelu_pair(before)
        act[:, cols] = value.astype(bf16)
        back = (product_right(grad_two[...], w_down[cols]) * slope).astype(bf16)
        grad_before[:, cols] = back
        sums[:, cols] = jnp.sum(back.astype(f32), axis=0, keepdims=True)
    p0[...] = product_right(grad_before[0:128], w_up[...])
    for k, ref in ((1, p1), (2, p2), (3, p3)):
        ref[...] = product_right(grad_before[k * 128 : (k + 1) * 128], w_up[...]).astype(bf16)


def core_rows(where, z, own):
    return at(2 * z + ((where[0] % 2) if own else 1 - (where[0] % 2)), 128)


def feed_weights(where, *refs):
    hidden, grad_before, act, grad_two, w_down = refs[:5]
    tokens, (vecs, seg_col, mine, theirs, sums, *two) = refs[5:9], refs[9:]
    for k in range(4):
        for ref, own in ((mine, True), (theirs, False)):
            cols = core_rows(where, where[2 + k], own)
            ref[k, 0:128] = product_left(hidden[:, cols], grad_before[...]).astype(bf16)
            ref[k, 128:256] = product_left(act[:, cols], grad_two[...]).astype(bf16)
    valid = (column_segments(where, seg_col) >= 0).astype(f32)
    scale = jnp.zeros((1, 1024), f32)
    for k in range(4):
        rows = slice(k * 128, (k + 1) * 128)
        part = product(act[rows], w_down[...])
        grad = tokens[k][128:256].astype(f32) * valid[rows]
        two[k][...] = part.astype(bf16)
        if k == 0:
            part = part + vecs[8:9]
        scale = scale + jnp.sum(grad * part, axis=0, keepdims=True)
    sums[0:1] = jnp.sum(grad_two[0:128].astype(f32), axis=0, keepdims=True)
    sums[1:2] = scale


def middle_back(
    where, p0, p1, p2, p3, own_middle, own_branch, tokens, seg_col, vecs, w0, w1, w2, w3,
    grad_middle, sums, m0, m1, m2, m3, attended, one,
):
    total = p0[...] + p1[...].astype(f32) + p2[...].astype(f32) + p3[...].astype(f32)
    normed, spread = normalize(own_middle[...])
    valid = (seg_col[at(where[1], 128)] >= 0).astype(f32)
    back = tokens[128:256].astype(f32) * valid + normalize_back(total * vecs[6:7], normed, spread)
    grad_middle[...] = back
    grad_one = (back * vecs[5:6]).astype(bf16)
    one[...] = grad_one
    sums[0:1] = jnp.sum(total * normed, axis=0, keepdims=True)
    sums[1:2] = jnp.sum(total, axis=0, keepdims=True)
    sums[2:3] = jnp.sum(back * own_branch[...], axis=0, keepdims=True)
    sums[3:4] = jnp.sum(grad_one.astype(f32), axis=0, keepdims=True)
    result = jnp.zeros((128, 1024), f32)
    for k, ref in enumerate((w0, w1, w2, w3)):
        result = result + product_right(one[:, at(where[1] ^ k, 256)], ref[...])
    attended[...] = result.astype(bf16)
    for k, ref in enumerate((m0, m1, m2, m3)):
        cols = at(where[1] ^ k, 256)
        ref[0:128] = attended[:, cols]
        ref[128:256] = one[:, cols]


def attention_back(
    where, triple, logsum, m0, m1, m2, m3, seg_col, seg_row, w_in, t0, t1, t2, t3,
    grad_triple, sums, *last,
):
    same = column_segments(where, seg_col) == row_segments(where, seg_row)
    grads = jnp.concatenate([m[0:128] for m in (m0, m1, m2, m3)], axis=0)
    pieces = []
    for h in range(4):
        q, k, v = (triple[:, h * 192 + c * 64 : h * 192 + (c + 1) * 64] for c in range(3))
        g = grads[:, h * 64 : (h + 1) * 64]
        scores = jnp.where(same, product_right(q, k) * HEAD_DIM**-0.5, masked_value)
        weights = jnp.exp(scores - logsum[:, h : h + 1])
        grad_v = product_left(weights.astype(bf16), g)
        grad_weights = product_right(g, v)
        dots = jnp.sum(weights * grad_weights, axis=1, keepdims=True)
        grad_scores = (weights * (grad_weights - dots)).astype(bf16)
        grad_q = product(grad_scores, k) * HEAD_DIM**-0.5
        grad_k = product_left(grad_scores, q) * HEAD_DIM**-0.5
        pieces += [grad_q.astype(bf16), grad_k.astype(bf16), grad_v.astype(bf16)]
    whole = jnp.concatenate(pieces, axis=1)
    grad_triple[...] = whole
    columns = jnp.sum(whole.astype(f32), axis=0, keepdims=True)
    sums[...] = jnp.zeros(sums.shape, f32)
    lanes = at(where[1], 256)
    for row, c in ((2, 0), (3, 2)):
        sums[row : row + 1, lanes] = jnp.concatenate(
            [columns[:, h * 192 + c * 64 : h * 192 + (c + 1) * 64] for h in range(4)], axis=1
        )
    gain = jnp.zeros((1, 1024), f32)
    offset = jnp.zeros((1, 1024), f32)
    for k, ref in enumerate((t0, t1, t2, t3)):
        part = product_right(grad_triple[k * 128 : (k + 1) * 128], w_in[...])
        normed, _ = normalize(ref[0:128].astype(f32))
        gain = gain + jnp.sum(part * normed, axis=0, keepdims=True)
        offset = offset + jnp.sum(part, axis=0, keepdims=True)
        last[k][...] = part.astype(bf16)
    sums[0:1] = gain
    sums[1:2] = offset


def attention_weights(
    where, hidden, grad_triple, attended, m0, m1, m2, m3, up_sums, two_sums, mid_sums, one_sums,
    mine, theirs, vecs,
):
    ones = jnp.concatenate([m[128:256] for m in (m0, m1, m2, m3)], axis=0)
    vecs[...] = jnp.zeros(vecs.shape, f32)
    vecs[0:4] = one_sums[...]
    vecs[4:5] = mid_sums[3:4]
    vecs[5:6] = mid_sums[2:3]
    vecs[6:8] = mid_sums[0:2]
    vecs[8:10] = two_sums[0:2]
    vecs[pl.ds(10 + where[1], 1)] = up_sums[...]
    blank = jnp.zeros((16, 896), bf16)
    for k in range(4):
        for ref, own in ((mine, True), (theirs, False)):
            cols = core_rows(where, where[2 + k], own)
            ref[k, 0:128, 0:768] = product_left(hidden[:, cols], grad_triple[...]).astype(bf16)
            ref[k, 0:128, 768:1024] = product_left(attended[:, cols], ones).astype(bf16)
            ref[k, 128:144] = jnp.concatenate([vecs[:, cols].astype(bf16), blank], axis=1)


def finish_rows(where, *refs):
    ones, twos, (own_middle, grad_middle, tokens, vecs, out, grad) = refs[:4], refs[4:8], refs[8:]
    total = sum(ref[...].astype(f32) for ref in ones)
    two = sum(ref[...].astype(f32) for ref in twos) + vecs[8:9]
    out[...] = (own_middle[...] + vecs[9:10] * two).astype(bf16)
    normed, spread = normalize(tokens[0:128].astype(f32))
    grad[...] = (grad_middle[...] + normalize_back(total * vecs[0:1], normed, spread)).astype(bf16)


def finish_feed(where, got, up, down):
    for m in range(4):
        down[m * 128 : (m + 1) * 128] = got[m, 128:256].astype(f32)
        for n in range(8):
            lanes = slice(n * 512 + m * 128, n * 512 + (m + 1) * 128)
            up[:, lanes] = got[m, 0:128, n * 128 : (n + 1) * 128].astype(f32)


def finish_attention(where, s0, s1, s2, s3, w_in, w_out, *refs):
    outs, held = refs[:-1], refs[-1]
    for k, ref in enumerate((s0, s1, s2, s3)):
        m = where[1] ^ k
        w_in[:, at(m, 768)] = ref[0:128, 0:768].astype(f32)
        w_out[:, at(m, 256)] = ref[0:128, 768:1024].astype(f32)
        held[m] = ref[128:144, 0:128].astype(f32)
    total = held[0] + held[1] + held[2] + held[3]
    for i in range(10):
        outs[i][...] = total[i : i + 1]
    outs[10][...] = jnp.concatenate([total[i : i + 1] for i in range(10, 14)], axis=1)


def ring(count):
    return list(range(0, count, 2)) + list(range(count - 1, 0, -2))


def step(x, hops=1):
    order = ring(lax.axis_size("fsdp") // 2)
    count = len(order)
    pairs = [(order[i], order[(i + hops) % count]) for i in range(count)]
    return lax.ppermute(x, "fsdp", [(2 * a + c, 2 * b + c) for a, b in pairs for c in (0, 1)])


def along(x):
    count = lax.axis_size("fsdp") // 2
    groups = [[2 * z + c for z in range(count)] for c in (0, 1)]
    return lax.all_to_all(
        x, "fsdp", split_axis=0, concat_axis=0, axis_index_groups=groups, tiled=True
    )


def after(x, *earlier):
    return lax.optimization_barrier((x,) + earlier)[0]


def both_cores(blocks):
    return [b for block in blocks for b in (block, swap(block, "fsdp", 1))]


def pair_sums(mine, theirs):
    return [add(mine[t], theirs[t]) for t in range(4)]


def deal(x):
    return lax.all_to_all(x, "seq", split_axis=0, concat_axis=0, tiled=True)


def share(where, received, own, out):
    total = (received[...].astype(f32) + own[...].astype(f32)).astype(bf16)
    for m in range(4):
        out[m] = total


def deal_sum(x, y, name):
    (copies,) = call(share, [x, y], [shape((4,) + x.shape, bf16)], name=name)
    return deal(copies)


def add(x, y):
    return (x.astype(f32) + y.astype(f32)).astype(bf16)


def body(*args):
    tokens, input_weight, up_weight = args[0], args[4], args[12]
    fits = (
        lax.axis_size("seq") == 4
        and lax.axis_size("fsdp") == 8
        and tokens.shape == (128, 1024)
        and input_weight.shape == (128, 3072)
        and up_weight.shape == (128, 4096)
    )
    return body_fast(*args) if fits else body_any(*args)


def body_fast(
    tokens,
    segment_ids,
    first_gain,
    first_bias,
    input_weight,
    query_bias,
    value_bias,
    output_weight,
    output_bias,
    scale_one,
    second_gain,
    second_bias,
    up_weight,
    up_bias,
    down_weight,
    down_bias,
    scale_two,
    out_grad,
):
    vectors = [
        first_gain, first_bias, query_bias, value_bias, output_bias,
        scale_one, second_gain, second_bias, down_bias, scale_two, up_bias,
    ]
    seg_col, seg_row = segment_ids.reshape(512, 1), segment_ids.reshape(1, 512)
    mat = shape((512, 1024), bf16)
    rows_f, rows_b = shape((128, 1024), f32), shape((128, 1024), bf16)

    first, rows = call(
        prepare_first,
        [input_weight, output_weight, tokens, out_grad] + vectors,
        [shape((4, 144, 1024), bf16), shape((256, 1024), bf16)],
        name="prepare_first",
        scratch=[pltpu.VMEM(v.shape, bf16) for v in vectors] + [pltpu.VMEM((16, 1024), f32), pltpu.SemaphoreType.DMA((32,))],
        in_hbm=True,
        limit=63,
    )
    shared = from_others(rows)
    first_own = along(first)
    (second,) = call(
        prepare_second,
        [up_weight, down_weight],
        [shape((256, 1024), bf16)],
        name="prepare_second",
        scratch=[pltpu.SemaphoreType.DMA((36,))],
        in_hbm=True,
        limit=63,
    )
    second_1 = step(after(second, first_own, *shared[1:]))
    w_in, w_out_own, vecs = call(
        place_first,
        [first_own, swap(after(first_own, second, *shared[1:]), "fsdp", 1)],
        [shape((1024, 768), bf16), shape((1024, 256), bf16), shape((16, 1024), f32)],
        name="place_first",
        limit=63,
    )
    w_out = from_others(w_out_own)
    triple, attended_own, logsum, hidden_one = call(
        attention,
        shared + [w_in, vecs, seg_col, seg_row],
        [shape((512, 768), bf16), shape((4, 512, 256), bf16), shape((512, 128), f32), mat],
        name="attention",
    )
    second_2 = step(after(second_1, attended_own))
    second_3 = step(after(second_2, *w_out[1:]))
    shares = deal(attended_own)
    attended, hidden_two, own_middle, own_branch = call(
        project,
        [shares] + w_out + shared + [vecs],
        [mat, mat, rows_f, rows_f],
        name="project",
        scratch=[pltpu.VMEM((512, 1024), f32)],
    )
    w_down, act, grad_two, grad_before, up_sums, *partial = call(
        feed,
        [hidden_two]
        + both_cores([after(x, shares) for x in (second, second_1, second_2)] + [after(second_3, hidden_two)])
        + shared + [vecs, seg_col],
        [shape((1024, 1024), bf16), mat, mat, mat, shape((1, 1024), f32), rows_f, rows_b, rows_b, rows_b],
        name="feed",
        scratch=[pltpu.VMEM((1024, 1024), bf16)],
    )
    partial = exchange(partial)
    second_mine, second_theirs, two_sums, *two = call(
        feed_weights,
        [hidden_two, grad_before, act, grad_two, w_down] + shared + [vecs, seg_col],
        [shape((4, 256, 1024), bf16)] * 2 + [shape((2, 1024), f32)] + [rows_b] * 4,
        name="feed_weights",
    )
    second_theirs = swap(after(second_theirs, two[0], *partial[1:]), "fsdp", 1)
    grad_middle, mid_sums, *messages = call(
        middle_back,
        partial + [own_middle, own_branch, rows, seg_col, vecs] + w_out,
        [rows_f, shape((4, 1024), f32)] + [shape((256, 256), bf16)] * 4,
        name="middle_back",
        scratch=[pltpu.VMEM((128, 1024), bf16), pltpu.VMEM((128, 1024), bf16)],
    )
    got = exchange(messages)
    second_sums = pair_sums(after(second_mine, messages[1]), second_theirs)
    second_added = add(step(second_sums[1]), after(second_sums[2], *got[1:]))
    got = [after(got[0], second_added)] + got[1:]
    second_total = step(second_added)
    twos = exchange([two[0]] + [after(x, *got[1:]) for x in two[1:]])
    grad_triple, one_sums, *last = call(
        attention_back,
        [triple, logsum] + got + [seg_col, seg_row, w_in] + shared,
        [shape((512, 768), bf16), shape((4, 1024), f32)] + [rows_b] * 4,
        flops=20 * 512 * 1024 * 1024,
        name="attention_back",
    )
    first_mine, first_theirs = call(
        attention_weights,
        [hidden_one, grad_triple, attended] + got + [up_sums, two_sums, mid_sums, one_sums],
        [shape((4, 144, 1024), bf16)] * 2,
        flops=20 * 512 * 1024 * 1024,
        name="attention_weights",
        scratch=[pltpu.VMEM((16, 1024), f32)],
    )
    ones = exchange([last[0]] + [after(x, *twos[1:]) for x in last[1:]])
    first_sums = pair_sums(first_mine, swap(after(first_theirs, second_total, *twos[1:]), "fsdp", 1))
    second_total = step(add(second_total, second_sums[3]))
    first_added = after(add(step(first_sums[1]), first_sums[2]), second_total, *ones[1:])
    layer_out, tokens_grad = call(
        finish_rows,
        ones + twos + [own_middle, grad_middle, rows, vecs],
        [rows_b, rows_b],
        name="finish_rows",
        limit=63,
    )
    grad_up, grad_down = call(
        finish_feed,
        [deal_sum(second_total, second_sums[0], "share_feed")],
        [shape((128, 4096), f32), shape((512, 1024), f32)],
        name="finish_feed",
    )
    first_total = step(first_added)
    first_total = step(after(add(first_total, first_sums[3]), layer_out))
    first_share = from_others(add(first_total, first_sums[0]))
    grad_in, grad_out, *small = call(
        finish_attention,
        [after(first_share[0], grad_up)] + first_share[1:],
        [shape((128, 3072), f32), rows_f] + [shape((1, 128), f32)] * 10 + [shape((1, 512), f32)],
        name="finish_attention",
        scratch=[pltpu.VMEM((4, 16, 128), f32)],
    )
    g = [v.reshape(-1) for v in small]
    return (
        layer_out, tokens_grad, g[0], g[1], grad_in, g[2], g[3], grad_out, g[4],
        g[5], g[6], g[7], grad_up, g[10], grad_down, g[8], g[9],
    )


def solution(mesh):
    rows, vec, mat = P(("fsdp", "seq"), None), P("fsdp"), P("fsdp", None)
    return jax.shard_map(
        body,
        mesh=mesh,
        in_specs=(
            rows, vec, vec, vec, mat, vec, vec, mat, vec,
            vec, vec, vec, mat, vec, mat, vec, vec, rows,
        ),
        out_specs=(
            rows, rows, vec, vec, mat, vec, vec, mat, vec,
            vec, vec, vec, mat, vec, mat, vec, vec,
        ),
        check_vma=False,
    )
```

```python
import math

import jax
import jax.numpy as jnp
from jax import lax
from jax.experimental import pallas as pl
from jax.experimental.pallas import tpu as pltpu
from jax.sharding import PartitionSpec as P

HEADS = 16
HEAD_DIM = 64
epsilon = 1e-06
masked_value = -1000000000.0
bf16 = jnp.bfloat16
f32 = jnp.float32


def product(left, right):
    return jnp.dot(left, right, preferred_element_type=f32)


def product_left(left, right):
    return lax.dot_general(left, right, (((0,), (0,)), ((), ())), preferred_element_type=f32)


def product_right(left, right):
    return lax.dot_general(left, right, (((1,), (1,)), ((), ())), preferred_element_type=f32)


def normalize(values):
    center = values - jnp.mean(values, axis=1, keepdims=True)
    spread = lax.rsqrt(jnp.mean(center * center, axis=1, keepdims=True) + epsilon)
    return (center * spread, spread)


def normalize_back(grad_normed, normed, spread):
    return spread * (
        grad_normed
        - jnp.mean(grad_normed, axis=1, keepdims=True)
        - normed * jnp.mean(grad_normed * normed, axis=1, keepdims=True)
    )


def gelu_pair(before):
    normal_cdf = 0.5 * (1.0 + lax.erf(before * (1.0 / math.sqrt(2.0))))
    density = jnp.exp(-0.5 * before * before) * (1.0 / math.sqrt(2.0 * math.pi))
    return (before * normal_cdf, normal_cdf + before * density)


def swap(x, axis, k):
    count = lax.axis_size(axis)
    return lax.ppermute(x, axis, [(i, i ^ k) for i in range(count)])


def from_others(x):
    return [x] + [swap(x, "seq", k) for k in range(1, lax.axis_size("seq"))]


def exchange(blocks):
    return [blocks[0]] + [swap(blocks[k], "seq", k) for k in range(1, len(blocks))]


def gather_fsdp(x):
    count = lax.axis_size("fsdp")
    f = lax.axis_index("fsdp")
    same = [x] + [swap(x, "fsdp", 2 * k) for k in range(1, count // 2)]
    other = swap(jnp.stack(same), "fsdp", 1)
    out = jnp.zeros((count,) + x.shape, x.dtype)
    for k in range(count // 2):
        out = lax.dynamic_update_index_in_dim(out, same[k], f ^ (2 * k), 0)
        out = lax.dynamic_update_index_in_dim(out, other[k], f ^ (2 * k + 1), 0)
    return out


def scatter_fsdp(g):
    count = g.shape[0]
    f = lax.axis_index("fsdp")
    z, core = f // 2, f % 2
    pairs = g.reshape((count // 2, 2) + g.shape[1:])
    mine = lax.dynamic_index_in_dim(pairs, core, 1, keepdims=False)
    theirs = lax.dynamic_index_in_dim(pairs, 1 - core, 1, keepdims=False)
    sums = (mine.astype(f32) + swap(theirs, "fsdp", 1).astype(f32)).astype(bf16)
    total = lax.dynamic_index_in_dim(sums, z, 0, keepdims=False).astype(f32)
    for k in range(1, count // 2):
        block = lax.dynamic_index_in_dim(sums, z ^ k, 0, keepdims=False)
        total = total + swap(block, "fsdp", 2 * k).astype(f32)
    return total


def attend(triple, segments, heads):
    rows = triple.shape[0]
    parts = triple.reshape(rows, heads, 3, HEAD_DIM)
    outs = []
    logsums = []
    same = segments[:, None] == segments[None, :]
    for h in range(heads):
        q, k, v = parts[:, h, 0], parts[:, h, 1], parts[:, h, 2]
        scores = jnp.where(same, product_right(q, k) * HEAD_DIM**-0.5, masked_value)
        highest = jnp.max(scores, axis=1, keepdims=True)
        powers = jnp.exp(scores - highest)
        totals = jnp.sum(powers, axis=1, keepdims=True)
        outs.append(product((powers / totals).astype(bf16), v).astype(bf16))
        logsums.append(highest + jnp.log(totals))
    return jnp.concatenate(outs, axis=1), logsums


def attend_back(triple, segments, logsums, grad, heads):
    rows = triple.shape[0]
    parts = triple.reshape(rows, heads, 3, HEAD_DIM)
    same = segments[:, None] == segments[None, :]
    outs = []
    for h in range(heads):
        q, k, v = parts[:, h, 0], parts[:, h, 1], parts[:, h, 2]
        g = grad[:, h * HEAD_DIM : (h + 1) * HEAD_DIM]
        scores = jnp.where(same, product_right(q, k) * HEAD_DIM**-0.5, masked_value)
        weights = jnp.exp(scores - logsums[h])
        grad_v = product_left(weights.astype(bf16), g)
        grad_weights = product_right(g, v)
        dots = jnp.sum(weights * grad_weights, axis=1, keepdims=True)
        grad_scores = (weights * (grad_weights - dots)).astype(bf16)
        grad_q = product(grad_scores, k) * HEAD_DIM**-0.5
        grad_k = product_left(grad_scores, q) * HEAD_DIM**-0.5
        outs.extend([grad_q, grad_k, grad_v])
    return jnp.concatenate(outs, axis=1).astype(bf16)


def body_any(
    tokens,
    segment_ids,
    first_gain,
    first_bias,
    input_weight,
    query_bias,
    value_bias,
    output_weight,
    output_bias,
    scale_one,
    second_gain,
    second_bias,
    up_weight,
    up_bias,
    down_weight,
    down_bias,
    scale_two,
    out_grad,
):
    members = lax.axis_size("seq")
    fsdp = lax.axis_size("fsdp")
    s = lax.axis_index("seq")
    rows, width = tokens.shape
    heads = HEADS // members
    own_cols = 3 * HEAD_DIM * heads
    part = width // members
    shard = input_weight.shape[0]
    ff_shard = down_weight.shape[0]
    ff_part = ff_shard // members

    local_vectors = (
        first_gain,
        first_bias,
        query_bias,
        value_bias,
        output_bias,
        scale_one,
        second_gain,
        second_bias,
        up_bias,
        down_bias,
        scale_two,
    )
    widths = [v.shape[0] for v in local_vectors]
    packed_width = sum(widths)

    own_in = lax.dynamic_slice_in_dim(input_weight, s * own_cols, own_cols, 1)
    own_out = lax.dynamic_slice_in_dim(output_weight, s * part, part, 1)
    own_up = lax.dynamic_slice_in_dim(
        up_weight.reshape(shard, fsdp, ff_shard), s * ff_part, ff_part, 2
    ).reshape(shard, fsdp * ff_part)
    own_down = lax.dynamic_slice_in_dim(down_weight, s * ff_part, ff_part, 0)

    vectors = gather_fsdp(jnp.concatenate(local_vectors)[None, :])[:, 0]
    w_in = gather_fsdp(own_in).reshape(width, own_cols)
    w_out_part = gather_fsdp(own_out).reshape(width, part)
    w_up = gather_fsdp(own_up).reshape(width, fsdp * ff_part)
    w_down = gather_fsdp(own_down).reshape(fsdp * ff_part, width)
    w_out = jnp.zeros((width, width), bf16)
    for k, block in enumerate(from_others(w_out_part)):
        w_out = lax.dynamic_update_slice_in_dim(w_out, block, (s ^ k) * part, 1)

    pieces = []
    offset = 0
    for size in widths:
        pieces.append(vectors[:, offset : offset + size].reshape(-1).astype(f32))
        offset += size
    (
        gain_one,
        offset_one,
        bias_query,
        bias_value,
        bias_output,
        factor_one,
        gain_two,
        offset_two,
        bias_up,
        bias_down,
        factor_two,
    ) = pieces
    own_bias_up = lax.dynamic_slice_in_dim(
        bias_up.reshape(fsdp, ff_shard), s * ff_part, ff_part, 1
    ).reshape(-1)
    own_query = lax.dynamic_slice_in_dim(bias_query, s * part, part, 0)
    own_value = lax.dynamic_slice_in_dim(bias_value, s * part, part, 0)

    inputs = jnp.concatenate(from_others(tokens), axis=0).astype(f32)
    out_grads = jnp.concatenate(from_others(out_grad), axis=0).astype(f32)
    segments = jnp.concatenate(
        [lax.dynamic_slice_in_dim(segment_ids, (s ^ k) * rows, rows, 0) for k in range(members)]
    )

    normed_one, spread_one = normalize(inputs)
    hidden_one = (normed_one * gain_one + offset_one).astype(bf16)
    bias_own = jnp.stack(
        [
            own_query.reshape(heads, HEAD_DIM),
            jnp.zeros((heads, HEAD_DIM), f32),
            own_value.reshape(heads, HEAD_DIM),
        ],
        axis=1,
    ).reshape(-1)
    triple = (product(hidden_one, w_in) + bias_own).astype(bf16)
    attended_own, logsums = attend(triple, segments, heads)

    attended = jnp.zeros((members * rows, width), bf16)
    for k, block in enumerate(from_others(attended_own)):
        block = block.reshape(members, rows, part)
        block = jnp.concatenate([block[j ^ k] for j in range(members)], axis=0)
        attended = lax.dynamic_update_slice_in_dim(attended, block, (s ^ k) * part, 1)

    branch_one = product(attended, w_out) + bias_output
    middle = inputs + factor_one * branch_one
    normed_two, spread_two = normalize(middle)
    hidden_two = (normed_two * gain_two + offset_two).astype(bf16)
    before = product(hidden_two, w_up) + own_bias_up
    activated_full, slope = gelu_pair(before)
    activated = activated_full.astype(bf16)

    grads = out_grads * (segments >= 0).astype(f32)[:, None]
    grad_two = (grads * factor_two).astype(bf16)
    grad_before = (product_right(grad_two, w_down) * slope).astype(bf16)
    partial_hidden_two = product_right(grad_before, w_up)
    grad_hidden_two = sum(
        block.astype(f32)
        for block in exchange(
            [partial_hidden_two[:rows]]
            + [partial_hidden_two[k * rows : (k + 1) * rows].astype(bf16) for k in range(1, members)]
        )
    )

    partial_two = product(activated, w_down)
    branch_two = bias_down + sum(
        block.astype(f32)
        for block in exchange(
            [partial_two[:rows]]
            + [partial_two[k * rows : (k + 1) * rows].astype(bf16) for k in range(1, members)]
        )
    )
    own_middle, own_grad = middle[:rows], grads[:rows]
    layer_out = (own_middle + factor_two * branch_two).astype(bf16)
    grad_factor_two = jnp.sum(own_grad * branch_two, axis=0)
    grad_bias_down = jnp.sum(grad_two[:rows].astype(f32), axis=0)
    grad_bias_up = jnp.sum(grad_before.astype(f32), axis=0)

    own_normed_two = normed_two[:rows]
    grad_gain_two = jnp.sum(grad_hidden_two * own_normed_two, axis=0)
    grad_offset_two = jnp.sum(grad_hidden_two, axis=0)
    grad_middle = own_grad + normalize_back(
        grad_hidden_two * gain_two, own_normed_two, spread_two[:rows]
    )
    grad_factor_one = jnp.sum(grad_middle * branch_one[:rows], axis=0)
    grad_one = (grad_middle * factor_one).astype(bf16)
    grad_bias_output = jnp.sum(grad_one.astype(f32), axis=0)
    grad_attended = product_right(grad_one, w_out).astype(bf16)

    def columns(x, k):
        return lax.dynamic_slice_in_dim(x, (s ^ k) * part, part, 1)

    grad_heads = jnp.concatenate(
        exchange([columns(grad_attended, k) for k in range(members)]), axis=0
    )
    grad_one_cols = jnp.concatenate(exchange([columns(grad_one, k) for k in range(members)]), axis=0)
    grad_triple = attend_back(triple, segments, logsums, grad_heads, heads)
    partial_hidden_one = product_right(grad_triple, w_in)
    grad_hidden_one = sum(
        block.astype(f32)
        for block in exchange(
            [partial_hidden_one[:rows]]
            + [partial_hidden_one[k * rows : (k + 1) * rows].astype(bf16) for k in range(1, members)]
        )
    )
    own_normed_one = normed_one[:rows]
    grad_gain_one = jnp.sum(grad_hidden_one * own_normed_one, axis=0)
    grad_offset_one = jnp.sum(grad_hidden_one, axis=0)
    tokens_grad = (
        grad_middle
        + normalize_back(grad_hidden_one * gain_one, own_normed_one, spread_one[:rows])
    ).astype(bf16)

    def own_share(left, right, lead):
        full = product_left(left, right).astype(bf16)
        return scatter_fsdp(full.reshape(fsdp, lead, full.shape[1])).astype(bf16)

    share_down = own_share(activated, grad_two, ff_part)
    share_up = own_share(hidden_two, grad_before, shard)
    share_out = own_share(attended, grad_one_cols, shard)
    share_in = own_share(hidden_one, grad_triple, shard)

    grad_down = jnp.zeros(down_weight.shape, f32)
    for k, block in enumerate(from_others(share_down)):
        grad_down = lax.dynamic_update_slice_in_dim(
            grad_down, block.astype(f32), (s ^ k) * ff_part, 0
        )
    grad_up = jnp.zeros((shard, fsdp, ff_shard), f32)
    for k, block in enumerate(from_others(share_up)):
        grad_up = lax.dynamic_update_slice_in_dim(
            grad_up, block.astype(f32).reshape(shard, fsdp, ff_part), (s ^ k) * ff_part, 2
        )
    grad_up = grad_up.reshape(up_weight.shape)
    grad_out = jnp.zeros(output_weight.shape, f32)
    for k, block in enumerate(from_others(share_out)):
        grad_out = lax.dynamic_update_slice_in_dim(
            grad_out, block.astype(f32), (s ^ k) * part, 1
        )
    grad_in = jnp.zeros(input_weight.shape, f32)
    for k, block in enumerate(from_others(share_in)):
        grad_in = lax.dynamic_update_slice_in_dim(
            grad_in, block.astype(f32), (s ^ k) * own_cols, 1
        )

    triple_sums = jnp.sum(grad_triple.astype(f32), axis=0).reshape(heads, 3, HEAD_DIM)

    def placed(x, total):
        return lax.dynamic_update_slice_in_dim(
            jnp.zeros((total,), f32), x.reshape(-1), s * x.size, 0
        )

    grad_bias_up_full = lax.dynamic_update_slice_in_dim(
        jnp.zeros((fsdp, ff_shard), f32), grad_bias_up.reshape(fsdp, ff_part), s * ff_part, 1
    )
    vector_grads = (
        grad_gain_one,
        grad_offset_one,
        placed(triple_sums[:, 0], width),
        placed(triple_sums[:, 2], width),
        grad_bias_output,
        grad_factor_one,
        grad_gain_two,
        grad_offset_two,
        grad_bias_up_full,
        grad_bias_down,
        grad_factor_two,
    )
    packed = jnp.concatenate([v.reshape(fsdp, -1) for v in vector_grads], axis=1)
    packed = lax.psum(packed, "seq")
    vector_total = scatter_fsdp(packed.astype(bf16)[:, None, :])[0]
    outs = []
    offset = 0
    for size in widths:
        outs.append(vector_total[offset : offset + size])
        offset += size
    return (
        layer_out,
        tokens_grad,
        outs[0],
        outs[1],
        grad_in,
        outs[2],
        outs[3],
        grad_out,
        outs[4],
        outs[5],
        outs[6],
        outs[7],
        grad_up,
        outs[8],
        grad_down,
        outs[9],
        outs[10],
    )


def spec(kind=pltpu.VMEM):
    return pl.BlockSpec(memory_space=kind)


def shape(dims, kind):
    return jax.ShapeDtypeStruct(dims, kind)


def place():
    f, s = lax.axis_index("fsdp"), lax.axis_index("seq")
    z = f // 2
    odd = (z ^ (z // 2)) % 2
    return (f, s, z, z ^ (1 + odd), z ^ 3, z ^ (2 - odd))


def call(kernel, ins, outs, flops=0, name=None, scratch=(), in_hbm=False, limit=50):
    def placed(*refs):
        kernel(place(), *refs)

    in_specs = [spec(pltpu.HBM) if in_hbm else spec() for _ in ins]
    return pl.pallas_call(
        placed,
        out_shape=outs,
        in_specs=in_specs,
        out_specs=[spec() for _ in outs],
        scratch_shapes=list(scratch),
        compiler_params=pltpu.CompilerParams(vmem_limit_bytes=limit * 1024 * 1024),
        cost_estimate=pl.CostEstimate(flops=0, bytes_accessed=0, transcendentals=0),
        name=name,
    )(*ins)


def at(index, size):
    return pl.ds(pl.multiple_of(index * size, size), size)


def run_copies(pairs, sems):
    copies = [pltpu.make_async_copy(a, b, sems.at[i]) for i, (a, b) in enumerate(pairs)]
    for copy in copies:
        copy.start()
    return copies


def prepare_first(where, *refs):
    w_in, w_out, tokens, grad, vectors = refs[0], refs[1], refs[2], refs[3], refs[4:15]
    first, rows, held, (pack, sems) = refs[15], refs[16], refs[17:28], refs[28:]
    s = where[1]
    pairs = list(zip(vectors, held)) + [
        (pair[0], pair[1])
        for m in range(4)
        for pair in (
            (w_in.at[:, at(s, 768)], first.at[m, 0:128, 0:768]),
            (w_out.at[:, at(s, 256)], first.at[m, 0:128, 768:1024]),
        )
    ]
    pairs += [(tokens, rows.at[0:128]), (grad, rows.at[128:256])]
    copies = run_copies(pairs, sems)
    for copy in copies[:11]:
        copy.wait()
    pack[...] = jnp.zeros(pack.shape, f32)
    for i in range(10):
        pack[i : i + 1, 0:128] = held[i][...].astype(f32).reshape(1, 128)
    for i in range(4):
        pack[10 + i : 11 + i, 0:128] = (
            held[10][i * 128 : (i + 1) * 128].astype(f32).reshape(1, 128)
        )
    for m in range(4):
        first[m, 128:144] = pack[...].astype(bf16)
    for copy in copies[11:]:
        copy.wait()


def prepare_second(where, w_up, w_down, second, sems):
    s = where[1]
    pairs = [(w_down.at[at(s, 128)], second.at[128:256])]
    for i in range(8):
        lanes = pl.ds(pl.multiple_of(i * 512 + s * 128, 128), 128)
        pairs.append((w_up.at[:, lanes], second.at[0:128, i * 128 : (i + 1) * 128]))
    for copy in run_copies(pairs, sems):
        copy.wait()


def owner(where, t, b):
    return 2 * where[2 + t] + ((where[0] % 2) ^ b)


def place_first(where, own, other, w_in, w_out, vecs):
    for b, blocks in enumerate((own, other)):
        for z in range(4):
            n = 2 * z + ((where[0] % 2) ^ b)
            w_in[at(n, 128)] = blocks[z, 0:128, 0:768]
            w_out[at(n, 128)] = blocks[z, 0:128, 768:1024]
            vecs[:, at(n, 128)] = blocks[z, 128:144, 0:128].astype(f32)


def column_segments(where, seg):
    return jnp.concatenate([seg[at(where[1] ^ k, 128)] for k in range(4)], axis=0)


def row_segments(where, seg):
    return jnp.concatenate([seg[:, at(where[1] ^ k, 128)] for k in range(4)], axis=1)


def attention(where, t0, t1, t2, t3, w_in, vecs, seg_col, seg_row, triple, attended, logsum, hidden):
    gain, offset = vecs[0:1], vecs[1:2]
    for k, ref in enumerate((t0, t1, t2, t3)):
        normed, _ = normalize(ref[0:128].astype(f32))
        hidden[k * 128 : (k + 1) * 128] = (normed * gain + offset).astype(bf16)
    own = at(where[1], 256)
    query, value = vecs[2:3, own], vecs[3:4, own]
    zero = jnp.zeros((1, 64), f32)
    pieces = []
    for h in range(4):
        pieces += [query[:, h * 64 : (h + 1) * 64], zero, value[:, h * 64 : (h + 1) * 64]]
    triple[...] = (product(hidden[...], w_in[...]) + jnp.concatenate(pieces, axis=1)).astype(bf16)
    same = column_segments(where, seg_col) == row_segments(where, seg_row)
    outs = []
    for h in range(4):
        q, k, v = (triple[:, h * 192 + c * 64 : h * 192 + (c + 1) * 64] for c in range(3))
        scores = jnp.where(same, product_right(q, k) * HEAD_DIM**-0.5, masked_value)
        highest = jnp.max(scores, axis=1, keepdims=True)
        powers = jnp.exp(scores - highest)
        totals = jnp.sum(powers, axis=1, keepdims=True)
        probs = (powers * (1.0 / totals)).astype(bf16)
        outs.append(product(probs, v).astype(bf16))
        logsum[:, h : h + 1] = highest + jnp.log(totals)
    whole = jnp.concatenate(outs, axis=1)
    for m in range(4):
        attended[m] = whole


def project(
    where, sent, w0, w1, w2, w3, t0, t1, t2, t3, vecs, full, hidden, own_middle, own_branch, branch
):
    for m in range(4):
        for j in range(4):
            rows = at(where[1] ^ (j ^ m), 128)
            full[j * 128 : (j + 1) * 128, m * 256 : (m + 1) * 256] = sent[m, rows]
    for k, ref in enumerate((w0, w1, w2, w3)):
        branch[:, at(where[1] ^ k, 256)] = product(full[...], ref[...])
    for r, ref in enumerate((t0, t1, t2, t3)):
        rows = slice(r * 128, (r + 1) * 128)
        piece = branch[rows] + vecs[4:5]
        middle = ref[0:128].astype(f32) + vecs[5:6] * piece
        normed, _ = normalize(middle)
        hidden[rows] = (normed * vecs[6:7] + vecs[7:8]).astype(bf16)
        if r == 0:
            own_middle[...] = middle
            own_branch[...] = piece


def feed(where, *refs):
    hidden, blocks, tokens, (vecs, seg_col) = refs[0], refs[1:9], refs[9:13], refs[13:15]
    w_down, act, grad_two, grad_before, sums, p0, p1, p2, p3, w_up = refs[15:]
    for j in range(8):
        rows = at(owner(where, j // 2, j % 2), 128)
        w_up[rows] = blocks[j][0:128]
        w_down[rows] = blocks[j][128:256]
    valid = (column_segments(where, seg_col) >= 0).astype(f32)
    for k in range(4):
        rows = slice(k * 128, (k + 1) * 128)
        grad = tokens[k][128:256].astype(f32) * valid[rows]
        grad_two[rows] = (grad * vecs[9:10]).astype(bf16)
    bias = vecs[pl.ds(10 + where[1], 1)]
    for c in range(4):
        cols = slice(c * 256, (c + 1) * 256)
        before = product(hidden[...], w_up[:, cols]) + bias[:, cols]
        value, slope = gelu_pair(before)
        act[:, cols] = value.astype(bf16)
        back = (product_right(grad_two[...], w_down[cols]) * slope).astype(bf16)
        grad_before[:, cols] = back
        sums[:, cols] = jnp.sum(back.astype(f32), axis=0, keepdims=True)
    p0[...] = product_right(grad_before[0:128], w_up[...])
    for k, ref in ((1, p1), (2, p2), (3, p3)):
        ref[...] = product_right(grad_before[k * 128 : (k + 1) * 128], w_up[...]).astype(bf16)


def core_rows(where, z, own):
    return at(2 * z + ((where[0] % 2) if own else 1 - (where[0] % 2)), 128)


def feed_weights(where, *refs):
    hidden, grad_before, act, grad_two, w_down = refs[:5]
    tokens, (vecs, seg_col, mine, theirs, sums, *two) = refs[5:9], refs[9:]
    for k in range(4):
        for ref, own in ((mine, True), (theirs, False)):
            cols = core_rows(where, where[2 + k], own)
            ref[k, 0:128] = product_left(hidden[:, cols], grad_before[...]).astype(bf16)
            ref[k, 128:256] = product_left(act[:, cols], grad_two[...]).astype(bf16)
    valid = (column_segments(where, seg_col) >= 0).astype(f32)
    scale = jnp.zeros((1, 1024), f32)
    for k in range(4):
        rows = slice(k * 128, (k + 1) * 128)
        part = product(act[rows], w_down[...])
        grad = tokens[k][128:256].astype(f32) * valid[rows]
        two[k][...] = part.astype(bf16)
        if k == 0:
            part = part + vecs[8:9]
        scale = scale + jnp.sum(grad * part, axis=0, keepdims=True)
    sums[0:1] = jnp.sum(grad_two[0:128].astype(f32), axis=0, keepdims=True)
    sums[1:2] = scale


def middle_back(
    where, p0, p1, p2, p3, own_middle, own_branch, tokens, seg_col, vecs, w0, w1, w2, w3,
    grad_middle, sums, m0, m1, m2, m3, attended, one,
):
    total = p0[...] + p1[...].astype(f32) + p2[...].astype(f32) + p3[...].astype(f32)
    normed, spread = normalize(own_middle[...])
    valid = (seg_col[at(where[1], 128)] >= 0).astype(f32)
    back = tokens[128:256].astype(f32) * valid + normalize_back(total * vecs[6:7], normed, spread)
    grad_middle[...] = back
    grad_one = (back * vecs[5:6]).astype(bf16)
    one[...] = grad_one
    sums[0:1] = jnp.sum(total * normed, axis=0, keepdims=True)
    sums[1:2] = jnp.sum(total, axis=0, keepdims=True)
    sums[2:3] = jnp.sum(back * own_branch[...], axis=0, keepdims=True)
    sums[3:4] = jnp.sum(grad_one.astype(f32), axis=0, keepdims=True)
    result = jnp.zeros((128, 1024), f32)
    for k, ref in enumerate((w0, w1, w2, w3)):
        result = result + product_right(one[:, at(where[1] ^ k, 256)], ref[...])
    attended[...] = result.astype(bf16)
    for k, ref in enumerate((m0, m1, m2, m3)):
        cols = at(where[1] ^ k, 256)
        ref[0:128] = attended[:, cols]
        ref[128:256] = one[:, cols]


def attention_back(
    where, triple, logsum, m0, m1, m2, m3, seg_col, seg_row, w_in, t0, t1, t2, t3,
    grad_triple, sums, *last,
):
    same = column_segments(where, seg_col) == row_segments(where, seg_row)
    grads = jnp.concatenate([m[0:128] for m in (m0, m1, m2, m3)], axis=0)
    pieces = []
    for h in range(4):
        q, k, v = (triple[:, h * 192 + c * 64 : h * 192 + (c + 1) * 64] for c in range(3))
        g = grads[:, h * 64 : (h + 1) * 64]
        scores = jnp.where(same, product_right(q, k) * HEAD_DIM**-0.5, masked_value)
        weights = jnp.exp(scores - logsum[:, h : h + 1])
        grad_v = product_left(weights.astype(bf16), g)
        grad_weights = product_right(g, v)
        dots = jnp.sum(weights * grad_weights, axis=1, keepdims=True)
        grad_scores = (weights * (grad_weights - dots)).astype(bf16)
        grad_q = product(grad_scores, k) * HEAD_DIM**-0.5
        grad_k = product_left(grad_scores, q) * HEAD_DIM**-0.5
        pieces += [grad_q.astype(bf16), grad_k.astype(bf16), grad_v.astype(bf16)]
    whole = jnp.concatenate(pieces, axis=1)
    grad_triple[...] = whole
    columns = jnp.sum(whole.astype(f32), axis=0, keepdims=True)
    sums[...] = jnp.zeros(sums.shape, f32)
    lanes = at(where[1], 256)
    for row, c in ((2, 0), (3, 2)):
        sums[row : row + 1, lanes] = jnp.concatenate(
            [columns[:, h * 192 + c * 64 : h * 192 + (c + 1) * 64] for h in range(4)], axis=1
        )
    gain = jnp.zeros((1, 1024), f32)
    offset = jnp.zeros((1, 1024), f32)
    for k, ref in enumerate((t0, t1, t2, t3)):
        part = product_right(grad_triple[k * 128 : (k + 1) * 128], w_in[...])
        normed, _ = normalize(ref[0:128].astype(f32))
        gain = gain + jnp.sum(part * normed, axis=0, keepdims=True)
        offset = offset + jnp.sum(part, axis=0, keepdims=True)
        last[k][...] = part.astype(bf16)
    sums[0:1] = gain
    sums[1:2] = offset


def attention_weights(
    where, hidden, grad_triple, attended, m0, m1, m2, m3, up_sums, two_sums, mid_sums, one_sums,
    mine, theirs, vecs,
):
    ones = jnp.concatenate([m[128:256] for m in (m0, m1, m2, m3)], axis=0)
    vecs[...] = jnp.zeros(vecs.shape, f32)
    vecs[0:4] = one_sums[...]
    vecs[4:5] = mid_sums[3:4]
    vecs[5:6] = mid_sums[2:3]
    vecs[6:8] = mid_sums[0:2]
    vecs[8:10] = two_sums[0:2]
    vecs[pl.ds(10 + where[1], 1)] = up_sums[...]
    blank = jnp.zeros((16, 896), bf16)
    for k in range(4):
        for ref, own in ((mine, True), (theirs, False)):
            cols = core_rows(where, where[2 + k], own)
            ref[k, 0:128, 0:768] = product_left(hidden[:, cols], grad_triple[...]).astype(bf16)
            ref[k, 0:128, 768:1024] = product_left(attended[:, cols], ones).astype(bf16)
            ref[k, 128:144] = jnp.concatenate([vecs[:, cols].astype(bf16), blank], axis=1)


def finish_rows(where, *refs):
    ones, twos, (own_middle, grad_middle, tokens, vecs, out, grad) = refs[:4], refs[4:8], refs[8:]
    total = sum(ref[...].astype(f32) for ref in ones)
    two = sum(ref[...].astype(f32) for ref in twos) + vecs[8:9]
    out[...] = (own_middle[...] + vecs[9:10] * two).astype(bf16)
    normed, spread = normalize(tokens[0:128].astype(f32))
    grad[...] = (grad_middle[...] + normalize_back(total * vecs[0:1], normed, spread)).astype(bf16)


def finish_feed(where, got, up, down):
    for m in range(4):
        down[m * 128 : (m + 1) * 128] = got[m, 128:256].astype(f32)
        for n in range(8):
            lanes = slice(n * 512 + m * 128, n * 512 + (m + 1) * 128)
            up[:, lanes] = got[m, 0:128, n * 128 : (n + 1) * 128].astype(f32)


def finish_attention(where, s0, s1, s2, s3, w_in, w_out, *refs):
    outs, held = refs[:-1], refs[-1]
    for k, ref in enumerate((s0, s1, s2, s3)):
        m = where[1] ^ k
        w_in[:, at(m, 768)] = ref[0:128, 0:768].astype(f32)
        w_out[:, at(m, 256)] = ref[0:128, 768:1024].astype(f32)
        held[m] = ref[128:144, 0:128].astype(f32)
    total = held[0] + held[1] + held[2] + held[3]
    for i in range(10):
        outs[i][...] = total[i : i + 1]
    outs[10][...] = jnp.concatenate([total[i : i + 1] for i in range(10, 14)], axis=1)


def ring(count):
    return list(range(0, count, 2)) + list(range(count - 1, 0, -2))


def step(x, hops=1):
    order = ring(lax.axis_size("fsdp") // 2)
    count = len(order)
    pairs = [(order[i], order[(i + hops) % count]) for i in range(count)]
    return lax.ppermute(x, "fsdp", [(2 * a + c, 2 * b + c) for a, b in pairs for c in (0, 1)])


def along(x):
    count = lax.axis_size("fsdp") // 2
    groups = [[2 * z + c for z in range(count)] for c in (0, 1)]
    return lax.all_to_all(
        x, "fsdp", split_axis=0, concat_axis=0, axis_index_groups=groups, tiled=True
    )


def after(x, *earlier):
    return lax.optimization_barrier((x,) + earlier)[0]


def both_cores(blocks):
    return [b for block in blocks for b in (block, swap(block, "fsdp", 1))]


def pair_sums(mine, theirs):
    return [add(mine[t], theirs[t]) for t in range(4)]


def deal(x):
    return lax.all_to_all(x, "seq", split_axis=0, concat_axis=0, tiled=True)


def share(where, received, own, out):
    total = (received[...].astype(f32) + own[...].astype(f32)).astype(bf16)
    for m in range(4):
        out[m] = total


def deal_sum(x, y, name):
    (copies,) = call(share, [x, y], [shape((4,) + x.shape, bf16)], name=name)
    return deal(copies)


def add(x, y):
    return (x.astype(f32) + y.astype(f32)).astype(bf16)


def body(*args):
    tokens, input_weight, up_weight = args[0], args[4], args[12]
    fits = (
        lax.axis_size("seq") == 4
        and lax.axis_size("fsdp") == 8
        and tokens.shape == (128, 1024)
        and input_weight.shape == (128, 3072)
        and up_weight.shape == (128, 4096)
    )
    return body_fast(*args) if fits else body_any(*args)


def body_fast(
    tokens,
    segment_ids,
    first_gain,
    first_bias,
    input_weight,
    query_bias,
    value_bias,
    output_weight,
    output_bias,
    scale_one,
    second_gain,
    second_bias,
    up_weight,
    up_bias,
    down_weight,
    down_bias,
    scale_two,
    out_grad,
):
    vectors = [
        first_gain, first_bias, query_bias, value_bias, output_bias,
        scale_one, second_gain, second_bias, down_bias, scale_two, up_bias,
    ]
    seg_col, seg_row = segment_ids.reshape(512, 1), segment_ids.reshape(1, 512)
    mat = shape((512, 1024), bf16)
    rows_f, rows_b = shape((128, 1024), f32), shape((128, 1024), bf16)

    first, rows = call(
        prepare_first,
        [input_weight, output_weight, tokens, out_grad] + vectors,
        [shape((4, 144, 1024), bf16), shape((256, 1024), bf16)],
        name="prepare_first",
        scratch=[pltpu.VMEM(v.shape, bf16) for v in vectors] + [pltpu.VMEM((16, 1024), f32), pltpu.SemaphoreType.DMA((32,))],
        in_hbm=True,
        limit=63,
    )
    shared = from_others(rows)
    first_own = along(first)
    (second,) = call(
        prepare_second,
        [up_weight, down_weight],
        [shape((256, 1024), bf16)],
        name="prepare_second",
        scratch=[pltpu.SemaphoreType.DMA((36,))],
        in_hbm=True,
        limit=63,
    )
    second_1 = step(after(second, first_own, *shared[1:]))
    w_in, w_out_own, vecs = call(
        place_first,
        [first_own, swap(after(first_own, second, *shared[1:]), "fsdp", 1)],
        [shape((1024, 768), bf16), shape((1024, 256), bf16), shape((16, 1024), f32)],
        name="place_first",
        limit=63,
    )
    w_out = from_others(w_out_own)
    triple, attended_own, logsum, hidden_one = call(
        attention,
        shared + [w_in, vecs, seg_col, seg_row],
        [shape((512, 768), bf16), shape((4, 512, 256), bf16), shape((512, 128), f32), mat],
        name="attention",
    )
    second_2 = step(after(second_1, attended_own))
    second_3 = step(after(second_2, *w_out[1:]))
    shares = deal(attended_own)
    attended, hidden_two, own_middle, own_branch = call(
        project,
        [shares] + w_out + shared + [vecs],
        [mat, mat, rows_f, rows_f],
        name="project",
        limit=63,
        scratch=[pltpu.VMEM((512, 1024), f32)],
    )
    w_down, act, grad_two, grad_before, up_sums, *partial = call(
        feed,
        [hidden_two]
        + both_cores([after(x, shares) for x in (second, second_1, second_2)] + [after(second_3, hidden_two)])
        + shared + [vecs, seg_col],
        [shape((1024, 1024), bf16), mat, mat, mat, shape((1, 1024), f32), rows_f, rows_b, rows_b, rows_b],
        name="feed",
        scratch=[pltpu.VMEM((1024, 1024), bf16)],
    )
    partial = exchange(partial)
    second_mine, second_theirs, two_sums, *two = call(
        feed_weights,
        [hidden_two, grad_before, act, grad_two, w_down] + shared + [vecs, seg_col],
        [shape((4, 256, 1024), bf16)] * 2 + [shape((2, 1024), f32)] + [rows_b] * 4,
        name="feed_weights",
    )
    second_theirs = swap(after(second_theirs, two[0], *partial[1:]), "fsdp", 1)
    grad_middle, mid_sums, *messages = call(
        middle_back,
        partial + [own_middle, own_branch, rows, seg_col, vecs] + w_out,
        [rows_f, shape((4, 1024), f32)] + [shape((256, 256), bf16)] * 4,
        name="middle_back",
        scratch=[pltpu.VMEM((128, 1024), bf16), pltpu.VMEM((128, 1024), bf16)],
    )
    got = exchange(messages)
    second_sums = pair_sums(after(second_mine, messages[1]), second_theirs)
    second_added = add(step(second_sums[1]), after(second_sums[2], *got[1:]))
    got = [after(got[0], second_added)] + got[1:]
    second_total = step(second_added)
    twos = exchange([two[0]] + [after(x, *got[1:]) for x in two[1:]])
    grad_triple, one_sums, *last = call(
        attention_back,
        [triple, logsum] + got + [seg_col, seg_row, w_in] + shared,
        [shape((512, 768), bf16), shape((4, 1024), f32)] + [rows_b] * 4,
        flops=20 * 512 * 1024 * 1024,
        name="attention_back",
    )
    first_mine, first_theirs = call(
        attention_weights,
        [hidden_one, grad_triple, attended] + got + [up_sums, two_sums, mid_sums, one_sums],
        [shape((4, 144, 1024), bf16)] * 2,
        flops=20 * 512 * 1024 * 1024,
        name="attention_weights",
        scratch=[pltpu.VMEM((16, 1024), f32)],
    )
    ones = exchange([last[0]] + [after(x, *twos[1:]) for x in last[1:]])
    first_sums = pair_sums(first_mine, swap(after(first_theirs, second_total, *twos[1:]), "fsdp", 1))
    second_total = step(add(second_total, second_sums[3]))
    first_added = after(add(step(first_sums[1]), first_sums[2]), second_total, *ones[1:])
    layer_out, tokens_grad = call(
        finish_rows,
        ones + twos + [own_middle, grad_middle, rows, vecs],
        [rows_b, rows_b],
        name="finish_rows",
        limit=63,
    )
    grad_up, grad_down = call(
        finish_feed,
        [deal_sum(second_total, second_sums[0], "share_feed")],
        [shape((128, 4096), f32), shape((512, 1024), f32)],
        name="finish_feed",
    )
    first_total = step(first_added)
    first_total = step(after(add(first_total, first_sums[3]), layer_out))
    first_share = from_others(add(first_total, first_sums[0]))
    grad_in, grad_out, *small = call(
        finish_attention,
        [after(first_share[0], grad_up)] + first_share[1:],
        [shape((128, 3072), f32), rows_f] + [shape((1, 128), f32)] * 10 + [shape((1, 512), f32)],
        name="finish_attention",
        scratch=[pltpu.VMEM((4, 16, 128), f32)],
    )
    g = [v.reshape(-1) for v in small]
    return (
        layer_out, tokens_grad, g[0], g[1], grad_in, g[2], g[3], grad_out, g[4],
        g[5], g[6], g[7], grad_up, g[10], grad_down, g[8], g[9],
    )


def solution(mesh):
    rows, vec, mat = P(("fsdp", "seq"), None), P("fsdp"), P("fsdp", None)
    return jax.shard_map(
        body,
        mesh=mesh,
        in_specs=(
            rows, vec, vec, vec, mat, vec, vec, mat, vec,
            vec, vec, vec, mat, vec, mat, vec, vec, rows,
        ),
        out_specs=(
            rows, rows, vec, vec, mat, vec, vec, mat, vec,
            vec, vec, vec, mat, vec, mat, vec, vec,
        ),
        check_vma=False,
    )
```
